256 devices in a mesh: dp: 8 (over x, core), seq: 32 (over y, z).
Axes of the slice: x: 4, y: 4, z: 8, core: 2. Of those that a mesh axis runs over, the one named last changes fastest.
Arguments:
- xbc_in: bfloat16 [8, 8192, 2816], P('dp', 'seq'), may hold values from -4 to 4
- conv_weight: float32 [4, 2816], replicated, may hold values from -3 to 3
- conv_bias: float32 [2816], replicated, may hold values from -3 to 3
- step_sizes: float32 [8, 40, 8192], P('dp', None, 'seq'), may hold values from 0 to 1, as said below
- decay_rates: float32 [40], replicated, may hold values from 0.7 to 1.4
- skip_gain: float32 [40], replicated, may hold values from 0.5 to 1.5
- grad_out: bfloat16 [8, 8192, 2560], P('dp', 'seq'), may hold values from -0.75 to 0.75
Outputs:
- grad_xbc: bfloat16 [8, 8192, 2816], P('dp', 'seq')
- grad_steps: float32 [8, 40, 8192], P('dp', None, 'seq')
- grad_conv_weight: float32 [4, 2816], replicated
- grad_conv_bias: float32 [2816], replicated
- grad_rates: float32 [40], replicated
- grad_skip: float32 [40], replicated
The draws below stay inside these ranges and needn't reach their ends.
Inputs may be any that keep to these rules, and one draw needn't show every extreme that they name: `step_sizes`: positive step sizes.
All inputs are finite; a program needn't handle non-finite values.
Results may differ from the reference program's by a relative error of at most 0.0056.
Values may be sent and summed in bfloat16 or wider, within the bound.
No kernel may reach another device: no remote copies, remote signals or barrier semaphores. Data moves between devices by JAX's collectives and lax.ppermute only.
A program may use at most 192 MiB of HBM per device.

```python
import math
import jax
import jax.numpy as jnp
from jax import lax

HEADS = 40
HEAD_DIM = 64
STATE = 128
GROUP = 256
KCONV = 4
TOKENS_PER_SEQ = 8192
BATCH_SEQUENCES = 8
CH = 2816


def draw_step_sizes(key, part):
    random_split_keys = jax.random.split(jax.random.fold_in(key, 11), 5)
    fast_count = 5
    slow_log = jax.random.uniform(random_split_keys[0], (BATCH_SEQUENCES, HEADS, 1), jnp.float32, math.log(0.8), math.log(3.3))
    slow_rate = jnp.exp(slow_log) / TOKENS_PER_SEQ
    fast_head = jax.random.randint(random_split_keys[1], (BATCH_SEQUENCES, HEADS, 1), 0, 20) < fast_count
    baseline_rate = jnp.where(fast_head, 1.0 / 40.0, slow_rate)
    jaggedness = jax.random.uniform(random_split_keys[2], (BATCH_SEQUENCES, HEADS, TOKENS_PER_SEQ), jnp.float32, 0.5, 1.5)
    spike_position = jax.random.randint(random_split_keys[3], (BATCH_SEQUENCES, 1, 1, 4), 0, TOKENS_PER_SEQ)
    token_position = lax.broadcasted_iota(jnp.int32, (BATCH_SEQUENCES, 1, TOKENS_PER_SEQ, 4), 2)
    spike_mask = jnp.any(token_position == spike_position, axis=3)
    spike_length = jax.random.uniform(random_split_keys[4], (BATCH_SEQUENCES, 1, TOKENS_PER_SEQ), jnp.float32, 0.22, 0.7)
    return baseline_rate * jaggedness + jnp.where(spike_mask, spike_length, 0.0)


def levels(rng, dims, pieces, low, largest):
    gain, own = 1.0, jax.random.fold_in(rng, 6)
    for position, blocks in pieces:
        heights = jnp.exp(jax.random.uniform(jax.random.fold_in(own, position), (blocks,), jnp.float32, low / len(pieces), largest / len(pieces)))
        gain = gain * jnp.repeat(heights, dims[position] // blocks).reshape([-1 if axis == position else 1 for axis in range(len(dims))])
    return gain


def noise(stream_key, extent, spread, most, pieces=(), dtype=jnp.bfloat16):
    factor_of = levels(stream_key, extent, pieces, -0.22, 0.18) if pieces else 1.0
    values = jax.random.normal(stream_key, extent, jnp.float32) * spread * factor_of
    return jnp.minimum(jnp.maximum(values, -most), most).astype(dtype)


def setup_inputs(seed: int = 0) -> dict:
    seeds = jax.random.split(jax.random.key(seed), 8)
    return {
        "xbc_in": noise(seeds[0], (BATCH_SEQUENCES, TOKENS_PER_SEQ, CH), 0.3, 4.0, ((0, 8), (1, 32))),
        "conv_weight": noise(seeds[1], (KCONV, CH), KCONV ** -0.5, 3.0, (), jnp.float32),
        "conv_bias": noise(seeds[2], (CH,), 0.2, 3.0, (), jnp.float32),
        "step_sizes": draw_step_sizes(jax.random.fold_in(seeds[7], 71), 0),
        "decay_rates": jnp.clip(jnp.exp(jax.random.uniform(seeds[4], (HEADS,), jnp.float32, math.log(0.7), math.log(1.4))), 0.7, 1.4),
        "skip_gain": jnp.clip(jax.random.uniform(seeds[5], (HEADS,), jnp.float32, 0.5, 1.5), 0.5, 1.5),
        "grad_out": noise(seeds[6], (BATCH_SEQUENCES, TOKENS_PER_SEQ, HEADS * HEAD_DIM), 0.05, 0.75, ((0, 8), (1, 32))),
    }


def silu_pair(pre_act):
    sigmoid_v = jax.nn.sigmoid(pre_act)
    return pre_act * sigmoid_v, sigmoid_v * (1.0 + pre_act * (1.0 - sigmoid_v))


def split_block(z_block, dy_block, cum_log):
    x_width = HEADS * HEAD_DIM
    x_heads = z_block[:, :x_width].astype(jnp.float32).reshape(GROUP, HEADS, HEAD_DIM)
    b_proj = z_block[:, x_width:x_width + STATE]
    c_proj = z_block[:, x_width + STATE:]
    dy_heads = dy_block.astype(jnp.float32).reshape(GROUP, HEADS, HEAD_DIM)
    log_end = cum_log[:, -1:]
    tail_decay = jnp.exp(log_end - cum_log).T
    x_weighted = (x_heads * tail_decay[:, :, None]).astype(jnp.bfloat16)
    dy_weighted = (dy_heads * jnp.exp(cum_log).T[:, :, None]).astype(jnp.bfloat16)
    return x_heads, b_proj, c_proj, dy_heads, log_end, tail_decay, x_weighted, dy_weighted


def block_locals(z_block, dy_block, cum_log):
    x_heads, b_proj, c_proj, dy_heads, log_end, tail_decay, x_weighted, dy_weighted = split_block(z_block, dy_block, cum_log)
    s_local = jnp.einsum("sn,shp->hpn", b_proj.astype(jnp.float32), x_weighted.astype(jnp.float32))
    u_local = jnp.einsum("sn,shp->hpn", c_proj.astype(jnp.float32), dy_weighted.astype(jnp.float32))
    return s_local, u_local


def block_grads(z_block, dy_block, cum_log, start_state, end_adjoint, skip_gain):
    x_heads, b_proj, c_proj, dy_heads, log_end, tail_decay, x_weighted, dy_weighted = split_block(z_block, dy_block, cum_log)
    gram_bc = jnp.dot(b_proj, c_proj.T, preferred_element_type=jnp.float32)
    row_index = lax.broadcasted_iota(jnp.int32, (GROUP, GROUP), 0)
    col_index = lax.broadcasted_iota(jnp.int32, (GROUP, GROUP), 1)
    causal = (row_index >= col_index)[None]
    log_gap = cum_log[:, :, None] - cum_log[:, None, :]
    decay_lower = jnp.where(causal, jnp.exp(jnp.where(causal, log_gap, 0.0)), 0.0)
    inner_dx = jnp.einsum("thp,shp->hts", dy_heads, x_heads)
    weights = decay_lower * inner_dx
    k_matrix = (jnp.swapaxes(decay_lower, 1, 2) * gram_bc[None]).astype(jnp.bfloat16)
    m_terms = weights * gram_bc.T[None]
    w_summed = jnp.sum(weights, axis=0).astype(jnp.bfloat16)
    states_low = start_state.astype(jnp.bfloat16).astype(jnp.float32)
    adjoint_low = end_adjoint.astype(jnp.bfloat16).astype(jnp.float32)
    b_float = b_proj.astype(jnp.float32)
    c_float = c_proj.astype(jnp.float32)
    b_adjoint = jnp.einsum("tn,hpn->thp", b_float, adjoint_low)
    dx_state = jnp.einsum("hts,shp->thp", k_matrix.astype(jnp.float32), dy_heads) + tail_decay[:, :, None] * b_adjoint
    grad_bproj = jnp.dot(w_summed.T, c_proj, preferred_element_type=jnp.float32) + jnp.einsum("thp,hpn->tn", x_weighted.astype(jnp.float32), adjoint_low)
    grad_cproj = jnp.dot(w_summed, b_proj, preferred_element_type=jnp.float32) + jnp.einsum("thp,hpn->tn", dy_weighted.astype(jnp.float32), states_low)
    c_state = jnp.einsum("tn,hpn->thp", c_float, states_low)
    q_terms = jnp.sum(c_state * dy_heads, axis=2).T
    r_terms = jnp.sum(b_adjoint * x_heads, axis=2).T
    col_sums = jnp.sum(m_terms, axis=1)
    row_sums = jnp.sum(m_terms, axis=2)
    term_one = jnp.cumsum(col_sums - row_sums, axis=1) + row_sums
    term_two = jnp.flip(jnp.cumsum(jnp.flip(jnp.exp(cum_log) * q_terms, 1), axis=1), 1)
    term_three = jnp.cumsum(jnp.exp(log_end - cum_log) * r_terms, axis=1)
    term_four = jnp.exp(log_end) * jnp.sum(end_adjoint * start_state, axis=(1, 2))[:, None]
    grad_log = term_one + term_two + term_three + term_four - jnp.sum(x_heads * dx_state, axis=2).T
    dx_full = dx_state + skip_gain[None, :, None] * dy_heads
    grad_z = jnp.concatenate([dx_full.reshape(GROUP, HEADS * HEAD_DIM), grad_bproj, grad_cproj], axis=1)
    return grad_z, grad_log


def one_sequence(xbc_seq, step_seq, dy_seq, conv_weight, conv_bias, decay_rates, skip_gain):
    rim_len = KCONV - 1
    x_width = HEADS * HEAD_DIM
    padded_in = jnp.concatenate([jnp.zeros((rim_len, CH), jnp.bfloat16), xbc_seq], axis=0)
    pre_act = jnp.zeros((TOKENS_PER_SEQ, CH), jnp.float32) + conv_bias[None, :]
    for tap_index in range(KCONV):
        pre_act = pre_act + conv_weight[tap_index][None, :] * padded_in[tap_index:tap_index + TOKENS_PER_SEQ].astype(jnp.float32)
    activated, derivative = silu_pair(pre_act)
    z_seq = activated.astype(jnp.bfloat16)
    block_count = TOKENS_PER_SEQ // GROUP
    log_steps = -(step_seq * decay_rates[:, None])
    cum_log = jnp.transpose(jnp.cumsum(log_steps.reshape(HEADS, block_count, GROUP), axis=2), (1, 0, 2))
    z_blocks = z_seq.reshape(block_count, GROUP, CH)
    dy_blocks = dy_seq.reshape(block_count, GROUP, x_width)
    s_local, u_local = lax.map(lambda block_item: block_locals(block_item[0], block_item[1], block_item[2]), (z_blocks, dy_blocks, cum_log))
    decay_end = jnp.exp(cum_log[:, :, -1])

    def advance(carried, block_item):
        return block_item[0][:, None, None] * carried + block_item[1], carried

    zero_state = jnp.zeros((HEADS, HEAD_DIM, STATE), jnp.float32)
    unused_one, block_starts = lax.scan(advance, zero_state, (decay_end, s_local))
    unused_two, block_ends = lax.scan(advance, zero_state, (decay_end, u_local), reverse=True)
    grad_z, grad_log = lax.map(lambda block_item: block_grads(block_item[0], block_item[1], block_item[2], block_item[3], block_item[4], skip_gain), (z_blocks, dy_blocks, cum_log, block_starts, block_ends))
    grad_pre = grad_z.reshape(TOKENS_PER_SEQ, CH) * derivative
    grad_log = jnp.transpose(grad_log, (1, 0, 2)).reshape(HEADS, TOKENS_PER_SEQ)
    padded_grad = jnp.concatenate([grad_pre, jnp.zeros((rim_len, CH), jnp.float32)], axis=0)
    grad_in = jnp.zeros((TOKENS_PER_SEQ, CH), jnp.float32)
    grad_taps = []
    for tap_index in range(KCONV):
        tap_start = rim_len - tap_index
        grad_in = grad_in + conv_weight[tap_index][None, :] * padded_grad[tap_start:tap_start + TOKENS_PER_SEQ]
        grad_taps.append(jnp.sum(grad_pre * padded_in[tap_index:tap_index + TOKENS_PER_SEQ].astype(jnp.float32), axis=0))
    grad_weight = jnp.stack(grad_taps)
    grad_bias = jnp.sum(grad_pre, axis=0)
    grad_steps = -decay_rates[:, None] * grad_log
    grad_rates = -jnp.sum(step_seq * grad_log, axis=1)
    skip_terms = (z_seq[:, :x_width].astype(jnp.float32) * dy_seq.astype(jnp.float32)).reshape(TOKENS_PER_SEQ, HEADS, HEAD_DIM)
    grad_skip = jnp.sum(skip_terms, axis=(0, 2))
    return grad_in.astype(jnp.bfloat16), grad_steps, grad_weight, grad_bias, grad_rates, grad_skip


def reference(xbc_in, conv_weight, conv_bias, step_sizes, decay_rates, skip_gain, grad_out):
    results = lax.map(lambda seq_item: one_sequence(seq_item[0], seq_item[1], seq_item[2], conv_weight, conv_bias, decay_rates, skip_gain), (xbc_in, step_sizes, grad_out))
    grad_in, grad_steps, grad_weight, grad_bias, grad_rates, grad_skip = results
    return (grad_in, grad_steps, jnp.sum(grad_weight, axis=0), jnp.sum(grad_bias, axis=0), jnp.sum(grad_rates, axis=0), jnp.sum(grad_skip, axis=0))
```

```python
import functools

import jax
import jax.numpy as jnp
from jax import lax
from jax.experimental import pallas as pl
from jax.experimental.pallas import tpu as pltpu
from jax.sharding import PartitionSpec as P

HEADS = 40
HEAD_DIM = 64
STATE = 128
GROUP = 256
KCONV = 4
LANE = 128
BF16 = jnp.bfloat16
F32 = jnp.float32
X_WIDTH = HEADS * HEAD_DIM
PAIRS = HEADS // 2
TAIL_ROWS = 16
VMEM_LIMIT = 56 * 1024 * 1024
HIGH = lax.Precision.HIGHEST


def mm(a, b, ca=1, cb=0, precision=None):
    return lax.dot_general(
        a, b, (((ca,), (cb,)), ((), ())), preferred_element_type=F32, precision=precision
    )


def lanes(c):
    return pl.ds(pl.multiple_of(c * LANE, LANE), LANE)


def taps_of(x_ref, halo_ref, c):
    full = jnp.concatenate(
        [
            jnp.zeros((8 - (KCONV - 1), LANE), F32),
            halo_ref[:, lanes(c)].astype(F32),
            x_ref[:, lanes(c)].astype(F32),
        ],
        axis=0,
    )
    return [full[5 + k : 5 + k + GROUP] for k in range(KCONV)]


def front_kernel(
    x_ref, halo_ref, w_ref, bias_ref, step_ref, rate_ref, dy_ref,
    zt_ref, bc_ref, dyt_ref, deriv_ref, cum_ref, msg_ref,
    tail_ref, head_ref, *, chunks, rows,
):
    tiles = X_WIDTH // LANE + 2

    def conv(c, carry):
        taps = taps_of(x_ref, halo_ref, c)
        pre = bias_ref[:, lanes(c)]
        for k in range(KCONV):
            pre = pre + w_ref[k : k + 1, lanes(c)] * taps[k]
        sig = jax.nn.sigmoid(pre)
        deriv_ref[:, lanes(c)] = sig * (1.0 + pre * (1.0 - sig))
        z = (pre * sig).astype(BF16)
        zt_ref[lanes(c), :] = z.astype(F32).T.astype(BF16)

        @pl.when(c >= PAIRS)
        def _():
            bc_ref[:, lanes(c - PAIRS)] = z

        return carry

    lax.fori_loop(0, tiles, conv, 0)

    def turn(c, carry):
        dyt_ref[lanes(c), :] = dy_ref[:, lanes(c)].astype(F32).T.astype(BF16)
        return carry

    lax.fori_loop(0, PAIRS, turn, 0)

    logs = -(step_ref[...] * rate_ref[...])
    row = lax.broadcasted_iota(jnp.int32, (GROUP, GROUP), 0)
    col = lax.broadcasted_iota(jnp.int32, (GROUP, GROUP), 1)
    upto = jnp.where(row <= col, 1.0, 0.0).astype(F32)
    cum = mm(logs, upto, precision=HIGH)
    cum_ref[...] = cum
    log_end = cum[:, GROUP - 1 : GROUP]
    tail_ref[...] = jnp.exp(log_end - cum)
    head_ref[...] = jnp.exp(cum)

    d_end = jnp.broadcast_to(jnp.exp(log_end), (HEADS, LANE))
    part_a = d_end.astype(BF16).astype(F32)
    part_b = (d_end - part_a).astype(BF16).astype(F32)
    part_c = (d_end - part_a - part_b).astype(BF16).astype(F32)
    blank = jnp.zeros((TAIL_ROWS - 6, LANE), F32)
    for j in range(chunks):
        first = rows * j // HEAD_DIM
        last = (rows * j + rows - 1) // HEAD_DIM
        picked = [p[h : h + 1] for h in (first, last) for p in (part_a, part_b, part_c)]
        msg_ref[j, 2 * rows :, :] = jnp.concatenate(picked + [blank], axis=0).astype(BF16)

    b_proj = bc_ref[:, :STATE]
    c_proj = bc_ref[:, STATE:]
    per = 5
    span = per * HEAD_DIM
    each = span // rows

    def local(g, carry):
        for source, scale, proj, at in (
            (zt_ref, tail_ref, b_proj, 0),
            (dyt_ref, head_ref, c_proj, rows),
        ):
            parts = []
            for i in range(per):
                start = pl.multiple_of(g * span + i * HEAD_DIM, HEAD_DIM)
                wide = source[pl.ds(start, HEAD_DIM), :].astype(F32)
                parts.append((wide * scale[pl.ds(g * per + i, 1), :]).astype(BF16))
            found = mm(jnp.concatenate(parts, axis=0), proj).astype(BF16)
            for i in range(each):
                msg_ref[g * each + i, at : at + rows, :] = found[i * rows : (i + 1) * rows]
        return carry

    lax.fori_loop(0, HEADS // per, local, 0)


def within_kernel(
    zt_ref, bc_ref, dyt_ref, dy_ref, cum_ref,
    intra_ref, gbt_ref, gct_ref, col_ref, row_ref,
    column_ref, wsum_ref, cb_ref, hold_ref,
):
    hold_ref[...] = jnp.zeros_like(hold_ref)
    hold_ref[:HEADS, :] = cum_ref[...]
    turned = hold_ref[...].T
    for h in range(HEADS):
        column_ref[h] = jnp.broadcast_to(turned[:, h : h + 1], (GROUP, LANE))
    wsum_ref[...] = jnp.zeros_like(wsum_ref)
    bt = zt_ref[X_WIDTH : X_WIDTH + STATE, :]
    ct = zt_ref[X_WIDTH + STATE :, :]
    cb_ref[...] = mm(bc_ref[:, STATE:], bt)
    t_index = lax.broadcasted_iota(jnp.int32, (GROUP, GROUP), 0)
    s_index = lax.broadcasted_iota(jnp.int32, (GROUP, GROUP), 1)
    causal = t_index >= s_index

    def pair(c, carry):
        dy_pair = dy_ref[:, lanes(c)]
        xt_pair = zt_ref[lanes(c), :]
        dyt_pair = dyt_ref[lanes(c), :]
        zero = jnp.zeros((HEAD_DIM, GROUP), BF16)
        total = wsum_ref[...]
        for i in range(2):
            h = 2 * c + i
            xt = xt_pair[i * HEAD_DIM : (i + 1) * HEAD_DIM]
            dyt = dyt_pair[i * HEAD_DIM : (i + 1) * HEAD_DIM]
            wide = jnp.concatenate([xt, zero] if i == 0 else [zero, xt], axis=0)
            inner = mm(dy_pair, wide)
            column = column_ref[h]
            column = jnp.concatenate([column, column], axis=1)
            gap = column - cum_ref[pl.ds(h, 1), :]
            decay = jnp.exp(jnp.where(causal, gap, -jnp.inf))
            total = total + decay * inner
            kt = (decay * cb_ref[...]).astype(BF16)
            intra = mm(dyt, kt)
            forth = mm(xt, kt, 1, 1)
            intra_ref[pl.ds(pl.multiple_of(h * HEAD_DIM, HEAD_DIM), HEAD_DIM), :] = intra
            col_ref[pl.ds(h, 1), :] = jnp.sum(intra * xt.astype(F32), axis=0, keepdims=True)
            row_ref[pl.ds(h, 1), :] = jnp.sum(forth * dyt.astype(F32), axis=0, keepdims=True)
        wsum_ref[...] = total
        return carry

    lax.fori_loop(0, PAIRS, pair, 0)
    w_summed = wsum_ref[...].astype(BF16)
    gbt_ref[...] = mm(ct, w_summed)
    gct_ref[...] = mm(bt, w_summed, 1, 1)


def chain_kernel(got_ref, out_ref, *, chunks, rows):
    j = lax.axis_index("seq")
    split = HEAD_DIM - lax.rem(rows * j, HEAD_DIM)
    ahead = lax.broadcasted_iota(jnp.int32, (rows, LANE), 0) < split

    def decay_of(i):
        ends = got_ref[i, 2 * rows :, :].astype(F32)
        one = ends[0:1] + ends[1:2] + ends[2:3]
        two = ends[3:4] + ends[4:5] + ends[5:6]
        return jnp.where(ahead, one, two)

    def step(k, carry):
        state, adjoint = carry
        out_ref[k, :rows, :] = state.astype(BF16)
        state = decay_of(k) * state + got_ref[k, :rows, :].astype(F32)
        m = chunks - 1 - k
        out_ref[m, rows:, :] = adjoint.astype(BF16)
        adjoint = decay_of(m) * adjoint + got_ref[m, rows : 2 * rows, :].astype(F32)
        return state, adjoint

    zero = jnp.zeros((rows, LANE), F32)
    lax.fori_loop(0, chunks, step, (zero, zero))


def back_kernel(
    back_ref, zt_ref, dyt_ref, cum_ref, intra_ref, gbt_ref, gct_ref, colin_ref, row_ref,
    deriv_ref, x_ref, halo_ref, step_ref, rate_ref, skip_ref,
    gpre_ref, edge_ref, gsteps_ref, params_ref,
    st_ref, ad_ref, tail_ref, head_ref, q_ref, r_ref, skiprow_ref, four_ref, gb_ref, gc_ref, sums_ref, flip_ref,
    *, chunks, rows,
):
    for j in range(chunks):
        st_ref[j * rows : (j + 1) * rows, :] = back_ref[j, :rows, :]
        ad_ref[j * rows : (j + 1) * rows, :] = back_ref[j, rows:, :]
    cum = cum_ref[...]
    log_end = cum[:, GROUP - 1 : GROUP]
    tail_ref[...] = jnp.exp(log_end - cum)
    head_ref[...] = jnp.exp(cum)
    bt = zt_ref[X_WIDTH : X_WIDTH + STATE, :]
    ct = zt_ref[X_WIDTH + STATE :, :]
    gb_ref[...] = gbt_ref[...]
    gc_ref[...] = gct_ref[...]

    def finish(c, grad_t):
        grad = grad_t.T * deriv_ref[:, lanes(c)]
        gpre_ref[:, lanes(c)] = grad
        edge_ref[:, lanes(c)] = grad[:8]
        taps = taps_of(x_ref, halo_ref, c)
        found = [jnp.sum(grad * tap, axis=0, keepdims=True) for tap in taps]
        found.append(jnp.sum(grad, axis=0, keepdims=True))
        found.append(jnp.zeros((8 - len(found), LANE), F32))
        sums_ref[c] = jnp.concatenate(found, axis=0)

    def pair(c, carry):
        xt = zt_ref[lanes(c), :]
        dyt = dyt_ref[lanes(c), :]
        xf = xt.astype(F32)
        dyf = dyt.astype(F32)
        states = st_ref[lanes(c), :]
        adjoint = ad_ref[lanes(c), :]
        c_state = mm(states, ct)
        b_adj = mm(adjoint, bt)
        both = states.astype(F32) * adjoint.astype(F32)
        tails, heads, skips = [], [], []
        for i in range(2):
            h = 2 * c + i
            part = slice(i * HEAD_DIM, (i + 1) * HEAD_DIM)
            at = pl.ds(h, 1)
            tails.append(jnp.broadcast_to(tail_ref[at, :], (HEAD_DIM, GROUP)))
            heads.append(jnp.broadcast_to(head_ref[at, :], (HEAD_DIM, GROUP)))
            skips.append(jnp.full((HEAD_DIM, GROUP), skip_ref[h], F32))
            q_ref[at, :] = jnp.sum((c_state * dyf)[part], axis=0, keepdims=True)
            r_ref[at, :] = jnp.sum((b_adj * xf)[part], axis=0, keepdims=True)
            skiprow_ref[at, :] = jnp.sum((xf * dyf)[part], axis=0, keepdims=True)
            four_ref[at, :] = jnp.sum(both[part], axis=0, keepdims=True)
        tail = jnp.concatenate(tails, axis=0)
        head = jnp.concatenate(heads, axis=0)
        skip = jnp.concatenate(skips, axis=0)
        gb_ref[...] += mm(adjoint, (xf * tail).astype(BF16), 0, 0)
        gc_ref[...] += mm(states, (dyf * head).astype(BF16), 0, 0)
        finish(c, intra_ref[lanes(c), :] + tail * b_adj + skip * dyf)
        return carry

    lax.fori_loop(0, PAIRS, pair, 0)
    finish(PAIRS, gb_ref[...])
    finish(PAIRS + 1, gc_ref[...])

    row_i = lax.broadcasted_iota(jnp.int32, (GROUP, GROUP), 0)
    col_i = lax.broadcasted_iota(jnp.int32, (GROUP, GROUP), 1)
    upto = jnp.where(row_i <= col_i, 1.0, 0.0).astype(F32)
    since = jnp.where(row_i >= col_i, 1.0, 0.0).astype(F32)
    col_sums = colin_ref[...]
    row_sums = row_ref[...]
    tail_r = tail_ref[...] * r_ref[...]
    running = mm(col_sums - row_sums + tail_r, upto, precision=HIGH)
    ending = mm(head_ref[...] * q_ref[...], since, precision=HIGH)
    four = jnp.exp(log_end) * jnp.sum(four_ref[...], axis=1, keepdims=True)
    grad_log = running + row_sums + ending + four - col_sums - tail_r
    gsteps_ref[...] = -rate_ref[...] * grad_log
    rates = -jnp.sum(step_ref[...] * grad_log, axis=1, keepdims=True)
    skips = jnp.sum(skiprow_ref[...], axis=1, keepdims=True)
    flip_ref[...] = jnp.zeros_like(flip_ref)
    lane = lax.broadcasted_iota(jnp.int32, (HEADS, LANE), 1)
    flip_ref[:HEADS, :] = jnp.where(lane == 0, rates, 0.0) + jnp.where(lane == 1, skips, 0.0)
    tiles = PAIRS + 2
    for c in range(tiles):
        sums = sums_ref[c]
        for k in range(KCONV + 1):
            at = k * tiles + c
            params_ref[at : at + 1, :] = sums[k : k + 1]
    at = (KCONV + 1) * tiles
    params_ref[at : at + 2, :] = flip_ref[...].T[:2]


def spread_kernel(gpre_ref, next_ref, w_ref, out_ref):
    rim = KCONV - 1

    def tile(c, carry):
        full = jnp.concatenate(
            [gpre_ref[:, lanes(c)], next_ref[:, lanes(c)]], axis=0
        )
        total = w_ref[rim : rim + 1, lanes(c)] * full[:GROUP]
        for k in range(rim):
            start = rim - k
            total = total + w_ref[k : k + 1, lanes(c)] * full[start : start + GROUP]
        out_ref[:, lanes(c)] = total.astype(BF16)
        return carry

    lax.fori_loop(0, X_WIDTH // LANE + 2, tile, 0)


def call(kernel, outs, scratch, *operands, in_specs=None):
    extra = {} if in_specs is None else {"in_specs": in_specs}
    return pl.pallas_call(
        kernel,
        out_shape=[jax.ShapeDtypeStruct(shape, dtype) for shape, dtype in outs],
        scratch_shapes=[pltpu.VMEM(shape, dtype) for shape, dtype in scratch],
        compiler_params=pltpu.CompilerParams(vmem_limit_bytes=VMEM_LIMIT),
        **extra,
    )(*operands)


def shifted(array, axis, by):
    length = lax.axis_size(axis)
    pairs = [(i, i + by) for i in range(length) if 0 <= i + by < length]
    return lax.ppermute(array, axis, pairs)


def total_over_devices(array):
    for axis in ("dp", "seq"):
        length = lax.axis_size(axis)
        bit = 1
        while bit < length:
            array = array + lax.ppermute(array, axis, [(i, i ^ bit) for i in range(length)])
            bit *= 2
    return array


def shards(xbc_in, conv_weight, conv_bias, step_sizes, decay_rates, skip_gain, grad_out):
    channels = xbc_in.shape[2]
    rim = KCONV - 1
    chunks = lax.axis_size("seq")
    rows = X_WIDTH // chunks
    x_in = xbc_in[0]
    dy = grad_out[0]
    steps = step_sizes[0]
    rates = decay_rates.reshape(HEADS, 1)
    halo = shifted(x_in[GROUP - rim :], "seq", 1)
    wide_heads = (HEADS, GROUP)
    zt, bc, dyt, deriv, cum, msg = call(
        functools.partial(front_kernel, chunks=chunks, rows=rows),
        [
            ((channels, GROUP), BF16),
            ((GROUP, 2 * STATE), BF16),
            ((X_WIDTH, GROUP), BF16),
            ((GROUP, channels), F32),
            (wide_heads, F32),
            ((chunks, 2 * rows + TAIL_ROWS, LANE), BF16),
        ],
        [(wide_heads, F32), (wide_heads, F32)],
        x_in, halo, conv_weight, conv_bias.reshape(1, channels), steps, rates, dy,
    )
    got = lax.all_to_all(msg, "seq", 0, 0, tiled=True)
    intra, gbt, gct, col_sums, row_sums = call(
        within_kernel,
        [
            ((X_WIDTH, GROUP), F32),
            ((STATE, GROUP), F32),
            ((STATE, GROUP), F32),
            (wide_heads, F32),
            (wide_heads, F32),
        ],
        [
            ((HEADS, GROUP, LANE), F32),
            ((GROUP, GROUP), F32),
            ((GROUP, GROUP), F32),
            ((LANE, GROUP), F32),
        ],
        zt, bc, dyt, dy, cum,
    )
    (turned,) = call(
        functools.partial(chain_kernel, chunks=chunks, rows=rows),
        [((chunks, 2 * rows, LANE), BF16)],
        [],
        got,
    )
    back = lax.all_to_all(turned, "seq", 0, 0, tiled=True)
    vmem = pl.BlockSpec(memory_space=pltpu.VMEM)
    gpre, edge, gsteps, params = call(
        functools.partial(back_kernel, chunks=chunks, rows=rows),
        [
            ((GROUP, channels), F32),
            ((8, channels), F32),
            (wide_heads, F32),
            (((KCONV + 1) * (PAIRS + 2) + 2, LANE), F32),
        ],
        [
            ((X_WIDTH, STATE), BF16),
            ((X_WIDTH, STATE), BF16),
            (wide_heads, F32),
            (wide_heads, F32),
            (wide_heads, F32),
            (wide_heads, F32),
            (wide_heads, F32),
            ((HEADS, LANE), F32),
            ((STATE, GROUP), F32),
            ((STATE, GROUP), F32),
            ((PAIRS + 2, 8, LANE), F32),
            ((LANE, LANE), F32),
        ],
        back, zt, dyt, cum, intra, gbt, gct, col_sums, row_sums,
        deriv, x_in, halo, steps, rates, skip_gain,
        in_specs=[vmem] * 14 + [pl.BlockSpec(memory_space=pltpu.SMEM)],
    )
    next_rows = shifted(edge, "seq", -1)
    (grad_in,) = call(
        spread_kernel, [((GROUP, channels), BF16)], [], gpre, next_rows, conv_weight
    )
    sums = total_over_devices(params)
    tiles = PAIRS + 2
    grad_weight = sums[: KCONV * tiles].reshape(KCONV, channels)
    grad_bias = sums[KCONV * tiles : (KCONV + 1) * tiles].reshape(channels)
    grad_rates = sums[(KCONV + 1) * tiles, :HEADS]
    grad_skip = sums[(KCONV + 1) * tiles + 1, :HEADS]
    return (grad_in[None], gsteps[None], grad_weight, grad_bias, grad_rates, grad_skip)


def solution(mesh):
    return jax.shard_map(
        shards,
        mesh=mesh,
        in_specs=(
            P("dp", "seq", None),
            P(),
            P(),
            P("dp", None, "seq"),
            P(),
            P(),
            P("dp", "seq", None),
        ),
        out_specs=(P("dp", "seq", None), P("dp", None, "seq"), P(), P(), P(), P()),
        check_vma=False,
    )
```

```python
import functools

import jax
import jax.numpy as jnp
from jax import lax
from jax.experimental import pallas as pl
from jax.experimental.pallas import tpu as pltpu
from jax.sharding import PartitionSpec as P

HEADS = 40
HEAD_DIM = 64
STATE = 128
GROUP = 256
KCONV = 4
LANE = 128
BF16 = jnp.bfloat16
F32 = jnp.float32
X_WIDTH = HEADS * HEAD_DIM
PAIRS = HEADS // 2
TAIL_ROWS = 16
VMEM_LIMIT = 24 * 1024 * 1024
HIGH = lax.Precision.HIGHEST


def mm(a, b, ca=1, cb=0, precision=None):
    return lax.dot_general(
        a, b, (((ca,), (cb,)), ((), ())), preferred_element_type=F32, precision=precision
    )


def lanes(c):
    return pl.ds(pl.multiple_of(c * LANE, LANE), LANE)


def taps_of(x_ref, halo_ref, c):
    full = jnp.concatenate(
        [
            jnp.zeros((8 - (KCONV - 1), LANE), F32),
            halo_ref[:, lanes(c)].astype(F32),
            x_ref[:, lanes(c)].astype(F32),
        ],
        axis=0,
    )
    return [full[5 + k : 5 + k + GROUP] for k in range(KCONV)]


def triangle(lower):
    row = lax.broadcasted_iota(jnp.int32, (GROUP, GROUP), 0)
    col = lax.broadcasted_iota(jnp.int32, (GROUP, GROUP), 1)
    return jnp.where(row >= col if lower else row <= col, 1.0, 0.0).astype(F32)


def head_column(scalar_ref):
    head = lax.broadcasted_iota(jnp.int32, (HEADS, GROUP), 0)
    found = jnp.zeros((HEADS, GROUP), F32)
    for h in range(HEADS):
        found = jnp.where(head == h, scalar_ref[h], found)
    return found


def pre_act_of(taps, w_ref, bias_ref, c):
    pre = bias_ref[lanes(c)].reshape(1, LANE)
    for k in range(KCONV):
        pre = pre + w_ref[k : k + 1, lanes(c)] * taps[k]
    return pre


def pair_rows(ref, c):
    return jnp.concatenate(
        [jnp.broadcast_to(ref[pl.ds(2 * c + i, 1), :], (HEAD_DIM, GROUP)) for i in range(2)], axis=0
    )


def decay_kernel(step_ref, rate_ref, dy_ref, dyt_ref, cum_ref, tail_ref, head_ref):
    logs = -(step_ref[...] * head_column(rate_ref))
    cum = mm(logs, triangle(False), precision=HIGH)
    cum_ref[...] = cum
    tail_ref[...] = jnp.exp(cum[:, GROUP - 1 :] - cum)
    head_ref[...] = jnp.exp(cum)

    def turn(c, carry):
        dyt_ref[lanes(c), :] = dy_ref[:, lanes(c)].T
        return carry

    lax.fori_loop(0, PAIRS, turn, 0)


def front_kernel(
    x_ref, halo_ref, w_ref, bias_ref, dyt_ref, tail_ref, head_ref,
    zt_ref, bc_ref, msg_ref, *, chunks, rows,
):
    def conv(c, carry):
        pre = pre_act_of(taps_of(x_ref, halo_ref, c), w_ref, bias_ref, c)
        z = (pre * jax.nn.sigmoid(pre)).astype(BF16)
        zt_ref[lanes(c), :] = z.T

        @pl.when(c >= PAIRS)
        def _():
            bc_ref[:, lanes(c - PAIRS)] = z

        return carry

    lax.fori_loop(0, PAIRS + 2, conv, 0)

    d_end = jnp.broadcast_to(head_ref[:, GROUP - 1 :], (HEADS, LANE))
    part_a = d_end.astype(BF16).astype(F32)
    part_b = (d_end - part_a).astype(BF16).astype(F32)
    part_c = (d_end - part_a - part_b).astype(BF16).astype(F32)
    blank = jnp.zeros((TAIL_ROWS - 6, LANE), F32)
    for j in range(chunks):
        first = rows * j // HEAD_DIM
        last = (rows * j + rows - 1) // HEAD_DIM
        picked = [p[h : h + 1] for h in (first, last) for p in (part_a, part_b, part_c)]
        msg_ref[j, 2 * rows :, :] = jnp.concatenate(picked + [blank], axis=0).astype(BF16)

    b_proj = bc_ref[:, :STATE]
    c_proj = bc_ref[:, STATE:]
    per = 5
    span = per * HEAD_DIM
    each = span // rows

    def local(g, carry):
        for source, scale, proj, at in (
            (zt_ref, tail_ref, b_proj, 0),
            (dyt_ref, head_ref, c_proj, rows),
        ):
            parts = []
            for i in range(per):
                start = pl.multiple_of(g * span + i * HEAD_DIM, HEAD_DIM)
                wide = source[pl.ds(start, HEAD_DIM), :].astype(F32)
                parts.append((wide * scale[pl.ds(g * per + i, 1), :]).astype(BF16))
            found = mm(jnp.concatenate(parts, axis=0), proj).astype(BF16)
            for i in range(each):
                msg_ref[g * each + i, at : at + rows, :] = found[i * rows : (i + 1) * rows]
        return carry

    lax.fori_loop(0, HEADS // per, local, 0)


def within_kernel(
    zt_ref, bc_ref, dyt_ref, dy_ref, cum_ref, skip_ref,
    base_ref, gb_ref, gc_ref, col_ref, row_ref, skiprow_ref,
    column_ref, wsum_ref, cb_ref, hold_ref,
):
    hold_ref[...] = jnp.zeros_like(hold_ref)
    hold_ref[:HEADS, :] = cum_ref[...]
    turned = hold_ref[...].T
    for h in range(HEADS):
        column_ref[h] = jnp.broadcast_to(turned[:, h : h + 1], (GROUP, LANE))
    wsum_ref[...] = jnp.zeros_like(wsum_ref)
    bt = zt_ref[X_WIDTH : X_WIDTH + STATE, :]
    cb_ref[...] = mm(bc_ref[:, STATE:], bt)
    t_index = lax.broadcasted_iota(jnp.int32, (GROUP, GROUP), 0)
    s_index = lax.broadcasted_iota(jnp.int32, (GROUP, GROUP), 1)
    causal = t_index >= s_index

    def pair(c, carry):
        dy_pair = dy_ref[:, lanes(c)]
        xt_pair = zt_ref[lanes(c), :]
        dyt_pair = dyt_ref[lanes(c), :]
        zero = jnp.zeros((HEAD_DIM, GROUP), BF16)
        total = wsum_ref[...]
        for i in range(2):
            h = 2 * c + i
            at = pl.ds(h, 1)
            xt = xt_pair[i * HEAD_DIM : (i + 1) * HEAD_DIM]
            dyt = dyt_pair[i * HEAD_DIM : (i + 1) * HEAD_DIM]
            wide = jnp.concatenate([xt, zero] if i == 0 else [zero, xt], axis=0)
            inner = mm(dy_pair, wide)
            column = column_ref[h]
            column = jnp.concatenate([column, column], axis=1)
            gap = column - cum_ref[at, :]
            decay = jnp.exp(jnp.where(causal, gap, -jnp.inf))
            total = total + decay * inner
            kt = (decay * cb_ref[...]).astype(BF16)
            intra = mm(dyt, kt)
            forth = mm(xt, kt, 1, 1)
            xf = xt.astype(F32)
            dyf = dyt.astype(F32)
            base_ref[pl.ds(pl.multiple_of(h * HEAD_DIM, HEAD_DIM), HEAD_DIM), :] = (
                intra + skip_ref[h] * dyf
            )
            col_ref[at, :] = jnp.sum(intra * xf, axis=0, keepdims=True)
            row_ref[at, :] = jnp.sum(forth * dyf, axis=0, keepdims=True)
            skiprow_ref[at, :] = jnp.sum(xf * dyf, axis=0, keepdims=True)
        wsum_ref[...] = total
        return carry

    lax.fori_loop(0, PAIRS, pair, 0)
    w_summed = wsum_ref[...].astype(BF16)
    gb_ref[...] = mm(w_summed, bc_ref[:, STATE:], 0, 0)
    gc_ref[...] = mm(w_summed, bc_ref[:, :STATE])


def ready_kernel(
    x_ref, halo_ref, w_ref, bias_ref, dy_ref, tail_ref, head_ref, base_ref,
    own_ref, scale_ref, xw_ref, dyw_ref,
):
    def slopes(c):
        pre = pre_act_of(taps_of(x_ref, halo_ref, c), w_ref, bias_ref, c)
        sig = jax.nn.sigmoid(pre)
        return pre * sig, sig * (1.0 + pre * (1.0 - sig))

    def pair(c, carry):
        act, slope = slopes(c)
        tail = pair_rows(tail_ref, c).T
        head = pair_rows(head_ref, c).T
        own_ref[:, lanes(c)] = base_ref[lanes(c), :].T * slope
        scale_ref[:, lanes(c)] = tail * slope
        xw_ref[:, lanes(c)] = (act.astype(BF16).astype(F32) * tail).astype(BF16)
        dyw_ref[:, lanes(c)] = (dy_ref[:, lanes(c)].astype(F32) * head).astype(BF16)
        return carry

    lax.fori_loop(0, PAIRS, pair, 0)
    for c in (PAIRS, PAIRS + 1):
        scale_ref[:, lanes(c)] = slopes(c)[1]


def chain_kernel(got_ref, out_ref, *, chunks, rows):
    j = lax.axis_index("seq")
    split = HEAD_DIM - lax.rem(rows * j, HEAD_DIM)
    ahead = lax.broadcasted_iota(jnp.int32, (rows, LANE), 0) < split

    def decay_of(i):
        ends = got_ref[i, 2 * rows :, :].astype(F32)
        one = ends[0:1] + ends[1:2] + ends[2:3]
        two = ends[3:4] + ends[4:5] + ends[5:6]
        return jnp.where(ahead, one, two)

    def step(k, carry):
        state, adjoint = carry
        out_ref[k, :rows, :] = state.astype(BF16)
        state = decay_of(k) * state + got_ref[k, :rows, :].astype(F32)
        m = chunks - 1 - k
        out_ref[m, rows:, :] = adjoint.astype(BF16)
        adjoint = decay_of(m) * adjoint + got_ref[m, rows : 2 * rows, :].astype(F32)
        return state, adjoint

    zero = jnp.zeros((rows, LANE), F32)
    lax.fori_loop(0, chunks, step, (zero, zero))


def back_kernel(
    back_ref, zt_ref, bc_ref, dyt_ref, tail_ref, head_ref, own_ref, scale_ref, xw_ref, dyw_ref,
    gbin_ref, gcin_ref, colin_ref, row_ref, skiprow_ref,
    x_ref, halo_ref, w_ref, step_ref, rate_ref,
    gin_ref, last_ref, edge_ref, gsteps_ref, params_ref,
    st_ref, ad_ref, q_ref, r_ref, four_ref, gb_ref, gc_ref, sums_ref, flip_ref,
    *, chunks, rows,
):
    rim = KCONV - 1
    for j in range(chunks):
        st_ref[j * rows : (j + 1) * rows, :] = back_ref[j, :rows, :]
        ad_ref[j * rows : (j + 1) * rows, :] = back_ref[j, rows:, :]
    gb_ref[...] = gbin_ref[...]
    gc_ref[...] = gcin_ref[...]

    def finish(c, grad):
        edge_ref[:, lanes(c)] = grad[:rim]
        found = [
            jnp.sum(grad * tap, axis=0, keepdims=True) for tap in taps_of(x_ref, halo_ref, c)
        ]
        found.append(jnp.sum(grad, axis=0, keepdims=True))
        found.append(jnp.zeros((8 - len(found), LANE), F32))
        sums_ref[c] = jnp.concatenate(found, axis=0)
        full = jnp.concatenate([grad, jnp.zeros((8, LANE), F32)], axis=0)
        spread = w_ref[rim : rim + 1, lanes(c)] * grad
        for k in range(rim):
            spread = spread + w_ref[k : k + 1, lanes(c)] * full[rim - k : rim - k + GROUP]
        gin_ref[:, lanes(c)] = spread.astype(BF16)
        last_ref[:, lanes(c)] = spread[GROUP - 16 :]

    def pair(c, carry):
        bt = zt_ref[X_WIDTH : X_WIDTH + STATE, :]
        ct = zt_ref[X_WIDTH + STATE :, :]
        states = st_ref[lanes(c), :]
        adjoint = ad_ref[lanes(c), :]
        c_dot = mm(states, ct) * dyt_ref[lanes(c), :].astype(F32)
        b_dot = mm(adjoint, bt) * zt_ref[lanes(c), :].astype(F32)
        both = states.astype(F32) * adjoint.astype(F32)
        for i in range(2):
            part = slice(i * HEAD_DIM, (i + 1) * HEAD_DIM)
            at = pl.ds(2 * c + i, 1)
            q_ref[at, :] = jnp.sum(c_dot[part], axis=0, keepdims=True)
            r_ref[at, :] = jnp.sum(b_dot[part], axis=0, keepdims=True)
            four_ref[at, :] = jnp.sum(both[part], axis=0, keepdims=True)
        gb_ref[...] += mm(xw_ref[:, lanes(c)], adjoint)
        gc_ref[...] += mm(dyw_ref[:, lanes(c)], states)
        finish(c, own_ref[:, lanes(c)] + scale_ref[:, lanes(c)] * mm(bc_ref[:, :STATE], adjoint, 1, 1))
        return carry

    lax.fori_loop(0, PAIRS, pair, 0)
    finish(PAIRS, gb_ref[...] * scale_ref[:, lanes(PAIRS)])
    finish(PAIRS + 1, gc_ref[...] * scale_ref[:, lanes(PAIRS + 1)])

    col_sums = colin_ref[...]
    row_sums = row_ref[...]
    tail_r = tail_ref[...] * r_ref[...]
    running = mm(col_sums - row_sums + tail_r, triangle(False), precision=HIGH)
    ending = mm(head_ref[...] * q_ref[...], triangle(True), precision=HIGH)
    four = head_ref[:, GROUP - 1 :] * jnp.sum(four_ref[...], axis=1, keepdims=True)
    grad_log = running + row_sums + ending + four - col_sums - tail_r
    gsteps_ref[...] = -head_column(rate_ref) * grad_log
    rates = -jnp.sum(step_ref[...] * grad_log, axis=1, keepdims=True)
    skips = jnp.sum(skiprow_ref[...], axis=1, keepdims=True)
    flip_ref[...] = jnp.zeros_like(flip_ref)
    lane = lax.broadcasted_iota(jnp.int32, (HEADS, LANE), 1)
    flip_ref[:HEADS, :] = jnp.where(lane == 0, rates, 0.0) + jnp.where(lane == 1, skips, 0.0)
    tiles = PAIRS + 2
    for c in range(tiles):
        sums = sums_ref[c]
        for k in range(KCONV + 1):
            at = k * tiles + c
            params_ref[at : at + 1, :] = sums[k : k + 1]
    at = (KCONV + 1) * tiles
    params_ref[at : at + 2, :] = flip_ref[...].T[:2]


def call(kernel, outs, scratch, *operands, scalars=0):
    vmem = pl.BlockSpec(memory_space=pltpu.VMEM)
    smem = pl.BlockSpec(memory_space=pltpu.SMEM)
    return pl.pallas_call(
        kernel,
        out_shape=[jax.ShapeDtypeStruct(shape, dtype) for shape, dtype in outs],
        in_specs=[vmem] * (len(operands) - scalars) + [smem] * scalars,
        scratch_shapes=[pltpu.VMEM(shape, dtype) for shape, dtype in scratch],
        compiler_params=pltpu.CompilerParams(vmem_limit_bytes=VMEM_LIMIT),
    )(*operands)


def shifted(array, axis, by):
    length = lax.axis_size(axis)
    pairs = [(i, i + by) for i in range(length) if 0 <= i + by < length]
    return lax.ppermute(array, axis, pairs)


def flipped(array, axis, bits):
    return lax.ppermute(array, axis, [(i, i ^ bits) for i in range(lax.axis_size(axis))])


def total_over_devices(array):
    for axis in ("dp", "seq"):
        length = lax.axis_size(axis)
        bit = 1
        if length.bit_length() % 2 == 0:
            array = array + flipped(array, axis, 1)
            bit = 2
        while bit < length:
            near = flipped(array, axis, bit)
            far = flipped(array, axis, 2 * bit)
            both = flipped(array, axis, 3 * bit)
            array = (array + near) + (far + both)
            bit *= 4
    return array


def shards(xbc_in, conv_weight, conv_bias, step_sizes, decay_rates, skip_gain, grad_out):
    channels = xbc_in.shape[2]
    rim = KCONV - 1
    chunks = lax.axis_size("seq")
    rows = X_WIDTH // chunks
    x_in = xbc_in[0]
    dy = grad_out[0]
    steps = step_sizes[0]
    wide_heads = ((HEADS, GROUP), F32)
    by_head = ((X_WIDTH, GROUP), F32)
    by_token = ((GROUP, STATE), F32)
    halo = shifted(x_in[GROUP - rim :], "seq", 1)
    dyt, cum, tail, head = call(
        lambda steps, dy, rates, *outs: decay_kernel(steps, rates, dy, *outs),
        [((X_WIDTH, GROUP), BF16), wide_heads, wide_heads, wide_heads],
        [],
        steps, dy, decay_rates, scalars=1,
    )
    zt, bc, msg = call(
        functools.partial(front_kernel, chunks=chunks, rows=rows),
        [
            ((channels, GROUP), BF16),
            ((GROUP, 2 * STATE), BF16),
            ((chunks, 2 * rows + TAIL_ROWS, LANE), BF16),
        ],
        [],
        x_in, halo, conv_weight, conv_bias, dyt, tail, head,
    )
    got = lax.all_to_all(msg, "seq", 0, 0, tiled=True)
    base, gb, gc, col_sums, row_sums, skip_rows = call(
        within_kernel,
        [by_head, by_token, by_token, wide_heads, wide_heads, wide_heads],
        [
            ((HEADS, GROUP, LANE), F32),
            ((GROUP, GROUP), F32),
            ((GROUP, GROUP), F32),
            ((LANE, GROUP), F32),
        ],
        zt, bc, dyt, dy, cum, skip_gain, scalars=1,
    )
    got, base = lax.optimization_barrier((got, base))
    (turned,) = call(
        functools.partial(chain_kernel, chunks=chunks, rows=rows),
        [((chunks, 2 * rows, LANE), BF16)],
        [],
        got,
    )
    back = lax.all_to_all(turned, "seq", 0, 0, tiled=True)
    own, scale, xw, dyw = call(
        ready_kernel,
        [
            ((GROUP, X_WIDTH), F32),
            ((GROUP, channels), F32),
            ((GROUP, X_WIDTH), BF16),
            ((GROUP, X_WIDTH), BF16),
        ],
        [],
        x_in, halo, conv_weight, conv_bias, dy, tail, head, base,
    )
    grad_in, last, edge, gsteps, params = call(
        functools.partial(back_kernel, chunks=chunks, rows=rows),
        [
            ((GROUP, channels), BF16),
            ((16, channels), F32),
            ((rim, channels), F32),
            wide_heads,
            (((KCONV + 1) * (PAIRS + 2) + 2, LANE), F32),
        ],
        [
            ((X_WIDTH, STATE), BF16),
            ((X_WIDTH, STATE), BF16),
            wide_heads,
            wide_heads,
            ((HEADS, LANE), F32),
            by_token,
            by_token,
            ((PAIRS + 2, 8, LANE), F32),
            ((LANE, LANE), F32),
        ],
        back, zt, bc, dyt, tail, head, own, scale, xw, dyw,
        gb, gc, col_sums, row_sums, skip_rows,
        x_in, halo, conv_weight, steps, decay_rates, scalars=1,
    )
    next_rows = shifted(edge, "seq", -1)
    ahead = jnp.concatenate([jnp.zeros_like(next_rows), next_rows], axis=0)
    added = last[16 - rim :]
    for k in range(rim):
        added = added + conv_weight[k][None] * ahead[rim - k : 2 * rim - k]
    ending = jnp.concatenate([last[: 16 - rim], added], axis=0).astype(BF16)
    grad_in = lax.dynamic_update_slice(grad_in, ending, (GROUP - 16, 0))
    sums = total_over_devices(params)
    tiles = PAIRS + 2
    grad_weight = sums[: KCONV * tiles].reshape(KCONV, channels)
    grad_bias = sums[KCONV * tiles : (KCONV + 1) * tiles].reshape(channels)
    grad_rates = sums[(KCONV + 1) * tiles, :HEADS]
    grad_skip = sums[(KCONV + 1) * tiles + 1, :HEADS]
    return (grad_in[None], gsteps[None], grad_weight, grad_bias, grad_rates, grad_skip)


def solution(mesh):
    return jax.shard_map(
        shards,
        mesh=mesh,
        in_specs=(
            P("dp", "seq", None),
            P(),
            P(),
            P("dp", None, "seq"),
            P(),
            P(),
            P("dp", "seq", None),
        ),
        out_specs=(P("dp", "seq", None), P("dp", None, "seq"), P(), P(), P(), P()),
        check_vma=False,
    )
```

```python
import functools

import jax
import jax.numpy as jnp
from jax import lax
from jax.experimental import pallas as pl
from jax.experimental.pallas import tpu as pltpu
from jax.sharding import PartitionSpec as P

HEADS = 40
HEAD_DIM = 64
STATE = 128
GROUP = 256
KCONV = 4
LANE = 128
BF16 = jnp.bfloat16
F32 = jnp.float32
X_WIDTH = HEADS * HEAD_DIM
PAIRS = HEADS // 2
TAIL_ROWS = 16
VMEM_LIMIT = 56 * 1024 * 1024
SMALL_LIMIT = 24 * 1024 * 1024
PARTS = 4
HIGH = lax.Precision.HIGHEST


def mm(a, b, ca=1, cb=0, precision=None):
    return lax.dot_general(
        a, b, (((ca,), (cb,)), ((), ())), preferred_element_type=F32, precision=precision
    )


def lanes(c):
    return pl.ds(pl.multiple_of(c * LANE, LANE), LANE)


def taps_of(x_ref, halo_ref, c):
    full = jnp.concatenate(
        [
            jnp.zeros((8 - (KCONV - 1), LANE), F32),
            halo_ref[:, lanes(c)].astype(F32),
            x_ref[:, lanes(c)].astype(F32),
        ],
        axis=0,
    )
    return [full[5 + k : 5 + k + GROUP] for k in range(KCONV)]


def triangle(lower):
    row = lax.broadcasted_iota(jnp.int32, (GROUP, GROUP), 0)
    col = lax.broadcasted_iota(jnp.int32, (GROUP, GROUP), 1)
    return jnp.where(row >= col if lower else row <= col, 1.0, 0.0).astype(F32)


def head_column(scalar_ref):
    head = lax.broadcasted_iota(jnp.int32, (HEADS, GROUP), 0)
    found = jnp.zeros((HEADS, GROUP), F32)
    for h in range(HEADS):
        found = jnp.where(head == h, scalar_ref[h], found)
    return found


def pre_act_of(taps, w_ref, bias_ref, c):
    pre = bias_ref[lanes(c)].reshape(1, LANE)
    for k in range(KCONV):
        pre = pre + w_ref[k : k + 1, lanes(c)] * taps[k]
    return pre


def pair_rows(ref, c):
    return jnp.concatenate(
        [jnp.broadcast_to(ref[pl.ds(2 * c + i, 1), :], (HEAD_DIM, GROUP)) for i in range(2)], axis=0
    )


def started(sem, *pairs):
    made = [pltpu.make_async_copy(a, b, sem.at[i]) for i, (a, b) in enumerate(pairs)]
    for copy in made:
        copy.start()
    return made


def decay_kernel(
    step_hbm, rate_hbm, dy_hbm,
    dywt_ref, cum_ref, tail_ref, head_ref,
    step_ref, rate_ref, dy_ref, few_sem, dy_sem,
):
    span = X_WIDTH // PARTS
    few = started(few_sem, (step_hbm, step_ref), (rate_hbm, rate_ref))
    cuts = [slice(g * span, (g + 1) * span) for g in range(PARTS)]
    many = started(dy_sem, *[(dy_hbm.at[:, cut], dy_ref.at[:, cut]) for cut in cuts])
    for copy in few:
        copy.wait()
    logs = -(step_ref[...] * head_column(rate_ref))
    cum = mm(logs, triangle(False), precision=HIGH)
    cum_ref[...] = cum
    tail_ref[...] = jnp.exp(cum[:, GROUP - 1 :] - cum)
    head_ref[...] = jnp.exp(cum)

    def turn(c, carry):
        head = pair_rows(head_ref, c)
        dywt_ref[lanes(c), :] = (dy_ref[:, lanes(c)].T.astype(F32) * head).astype(BF16)
        return carry

    per = PAIRS // PARTS
    for g in range(PARTS):
        many[g].wait()
        lax.fori_loop(g * per, (g + 1) * per, turn, 0)


def front_kernel(
    halo_ref, dywt_ref, tail_ref, head_ref,
    x_hbm, w_hbm, bias_hbm,
    msg_hbm,
    x_ref, w_ref, bias_ref, msg_ref, bc_ref, xwt_ref, few_sem, x_sem, msg_sem,
    *, chunks, rows,
):
    per = PAIRS // PARTS
    span = per * LANE
    held = chunks // PARTS
    few = started(
        few_sem, (w_hbm, w_ref), (bias_hbm, bias_ref), (x_hbm.at[:, X_WIDTH:], x_ref.at[:, X_WIDTH:])
    )
    cuts = [slice(g * span, (g + 1) * span) for g in range(PARTS)]
    many = started(x_sem, *[(x_hbm.at[:, cut], x_ref.at[:, cut]) for cut in cuts])

    d_end = jnp.broadcast_to(head_ref[:, GROUP - 1 :], (HEADS, LANE))
    part_a = d_end.astype(BF16).astype(F32)
    part_b = (d_end - part_a).astype(BF16).astype(F32)
    part_c = (d_end - part_a - part_b).astype(BF16).astype(F32)
    blank = jnp.zeros((TAIL_ROWS - 6, LANE), F32)
    for j in range(chunks):
        first = rows * j // HEAD_DIM
        last = (rows * j + rows - 1) // HEAD_DIM
        picked = [p[h : h + 1] for h in (first, last) for p in (part_a, part_b, part_c)]
        msg_ref[j, 2 * rows :, :] = jnp.concatenate(picked + [blank], axis=0).astype(BF16)

    def active(c):
        pre = pre_act_of(taps_of(x_ref, halo_ref, c), w_ref, bias_ref, c)
        return (pre * jax.nn.sigmoid(pre)).astype(BF16)

    for copy in few:
        copy.wait()
    bc_ref[:, :STATE] = active(PAIRS)
    bc_ref[:, STATE:] = active(PAIRS + 1)
    sent = []
    for g in range(PARTS):
        many[g].wait()

        def conv(p, carry, g=g):
            c = g * per + p
            tail = pair_rows(tail_ref, c)
            xwt_ref[lanes(p), :] = (active(c).T.astype(F32) * tail).astype(BF16)
            return carry

        lax.fori_loop(0, per, conv, 0, unroll=True)
        s_local = mm(xwt_ref[...], bc_ref[:, :STATE]).astype(BF16)
        u_local = mm(dywt_ref[cuts[g], :], bc_ref[:, STATE:]).astype(BF16)
        for i in range(held):
            at = slice(i * rows, (i + 1) * rows)
            msg_ref[g * held + i, :rows, :] = s_local[at]
            msg_ref[g * held + i, rows : 2 * rows, :] = u_local[at]
        block = slice(g * held, (g + 1) * held)
        sent.append(pltpu.make_async_copy(msg_ref.at[block], msg_hbm.at[block], msg_sem.at[g]))
        sent[-1].start()
    for copy in sent:
        copy.wait()


def within_kernel(
    x_ref, halo_ref, w_ref, bias_ref, dy_ref, cum_ref, tail_ref, head_ref, skip_ref,
    own_ref, scale_ref, xwt_ref, dywt_ref, bc_ref, bct_ref, slope_ref,
    gb_ref, gc_ref, col_ref, row_ref, skiprow_ref,
    column_ref, wsum_ref, cb_ref, hold_ref, base_ref,
):
    def conv(c):
        pre = pre_act_of(taps_of(x_ref, halo_ref, c), w_ref, bias_ref, c)
        sig = jax.nn.sigmoid(pre)
        return (pre * sig).astype(BF16), sig * (1.0 + pre * (1.0 - sig))

    for i in range(2):
        at = slice(i * STATE, (i + 1) * STATE)
        z, slope_ref[:, at] = conv(PAIRS + i)
        bc_ref[:, at] = z
        bct_ref[at, :] = z.T
    hold_ref[...] = jnp.zeros_like(hold_ref)
    hold_ref[:HEADS, :] = cum_ref[...]
    turned = hold_ref[...].T
    for h in range(HEADS):
        column_ref[h] = jnp.broadcast_to(turned[:, h : h + 1], (GROUP, LANE))
    wsum_ref[...] = jnp.zeros_like(wsum_ref)
    cb_ref[...] = mm(bc_ref[:, STATE:], bct_ref[:STATE, :])
    t_index = lax.broadcasted_iota(jnp.int32, (GROUP, GROUP), 0)
    s_index = lax.broadcasted_iota(jnp.int32, (GROUP, GROUP), 1)
    causal = t_index >= s_index

    def pair(c, carry):
        z, slope = conv(c)
        xt_pair = z.T
        dy_pair = dy_ref[:, lanes(c)]
        dyt_pair = dy_pair.T
        tail = pair_rows(tail_ref, c)
        head = pair_rows(head_ref, c)
        xwt_ref[lanes(c), :] = (xt_pair.astype(F32) * tail).astype(BF16)
        dywt_ref[lanes(c), :] = (dyt_pair.astype(F32) * head).astype(BF16)
        scale_ref[:, lanes(c)] = (tail.T * slope).astype(BF16)
        zero = jnp.zeros((HEAD_DIM, GROUP), BF16)
        total = wsum_ref[...]
        for i in range(2):
            h = 2 * c + i
            at = pl.ds(h, 1)
            part = slice(i * HEAD_DIM, (i + 1) * HEAD_DIM)
            xt = xt_pair[part]
            dyt = dyt_pair[part]
            wide = jnp.concatenate([xt, zero] if i == 0 else [zero, xt], axis=0)
            inner = mm(dy_pair, wide)
            column = column_ref[h]
            column = jnp.concatenate([column, column], axis=1)
            gap = column - cum_ref[at, :]
            decay = jnp.exp(jnp.where(causal, gap, -jnp.inf))
            total = total + decay * inner
            kt = (decay * cb_ref[...]).astype(BF16)
            intra = mm(dyt, kt)
            forth = mm(xt, kt, 1, 1)
            xf = xt.astype(F32)
            dyf = dyt.astype(F32)
            base_ref[part, :] = intra + skip_ref[h] * dyf
            col_ref[at, :] = jnp.sum(intra * xf, axis=0, keepdims=True)
            row_ref[at, :] = jnp.sum(forth * dyf, axis=0, keepdims=True)
            skiprow_ref[at, :] = jnp.sum(xf * dyf, axis=0, keepdims=True)
        wsum_ref[...] = total
        own_ref[:, lanes(c)] = base_ref[...].T * slope
        return carry

    lax.fori_loop(0, PAIRS, pair, 0)
    w_summed = wsum_ref[...].astype(BF16)
    gb_ref[...] = mm(bct_ref[STATE:, :], w_summed)
    gc_ref[...] = mm(bct_ref[:STATE, :], w_summed, 1, 1)


def chain_kernel(got_ref, out_hbm, out_ref, sem, *, chunks, rows):
    j = lax.axis_index("seq")
    split = HEAD_DIM - lax.rem(rows * j, HEAD_DIM)
    ahead = lax.broadcasted_iota(jnp.int32, (rows, LANE), 0) < split

    def decay_of(i):
        ends = got_ref[i, 2 * rows :, :].astype(F32)
        one = ends[0:1] + ends[1:2] + ends[2:3]
        two = ends[3:4] + ends[4:5] + ends[5:6]
        return jnp.where(ahead, one, two)

    def step(k, carry):
        state, adjoint = carry
        out_ref[k, :rows, :] = state.astype(BF16)
        state = decay_of(k) * state + got_ref[k, :rows, :].astype(F32)
        m = chunks - 1 - k
        out_ref[m, rows:, :] = adjoint.astype(BF16)
        adjoint = decay_of(m) * adjoint + got_ref[m, rows : 2 * rows, :].astype(F32)
        return state, adjoint

    carry = (jnp.zeros((rows, LANE), F32), jnp.zeros((rows, LANE), F32))
    half = chunks // 2
    sent = []
    for g in range(2):
        carry = lax.fori_loop(g * half, (g + 1) * half, step, carry, unroll=4)
        fore = (slice(g * half, (g + 1) * half), slice(0, rows))
        rear = (slice((1 - g) * half, (2 - g) * half), slice(rows, 2 * rows))
        for i, at in enumerate((fore, rear)):
            sent.append(pltpu.make_async_copy(out_ref.at[at], out_hbm.at[at], sem.at[2 * g + i]))
            sent[-1].start()
    for copy in sent:
        copy.wait()


def back_kernel(
    back_ref, bc_ref, bct_ref, slope_ref,
    gbin_ref, gcin_ref, colin_ref, row_ref, skiprow_ref,
    halo_ref, w_ref, step_ref, head_ref,
    own_hbm, scale_hbm, xwt_hbm, dywt_hbm, x_hbm,
    rate_ref,
    gin_ref, last_ref, edge_ref, gsteps_ref, params_ref,
    own_ref, scale_ref, xwt_ref, dywt_ref, x_ref,
    cdot_ref, bdot_ref, btok_ref, q_ref, r_ref, four_ref, grad_ref, sums_ref, flip_ref, part_sem,
    *, chunks, rows,
):
    rim = KCONV - 1
    per = PAIRS // PARTS
    span = per * LANE
    held = chunks // PARTS

    def finish(c, grad):
        edge_ref[:, lanes(c)] = grad[:rim]
        x = x_ref[:, lanes(c)].astype(F32)
        halo = halo_ref[:, lanes(c)].astype(F32)
        full = jnp.concatenate([grad, jnp.zeros((8, LANE), F32)], axis=0)
        spread = w_ref[rim : rim + 1, lanes(c)] * grad
        found = []
        for k in range(rim):
            moved = full[rim - k : rim - k + GROUP]
            spread = spread + w_ref[k : k + 1, lanes(c)] * moved
            entering = jnp.sum(grad[: rim - k] * halo[k:], axis=0, keepdims=True)
            found.append(jnp.sum(moved * x, axis=0, keepdims=True) + entering)
        found.append(jnp.sum(grad * x, axis=0, keepdims=True))
        found.append(jnp.sum(grad, axis=0, keepdims=True))
        found.append(jnp.zeros((8 - len(found), LANE), F32))
        sums_ref[c] = jnp.concatenate(found, axis=0)
        gin_ref[:, lanes(c)] = spread.astype(BF16)
        last_ref[:, lanes(c)] = spread[GROUP - 16 :]

    def begin(g):
        if g == PARTS:
            return started(part_sem.at[g], (x_hbm.at[:, X_WIDTH:], x_ref.at[:, X_WIDTH:]))
        at = slice(g * span, (g + 1) * span)
        return started(
            part_sem.at[g],
            (xwt_hbm.at[at], xwt_ref.at[at]),
            (dywt_hbm.at[at], dywt_ref.at[at]),
            (own_hbm.at[:, at], own_ref.at[:, at]),
            (scale_hbm.at[:, at], scale_ref.at[:, at]),
            (x_hbm.at[:, at], x_ref.at[:, at]),
        )

    coming = [begin(0), begin(1)]
    b_proj = bc_ref[:, :STATE]
    gb = gbin_ref[...]
    gc = gcin_ref[...]
    for g in range(PARTS):
        at = slice(g * span, (g + 1) * span)
        states = back_ref[g * held : (g + 1) * held, :rows, :].reshape(span, STATE)
        adjoint = back_ref[g * held : (g + 1) * held, rows:, :].reshape(span, STATE)
        cdot_ref[...] = mm(states, bct_ref[STATE:, :])
        bdot_ref[...] = mm(adjoint, bct_ref[:STATE, :])
        btok_ref[...] = mm(b_proj, adjoint, 1, 1)
        both = states.astype(F32) * adjoint.astype(F32)
        for i in range(2 * per):
            h = 2 * per * g + i
            product = both[i * HEAD_DIM : (i + 1) * HEAD_DIM]
            four_ref[h : h + 1, :] = jnp.sum(product, axis=0, keepdims=True)
        for copy in coming[g]:
            copy.wait()
        if g + 2 <= PARTS:
            coming.append(begin(g + 2))
        gb = gb + mm(adjoint, xwt_ref[at, :], 0, 0)
        gc = gc + mm(states, dywt_ref[at, :], 0, 0)

        def pair(p, carry, g=g):
            c = g * per + p
            c_dot = cdot_ref[lanes(p), :] * dywt_ref[lanes(c), :].astype(F32)
            b_dot = bdot_ref[lanes(p), :] * xwt_ref[lanes(c), :].astype(F32)
            for i in range(2):
                part = slice(i * HEAD_DIM, (i + 1) * HEAD_DIM)
                h = pl.ds(2 * c + i, 1)
                q_ref[h, :] = jnp.sum(c_dot[part], axis=0, keepdims=True)
                r_ref[h, :] = jnp.sum(b_dot[part], axis=0, keepdims=True)
            state_part = scale_ref[:, lanes(c)].astype(F32) * btok_ref[:, lanes(p)]
            finish(c, own_ref[:, lanes(c)] + state_part)
            return carry

        lax.fori_loop(0, per, pair, 0, unroll=True)
    for copy in coming[PARTS]:
        copy.wait()
    for i, total in enumerate((gb, gc)):
        grad_ref[...] = total
        finish(PAIRS + i, grad_ref[...].T * slope_ref[:, i * STATE : (i + 1) * STATE])

    col_sums = colin_ref[...]
    row_sums = row_ref[...]
    tail_r = r_ref[...]
    running = mm(col_sums - row_sums + tail_r, triangle(False), precision=HIGH)
    ending = mm(q_ref[...], triangle(True), precision=HIGH)
    four = head_ref[:, GROUP - 1 :] * jnp.sum(four_ref[...], axis=1, keepdims=True)
    grad_log = running + row_sums + ending + four - col_sums - tail_r
    gsteps_ref[...] = -head_column(rate_ref) * grad_log
    rates = -jnp.sum(step_ref[...] * grad_log, axis=1, keepdims=True)
    skips = jnp.sum(skiprow_ref[...], axis=1, keepdims=True)
    flip_ref[...] = jnp.zeros_like(flip_ref)
    lane = lax.broadcasted_iota(jnp.int32, (HEADS, LANE), 1)
    flip_ref[:HEADS, :] = jnp.where(lane == 0, rates, 0.0) + jnp.where(lane == 1, skips, 0.0)
    tiles = PAIRS + 2
    for c in range(tiles):
        sums = sums_ref[c]
        for k in range(KCONV + 1):
            at = k * tiles + c
            params_ref[at : at + 1, :] = sums[k : k + 1]
    at = (KCONV + 1) * tiles
    params_ref[at : at + 2, :] = flip_ref[...].T[:2]


def call(
    kernel, outs, scratch, *operands, large=0, scalars=0, kept=(), large_out=False, limit=VMEM_LIMIT
):
    small = len(operands) - large - scalars
    spaces = [pltpu.VMEM] * small + [pltpu.HBM] * large + [pltpu.SMEM] * scalars
    operands = [
        pltpu.with_memory_space_constraint(operand, pltpu.HBM)
        if space == pltpu.HBM
        else operand
        for operand, space in zip(operands, spaces)
    ]
    out_space = pltpu.HBM if large_out else pltpu.VMEM
    return pl.pallas_call(
        kernel,
        out_shape=[
            out_space(*out) if large_out or i in kept else jax.ShapeDtypeStruct(*out)
            for i, out in enumerate(outs)
        ],
        in_specs=[pl.BlockSpec(memory_space=space) for space in spaces],
        out_specs=[pl.BlockSpec(memory_space=out_space)] * len(outs),
        scratch_shapes=[pltpu.VMEM(*item) if isinstance(item, tuple) else item for item in scratch],
        compiler_params=pltpu.CompilerParams(vmem_limit_bytes=limit),
    )(*operands)


def shifted(array, axis, by):
    length = lax.axis_size(axis)
    pairs = [(i, i + by) for i in range(length) if 0 <= i + by < length]
    return lax.ppermute(array, axis, pairs)


def flipped(array, axis, bits):
    return lax.ppermute(array, axis, [(i, i ^ bits) for i in range(lax.axis_size(axis))])


def total_over_devices(array):
    for axis in ("dp", "seq"):
        length = lax.axis_size(axis)
        bit = 1
        if length.bit_length() % 2 == 0:
            array = array + flipped(array, axis, 1)
            bit = 2
        while bit < length:
            near = flipped(array, axis, bit)
            far = flipped(array, axis, 2 * bit)
            both = flipped(array, axis, 3 * bit)
            array = (array + near) + (far + both)
            bit *= 4
    return array


def shards(xbc_in, conv_weight, conv_bias, step_sizes, decay_rates, skip_gain, grad_out):
    channels = xbc_in.shape[2]
    rim = KCONV - 1
    chunks = lax.axis_size("seq")
    rows = X_WIDTH // chunks
    x_in = xbc_in[0]
    dy = grad_out[0]
    steps = step_sizes[0]
    wide_heads = ((HEADS, GROUP), F32)
    by_head = ((X_WIDTH, GROUP), BF16)
    halo = shifted(x_in[GROUP - rim :], "seq", 1)
    dma = pltpu.SemaphoreType.DMA
    dywt, cum, tail, head = call(
        decay_kernel,
        [((X_WIDTH, GROUP), BF16), wide_heads, wide_heads, wide_heads],
        [wide_heads, pltpu.SMEM((HEADS,), F32), ((GROUP, X_WIDTH), BF16), dma((2,)), dma((PARTS,))],
        steps, decay_rates, dy, large=3, kept=(0,), limit=SMALL_LIMIT,
    )
    (msg,) = call(
        functools.partial(front_kernel, chunks=chunks, rows=rows),
        [((chunks, 2 * rows + TAIL_ROWS, LANE), BF16)],
        [
            ((GROUP, channels), BF16),
            ((KCONV, channels), F32),
            ((channels,), F32),
            ((chunks, 2 * rows + TAIL_ROWS, LANE), BF16),
            ((GROUP, 2 * STATE), BF16),
            ((X_WIDTH // PARTS, GROUP), BF16),
            dma((3,)),
            dma((PARTS,)),
            dma((PARTS,)),
        ],
        halo, dywt, tail, head, x_in, conv_weight, conv_bias,
        large=3, large_out=True, limit=SMALL_LIMIT,
    )
    got = lax.all_to_all(msg, "seq", 0, 0, tiled=True)
    own, scale, xwt, dywt, bc, bct, slope, gb, gc, col_sums, row_sums, skip_rows = call(
        within_kernel,
        [
            ((GROUP, X_WIDTH), F32),
            ((GROUP, X_WIDTH), BF16),
            by_head,
            by_head,
            ((GROUP, 2 * STATE), BF16),
            ((2 * STATE, GROUP), BF16),
            ((GROUP, 2 * STATE), F32),
            ((STATE, GROUP), F32),
            ((STATE, GROUP), F32),
            wide_heads,
            wide_heads,
            wide_heads,
        ],
        [
            ((HEADS, GROUP, LANE), F32),
            ((GROUP, GROUP), F32),
            ((GROUP, GROUP), F32),
            ((LANE, GROUP), F32),
            ((LANE, GROUP), F32),
        ],
        x_in, halo, conv_weight, conv_bias, dy, cum, tail, head, skip_gain, scalars=1,
    )
    got, own = lax.optimization_barrier((got, own))
    (turned,) = call(
        functools.partial(chain_kernel, chunks=chunks, rows=rows),
        [((chunks, 2 * rows, LANE), BF16)],
        [((chunks, 2 * rows, LANE), BF16), dma((4,))],
        got, large_out=True, limit=SMALL_LIMIT,
    )
    back = lax.all_to_all(turned, "seq", 0, 0, tiled=True)
    grad_in, last, edge, gsteps, params = call(
        functools.partial(back_kernel, chunks=chunks, rows=rows),
        [
            ((GROUP, channels), BF16),
            ((16, channels), F32),
            ((rim, channels), F32),
            wide_heads,
            (((KCONV + 1) * (PAIRS + 2) + 2, LANE), F32),
        ],
        [
            ((GROUP, X_WIDTH), F32),
            ((GROUP, X_WIDTH), BF16),
            by_head,
            by_head,
            ((GROUP, channels), BF16),
            ((X_WIDTH // PARTS, GROUP), F32),
            ((X_WIDTH // PARTS, GROUP), F32),
            ((GROUP, X_WIDTH // PARTS), F32),
            wide_heads,
            wide_heads,
            ((HEADS, LANE), F32),
            ((STATE, GROUP), F32),
            ((PAIRS + 2, 8, LANE), F32),
            ((LANE, LANE), F32),
            dma((PARTS + 1, 5)),
        ],
        back, bc, bct, slope, gb, gc, col_sums, row_sums, skip_rows,
        halo, conv_weight, steps, head,
        own, scale, xwt, dywt, x_in, decay_rates,
        large=5, scalars=1, limit=SMALL_LIMIT,
    )
    next_rows = shifted(edge, "seq", -1)
    ahead = jnp.concatenate([jnp.zeros_like(next_rows), next_rows], axis=0)
    added = last[16 - rim :]
    for k in range(rim):
        added = added + conv_weight[k][None] * ahead[rim - k : 2 * rim - k]
    ending = jnp.concatenate([last[: 16 - rim], added], axis=0).astype(BF16)
    grad_in = lax.dynamic_update_slice(grad_in, ending, (GROUP - 16, 0))
    sums = total_over_devices(params)
    tiles = PAIRS + 2
    grad_weight = sums[: KCONV * tiles].reshape(KCONV, channels)
    grad_bias = sums[KCONV * tiles : (KCONV + 1) * tiles].reshape(channels)
    grad_rates = sums[(KCONV + 1) * tiles, :HEADS]
    grad_skip = sums[(KCONV + 1) * tiles + 1, :HEADS]
    return (grad_in[None], gsteps[None], grad_weight, grad_bias, grad_rates, grad_skip)


def solution(mesh):
    return jax.shard_map(
        shards,
        mesh=mesh,
        in_specs=(
            P("dp", "seq", None),
            P(),
            P(),
            P("dp", None, "seq"),
            P(),
            P(),
            P("dp", "seq", None),
        ),
        out_specs=(P("dp", "seq", None), P("dp", None, "seq"), P(), P(), P(), P()),
        check_vma=False,
    )
```

```python
import functools

import jax
import jax.numpy as jnp
from jax import lax
from jax.experimental import pallas as pl
from jax.experimental.pallas import tpu as pltpu
from jax.sharding import PartitionSpec as P

HEADS = 40
HEAD_DIM = 64
STATE = 128
GROUP = 256
KCONV = 4
LANE = 128
BF16 = jnp.bfloat16
F32 = jnp.float32
X_WIDTH = HEADS * HEAD_DIM
PAIRS = HEADS // 2
TAIL_ROWS = 16
VMEM_LIMIT = 56 * 1024 * 1024
SMALL_LIMIT = 24 * 1024 * 1024
PARTS = 4
HIGH = lax.Precision.HIGHEST


def mm(a, b, ca=1, cb=0, precision=None):
    return lax.dot_general(
        a, b, (((ca,), (cb,)), ((), ())), preferred_element_type=F32, precision=precision
    )


def lanes(c):
    return pl.ds(pl.multiple_of(c * LANE, LANE), LANE)


def taps_of(x_ref, halo_ref, c):
    full = jnp.concatenate(
        [
            jnp.zeros((8 - (KCONV - 1), LANE), F32),
            halo_ref[:, lanes(c)].astype(F32),
            x_ref[:, lanes(c)].astype(F32),
        ],
        axis=0,
    )
    return [full[5 + k : 5 + k + GROUP] for k in range(KCONV)]


def triangle(lower):
    row = lax.broadcasted_iota(jnp.int32, (GROUP, GROUP), 0)
    col = lax.broadcasted_iota(jnp.int32, (GROUP, GROUP), 1)
    return jnp.where(row >= col if lower else row <= col, 1.0, 0.0).astype(F32)


def head_column(scalar_ref):
    head = lax.broadcasted_iota(jnp.int32, (HEADS, GROUP), 0)
    found = jnp.zeros((HEADS, GROUP), F32)
    for h in range(HEADS):
        found = jnp.where(head == h, scalar_ref[h], found)
    return found


def pre_act_of(taps, w_ref, bias_ref, c):
    pre = bias_ref[lanes(c)].reshape(1, LANE)
    for k in range(KCONV):
        pre = pre + w_ref[k : k + 1, lanes(c)] * taps[k]
    return pre


def pair_rows(ref, c):
    return jnp.concatenate(
        [jnp.broadcast_to(ref[pl.ds(2 * c + i, 1), :], (HEAD_DIM, GROUP)) for i in range(2)], axis=0
    )


def started(sem, *pairs):
    made = [pltpu.make_async_copy(a, b, sem.at[i]) for i, (a, b) in enumerate(pairs)]
    for copy in made:
        copy.start()
    return made


def logs_of(step_ref, rate_ref):
    return mm(-(step_ref[...] * head_column(rate_ref)), triangle(False), precision=HIGH)


def decay_kernel(
    step_hbm, rate_hbm, dy_hbm, x_hbm,
    dywt_ref, tail_ref, head_ref, rim_ref,
    step_ref, rate_ref, dy_ref, last_ref, few_sem, dy_sem,
):
    span = X_WIDTH // PARTS
    few = started(
        few_sem, (step_hbm, step_ref), (rate_hbm, rate_ref), (x_hbm.at[GROUP - 16 :], last_ref)
    )
    cuts = [slice(g * span, (g + 1) * span) for g in range(PARTS)]
    many = started(dy_sem, *[(dy_hbm.at[:, cut], dy_ref.at[:, cut]) for cut in cuts])
    for copy in few:
        copy.wait()
    rim_ref[...] = last_ref[...].astype(F32)[16 - (KCONV - 1) :].astype(BF16)
    cum = logs_of(step_ref, rate_ref)
    tail_ref[...] = jnp.exp(cum[:, GROUP - 1 :] - cum)
    head_ref[...] = jnp.exp(cum)

    def turn(c, carry):
        head = pair_rows(head_ref, c)
        dywt_ref[lanes(c), :] = (dy_ref[:, lanes(c)].T.astype(F32) * head).astype(BF16)
        return carry

    per = PAIRS // PARTS
    for g in range(PARTS):
        many[g].wait()
        lax.fori_loop(g * per, (g + 1) * per, turn, 0, unroll=True)


def front_kernel(
    halo_ref, dywt_ref, tail_ref, head_ref,
    x_hbm, w_hbm, bias_hbm,
    msg_hbm,
    x_ref, w_ref, bias_ref, msg_ref, bc_ref, xwt_ref, few_sem, x_sem, msg_sem,
    *, chunks, rows,
):
    per = PAIRS // PARTS
    span = per * LANE
    held = chunks // PARTS
    few = started(
        few_sem, (w_hbm, w_ref), (bias_hbm, bias_ref), (x_hbm.at[:, X_WIDTH:], x_ref.at[:, X_WIDTH:])
    )
    cuts = [slice(g * span, (g + 1) * span) for g in range(PARTS)]
    many = started(x_sem, *[(x_hbm.at[:, cut], x_ref.at[:, cut]) for cut in cuts])

    d_end = jnp.broadcast_to(head_ref[:, GROUP - 1 :], (HEADS, LANE))
    part_a = d_end.astype(BF16).astype(F32)
    part_b = (d_end - part_a).astype(BF16).astype(F32)
    part_c = (d_end - part_a - part_b).astype(BF16).astype(F32)
    blank = jnp.zeros((TAIL_ROWS - 6, LANE), F32)
    for j in range(chunks):
        first = rows * j // HEAD_DIM
        last = (rows * j + rows - 1) // HEAD_DIM
        picked = [p[h : h + 1] for h in (first, last) for p in (part_a, part_b, part_c)]
        msg_ref[j, 2 * rows :, :] = jnp.concatenate(picked + [blank], axis=0).astype(BF16)

    def active(c):
        pre = pre_act_of(taps_of(x_ref, halo_ref, c), w_ref, bias_ref, c)
        return (pre * jax.nn.sigmoid(pre)).astype(BF16)

    for copy in few:
        copy.wait()
    bc_ref[:, :STATE] = active(PAIRS)
    bc_ref[:, STATE:] = active(PAIRS + 1)
    sent = []
    for g in range(PARTS):
        many[g].wait()

        def conv(p, carry, g=g):
            c = g * per + p
            tail = pair_rows(tail_ref, c)
            xwt_ref[lanes(p), :] = (active(c).T.astype(F32) * tail).astype(BF16)
            return carry

        lax.fori_loop(0, per, conv, 0, unroll=True)
        s_local = mm(xwt_ref[...], bc_ref[:, :STATE]).astype(BF16)
        u_local = mm(dywt_ref[cuts[g], :], bc_ref[:, STATE:]).astype(BF16)
        for i in range(held):
            at = slice(i * rows, (i + 1) * rows)
            msg_ref[g * held + i, :rows, :] = s_local[at]
            msg_ref[g * held + i, rows : 2 * rows, :] = u_local[at]
        block = slice(g * held, (g + 1) * held)
        sent.append(pltpu.make_async_copy(msg_ref.at[block], msg_hbm.at[block], msg_sem.at[g]))
        sent[-1].start()
    for copy in sent:
        copy.wait()


def within_kernel(
    x_ref, halo_ref, w_ref, bias_ref, dy_ref, step_ref, rate_ref, skip_ref,
    own_ref, scale_ref, xwt_ref, dywt_ref, bc_ref, bct_ref, slope_ref,
    gb_ref, gc_ref, col_ref, row_ref, skiprow_ref, sofar_ref, end_ref,
    column_ref, wsum_ref, cb_ref, hold_ref, base_ref, cum_ref, tail_ref, head_ref,
):
    cum = logs_of(step_ref, rate_ref)
    cum_ref[...] = cum
    tail_ref[...] = jnp.exp(cum[:, GROUP - 1 :] - cum)
    head_ref[...] = jnp.exp(cum)
    end_ref[...] = jnp.broadcast_to(jnp.exp(cum[:, GROUP - 1 :]), (HEADS, LANE))
    sofar_ref[...] = mm(step_ref[...], triangle(False), precision=HIGH)

    def conv(c):
        pre = pre_act_of(taps_of(x_ref, halo_ref, c), w_ref, bias_ref, c)
        sig = jax.nn.sigmoid(pre)
        return (pre * sig).astype(BF16), sig * (1.0 + pre * (1.0 - sig))

    for i in range(2):
        at = slice(i * STATE, (i + 1) * STATE)
        z, slope_ref[:, at] = conv(PAIRS + i)
        bc_ref[:, at] = z
        bct_ref[at, :] = z.T
    hold_ref[...] = jnp.zeros_like(hold_ref)
    hold_ref[:HEADS, :] = cum_ref[...]
    turned = hold_ref[...].T
    for h in range(HEADS):
        column_ref[h] = jnp.broadcast_to(turned[:, h : h + 1], (GROUP, LANE))
    wsum_ref[...] = jnp.zeros_like(wsum_ref)
    cb_ref[...] = mm(bc_ref[:, STATE:], bct_ref[:STATE, :])
    t_index = lax.broadcasted_iota(jnp.int32, (GROUP, GROUP), 0)
    s_index = lax.broadcasted_iota(jnp.int32, (GROUP, GROUP), 1)
    causal = t_index >= s_index

    def pair(c, carry):
        z, slope = conv(c)
        xt_pair = z.T
        dy_pair = dy_ref[:, lanes(c)]
        dyt_pair = dy_pair.T
        tail = pair_rows(tail_ref, c)
        head = pair_rows(head_ref, c)
        xwt_ref[lanes(c), :] = (xt_pair.astype(F32) * tail).astype(BF16)
        dywt_ref[lanes(c), :] = (dyt_pair.astype(F32) * head).astype(BF16)
        scale_ref[:, lanes(c)] = (tail.T * slope).astype(BF16)
        zero = jnp.zeros((HEAD_DIM, GROUP), BF16)
        total = wsum_ref[...]
        for i in range(2):
            h = 2 * c + i
            at = pl.ds(h, 1)
            part = slice(i * HEAD_DIM, (i + 1) * HEAD_DIM)
            xt = xt_pair[part]
            dyt = dyt_pair[part]
            wide = jnp.concatenate([xt, zero] if i == 0 else [zero, xt], axis=0)
            inner = mm(dy_pair, wide)
            column = column_ref[h]
            column = jnp.concatenate([column, column], axis=1)
            gap = column - cum_ref[at, :]
            decay = jnp.exp(jnp.where(causal, gap, -jnp.inf))
            total = total + decay * inner
            kt = (decay * cb_ref[...]).astype(BF16)
            intra = mm(dyt, kt)
            forth = mm(xt, kt, 1, 1)
            xf = xt.astype(F32)
            dyf = dyt.astype(F32)
            base_ref[part, :] = intra + skip_ref[h] * dyf
            col_ref[at, :] = jnp.sum(intra * xf, axis=0, keepdims=True)
            row_ref[at, :] = jnp.sum(forth * dyf, axis=0, keepdims=True)
            skiprow_ref[at, :] = jnp.sum(xf * dyf, axis=0, keepdims=True)
        wsum_ref[...] = total
        own_ref[:, lanes(c)] = base_ref[...].T * slope
        return carry

    lax.fori_loop(0, PAIRS, pair, 0)
    w_summed = wsum_ref[...].astype(BF16)
    gb_ref[...] = mm(bct_ref[STATE:, :], w_summed)
    gc_ref[...] = mm(bct_ref[:STATE, :], w_summed, 1, 1)


def chain_kernel(got_ref, out_hbm, out_ref, sem, *, chunks, rows):
    j = lax.axis_index("seq")
    split = HEAD_DIM - lax.rem(rows * j, HEAD_DIM)
    ahead = lax.broadcasted_iota(jnp.int32, (rows, LANE), 0) < split

    def decay_of(i):
        ends = got_ref[i, 2 * rows :, :].astype(F32)
        one = ends[0:1] + ends[1:2] + ends[2:3]
        two = ends[3:4] + ends[4:5] + ends[5:6]
        return jnp.where(ahead, one, two)

    def step(k, carry):
        state, adjoint = carry
        out_ref[k, :rows, :] = state.astype(BF16)
        state = decay_of(k) * state + got_ref[k, :rows, :].astype(F32)
        m = chunks - 1 - k
        out_ref[m, rows:, :] = adjoint.astype(BF16)
        adjoint = decay_of(m) * adjoint + got_ref[m, rows : 2 * rows, :].astype(F32)
        return state, adjoint

    carry = (jnp.zeros((rows, LANE), F32), jnp.zeros((rows, LANE), F32))
    half = chunks // 2
    sent = []
    for g in range(2):
        carry = lax.fori_loop(g * half, (g + 1) * half, step, carry, unroll=4)
        fore = (slice(g * half, (g + 1) * half), slice(0, rows))
        rear = (slice((1 - g) * half, (2 - g) * half), slice(rows, 2 * rows))
        for i, at in enumerate((fore, rear)):
            sent.append(pltpu.make_async_copy(out_ref.at[at], out_hbm.at[at], sem.at[2 * g + i]))
            sent[-1].start()
    for copy in sent:
        copy.wait()


def back_kernel(
    back_ref, bc_ref, bct_ref, slope_ref,
    gbin_ref, gcin_ref, colin_ref, row_ref, skiprow_ref,
    halo_ref, w_ref, step_ref, sofar_ref, end_ref,
    own_hbm, scale_hbm, xwt_hbm, dywt_hbm, x_hbm,
    gin_ref, last_ref, edge_ref, q_ref, r_ref, four_ref, params_ref,
    own_ref, scale_ref, xwt_ref, dywt_ref, x_ref,
    cdot_ref, bdot_ref, btok_ref, product_ref, grad_ref, sums_ref, flip_ref, part_sem,
    *, chunks, rows,
):
    rim = KCONV - 1
    per = PAIRS // PARTS
    span = per * LANE
    held = chunks // PARTS

    def finish(c, grad):
        edge_ref[:, lanes(c)] = grad[:rim]
        x = x_ref[:, lanes(c)].astype(F32)
        halo = halo_ref[:, lanes(c)].astype(F32)
        full = jnp.concatenate([grad, jnp.zeros((8, LANE), F32)], axis=0)
        spread = w_ref[rim : rim + 1, lanes(c)] * grad
        found = []
        for k in range(rim):
            moved = full[rim - k : rim - k + GROUP]
            spread = spread + w_ref[k : k + 1, lanes(c)] * moved
            entering = jnp.sum(grad[: rim - k] * halo[k:], axis=0, keepdims=True)
            found.append(jnp.sum(moved * x, axis=0, keepdims=True) + entering)
        found.append(jnp.sum(grad * x, axis=0, keepdims=True))
        found.append(jnp.sum(grad, axis=0, keepdims=True))
        found.append(jnp.zeros((8 - len(found), LANE), F32))
        sums_ref[c] = jnp.concatenate(found, axis=0)
        gin_ref[:, lanes(c)] = spread.astype(BF16)
        last_ref[:, lanes(c)] = spread[GROUP - 16 :]

    def begin(g):
        if g == PARTS:
            return started(part_sem.at[g], (x_hbm.at[:, X_WIDTH:], x_ref.at[:, X_WIDTH:]))
        at = slice(g * span, (g + 1) * span)
        return started(
            part_sem.at[g],
            (xwt_hbm.at[at], xwt_ref.at[at]),
            (dywt_hbm.at[at], dywt_ref.at[at]),
            (own_hbm.at[:, at], own_ref.at[:, at]),
            (scale_hbm.at[:, at], scale_ref.at[:, at]),
            (x_hbm.at[:, at], x_ref.at[:, at]),
        )

    coming = [begin(0), begin(1)]
    b_proj = bc_ref[:, :STATE]
    gb = gbin_ref[...]
    gc = gcin_ref[...]
    for g in range(PARTS):
        at = slice(g * span, (g + 1) * span)
        states = back_ref[g * held : (g + 1) * held, :rows, :].reshape(span, STATE)
        adjoint = back_ref[g * held : (g + 1) * held, rows:, :].reshape(span, STATE)
        cdot_ref[...] = mm(states, bct_ref[STATE:, :])
        bdot_ref[...] = mm(adjoint, bct_ref[:STATE, :])
        btok_ref[...] = mm(b_proj, adjoint, 1, 1)
        both = states.astype(F32) * adjoint.astype(F32)
        for i in range(2 * per):
            h = 2 * per * g + i
            product = both[i * HEAD_DIM : (i + 1) * HEAD_DIM]
            product_ref[h : h + 1, :] = jnp.sum(product, axis=0, keepdims=True)
        for copy in coming[g]:
            copy.wait()
        if g + 2 <= PARTS:
            coming.append(begin(g + 2))
        gb = gb + mm(adjoint, xwt_ref[at, :], 0, 0)
        gc = gc + mm(states, dywt_ref[at, :], 0, 0)

        def pair(p, carry, g=g):
            c = g * per + p
            c_dot = cdot_ref[lanes(p), :] * dywt_ref[lanes(c), :].astype(F32)
            b_dot = bdot_ref[lanes(p), :] * xwt_ref[lanes(c), :].astype(F32)
            for i in range(2):
                part = slice(i * HEAD_DIM, (i + 1) * HEAD_DIM)
                h = pl.ds(2 * c + i, 1)
                q_ref[h, :] = jnp.sum(c_dot[part], axis=0, keepdims=True)
                r_ref[h, :] = jnp.sum(b_dot[part], axis=0, keepdims=True)
            state_part = scale_ref[:, lanes(c)].astype(F32) * btok_ref[:, lanes(p)]
            finish(c, own_ref[:, lanes(c)] + state_part)
            return carry

        lax.fori_loop(0, per, pair, 0, unroll=True)
    for copy in coming[PARTS]:
        copy.wait()
    for i, total in enumerate((gb, gc)):
        grad_ref[...] = total
        finish(PAIRS + i, grad_ref[...].T * slope_ref[:, i * STATE : (i + 1) * STATE])

    four = end_ref[...] * jnp.sum(product_ref[...], axis=1, keepdims=True)
    four_ref[...] = four
    steps = step_ref[...]
    sofar = sofar_ref[...]
    every = sofar[:, GROUP - 1 :]
    own = row_ref[...] - colin_ref[...] - r_ref[...]
    met = steps * own - (every - sofar + steps) * own + sofar * q_ref[...]
    rates = -(jnp.sum(met, axis=1, keepdims=True) + four[:, :1] * every)
    skips = jnp.sum(skiprow_ref[...], axis=1, keepdims=True)
    flip_ref[...] = jnp.zeros_like(flip_ref)
    lane = lax.broadcasted_iota(jnp.int32, (HEADS, LANE), 1)
    flip_ref[:HEADS, :] = jnp.where(lane == 0, rates, 0.0) + jnp.where(lane == 1, skips, 0.0)
    tiles = PAIRS + 2
    for c in range(tiles):
        sums = sums_ref[c]
        for k in range(KCONV + 1):
            at = k * tiles + c
            params_ref[at : at + 1, :] = sums[k : k + 1]
    at = (KCONV + 1) * tiles
    params_ref[at : at + 2, :] = flip_ref[...].T[:2]


def log_kernel(q_ref, r_ref, four_ref, col_ref, row_ref, rate_ref, gsteps_ref):
    own = row_ref[...] - col_ref[...] - r_ref[...]
    running = mm(own, triangle(False), precision=HIGH)
    ending = mm(q_ref[...], triangle(True), precision=HIGH)
    grad_log = own - running + ending + four_ref[:, :1]
    gsteps_ref[...] = -head_column(rate_ref) * grad_log


def unpack_kernel(near_ref, far_ref, weight_ref, bias_ref, rates_ref, skip_ref, sum_ref):
    sum_ref[...] = near_ref[...] + far_ref[...]
    tiles = PAIRS + 2
    for c in range(tiles):
        at = slice(c * LANE, (c + 1) * LANE)
        for k in range(KCONV):
            weight_ref[k : k + 1, at] = sum_ref[k * tiles + c : k * tiles + c + 1, :]
        bias_ref[at] = sum_ref[KCONV * tiles + c, :]
    at = (KCONV + 1) * tiles
    rates_ref[...] = sum_ref[at, :HEADS]
    skip_ref[...] = sum_ref[at + 1, :HEADS]


def call(
    kernel, outs, scratch, *operands, large=0, scalars=0, kept=(), large_out=False, limit=VMEM_LIMIT
):
    small = len(operands) - large - scalars
    spaces = [pltpu.VMEM] * small + [pltpu.HBM] * large + [pltpu.SMEM] * scalars
    operands = [
        pltpu.with_memory_space_constraint(operand, pltpu.HBM)
        if space == pltpu.HBM
        else operand
        for operand, space in zip(operands, spaces)
    ]
    out_space = pltpu.HBM if large_out else pltpu.VMEM
    return pl.pallas_call(
        kernel,
        out_shape=[
            out_space(*out) if large_out or i in kept else jax.ShapeDtypeStruct(*out)
            for i, out in enumerate(outs)
        ],
        in_specs=[pl.BlockSpec(memory_space=space) for space in spaces],
        out_specs=[pl.BlockSpec(memory_space=out_space)] * len(outs),
        scratch_shapes=[pltpu.VMEM(*item) if isinstance(item, tuple) else item for item in scratch],
        compiler_params=pltpu.CompilerParams(vmem_limit_bytes=limit),
    )(*operands)


def shifted(array, axis, by):
    length = lax.axis_size(axis)
    pairs = [(i, i + by) for i in range(length) if 0 <= i + by < length]
    return lax.ppermute(array, axis, pairs)


def flipped(array, axis, bits):
    return lax.ppermute(array, axis, [(i, i ^ bits) for i in range(lax.axis_size(axis))])


def four_summed(array, axis, bit):
    near = flipped(array, axis, bit)
    far = flipped(array, axis, 2 * bit)
    both = flipped(array, axis, 3 * bit)
    return (array + near) + (far + both)


def shards(xbc_in, conv_weight, conv_bias, step_sizes, decay_rates, skip_gain, grad_out):
    channels = xbc_in.shape[2]
    rim = KCONV - 1
    chunks = lax.axis_size("seq")
    rows = X_WIDTH // chunks
    x_in = xbc_in[0]
    dy = grad_out[0]
    steps = step_sizes[0]
    wide_heads = ((HEADS, GROUP), F32)
    by_head = ((X_WIDTH, GROUP), BF16)
    dma = pltpu.SemaphoreType.DMA
    dywt, tail, head, x_rim = call(
        decay_kernel,
        [((X_WIDTH, GROUP), BF16), wide_heads, wide_heads, ((rim, channels), BF16)],
        [
            wide_heads,
            pltpu.SMEM((HEADS,), F32),
            ((GROUP, X_WIDTH), BF16),
            ((16, channels), BF16),
            dma((3,)),
            dma((PARTS,)),
        ],
        steps, decay_rates, dy, x_in, large=4, kept=(0,), limit=SMALL_LIMIT,
    )
    halo = shifted(x_rim, "seq", 1)
    (msg,) = call(
        functools.partial(front_kernel, chunks=chunks, rows=rows),
        [((chunks, 2 * rows + TAIL_ROWS, LANE), BF16)],
        [
            ((GROUP, channels), BF16),
            ((KCONV, channels), F32),
            ((channels,), F32),
            ((chunks, 2 * rows + TAIL_ROWS, LANE), BF16),
            ((GROUP, 2 * STATE), BF16),
            ((X_WIDTH // PARTS, GROUP), BF16),
            dma((3,)),
            dma((PARTS,)),
            dma((PARTS,)),
        ],
        halo, dywt, tail, head, x_in, conv_weight, conv_bias,
        large=3, large_out=True, limit=SMALL_LIMIT,
    )
    got = lax.all_to_all(msg, "seq", 0, 0, tiled=True)
    (own, scale, xwt, dywt, bc, bct, slope, gb, gc, col_sums, row_sums, skip_rows, sofar, d_end) = call(
        within_kernel,
        [
            ((GROUP, X_WIDTH), F32),
            ((GROUP, X_WIDTH), BF16),
            by_head,
            by_head,
            ((GROUP, 2 * STATE), BF16),
            ((2 * STATE, GROUP), BF16),
            ((GROUP, 2 * STATE), F32),
            ((STATE, GROUP), F32),
            ((STATE, GROUP), F32),
            wide_heads,
            wide_heads,
            wide_heads,
            wide_heads,
            ((HEADS, LANE), F32),
        ],
        [
            ((HEADS, GROUP, LANE), F32),
            ((GROUP, GROUP), F32),
            ((GROUP, GROUP), F32),
            ((LANE, GROUP), F32),
            ((LANE, GROUP), F32),
            wide_heads,
            wide_heads,
            wide_heads,
        ],
        x_in, halo, conv_weight, conv_bias, dy, steps, decay_rates, skip_gain, scalars=2,
    )
    got, own = lax.optimization_barrier((got, own))
    (turned,) = call(
        functools.partial(chain_kernel, chunks=chunks, rows=rows),
        [((chunks, 2 * rows, LANE), BF16)],
        [((chunks, 2 * rows, LANE), BF16), dma((4,))],
        got, large_out=True, limit=SMALL_LIMIT,
    )
    back = lax.all_to_all(turned, "seq", 0, 0, tiled=True)
    grad_in, last, edge, q_rows, r_rows, four, params = call(
        functools.partial(back_kernel, chunks=chunks, rows=rows),
        [
            ((GROUP, channels), BF16),
            ((16, channels), F32),
            ((rim, channels), F32),
            wide_heads,
            wide_heads,
            ((HEADS, LANE), F32),
            (((KCONV + 1) * (PAIRS + 2) + 2, LANE), F32),
        ],
        [
            ((GROUP, X_WIDTH), F32),
            ((GROUP, X_WIDTH), BF16),
            by_head,
            by_head,
            ((GROUP, channels), BF16),
            ((X_WIDTH // PARTS, GROUP), F32),
            ((X_WIDTH // PARTS, GROUP), F32),
            ((GROUP, X_WIDTH // PARTS), F32),
            ((HEADS, LANE), F32),
            ((STATE, GROUP), F32),
            ((PAIRS + 2, 8, LANE), F32),
            ((LANE, LANE), F32),
            dma((PARTS + 1, 5)),
        ],
        back, bc, bct, slope, gb, gc, col_sums, row_sums, skip_rows,
        halo, conv_weight, steps, sofar, d_end,
        own, scale, xwt, dywt, x_in,
        large=5, limit=SMALL_LIMIT,
    )
    sums = params + flipped(params, "dp", 1)
    sums = four_summed(sums, "dp", 2)
    sums = four_summed(sums, "seq", 8)
    sums = four_summed(sums, "seq", 1)
    sums, edge, q_rows = lax.optimization_barrier((sums, edge, q_rows))
    far_sums = flipped(sums, "seq", 4)
    next_rows = shifted(edge, "seq", -1)
    (gsteps,) = call(
        log_kernel, [wide_heads], [], q_rows, r_rows, four, col_sums, row_sums, decay_rates,
        scalars=1, limit=SMALL_LIMIT,
    )
    ahead = jnp.concatenate([jnp.zeros_like(next_rows), next_rows], axis=0)
    added = last[16 - rim :]
    for k in range(rim):
        added = added + conv_weight[k][None] * ahead[rim - k : 2 * rim - k]
    ending = jnp.concatenate([last[: 16 - rim], added], axis=0).astype(BF16)
    grad_in = lax.dynamic_update_slice(grad_in, ending, (GROUP - 16, 0))
    grad_weight, grad_bias, grad_rates, grad_skip = call(
        unpack_kernel,
        [((KCONV, channels), F32), ((channels,), F32), ((HEADS,), F32), ((HEADS,), F32)],
        [(params.shape, F32)],
        sums, far_sums, limit=SMALL_LIMIT,
    )
    return (grad_in[None], gsteps[None], grad_weight, grad_bias, grad_rates, grad_skip)


def solution(mesh):
    return jax.shard_map(
        shards,
        mesh=mesh,
        in_specs=(
            P("dp", "seq", None),
            P(),
            P(),
            P("dp", None, "seq"),
            P(),
            P(),
            P("dp", "seq", None),
        ),
        out_specs=(P("dp", "seq", None), P("dp", None, "seq"), P(), P(), P(), P()),
        check_vma=False,
    )
```

```python
import functools

import jax
import jax.numpy as jnp
from jax import lax
from jax.experimental import pallas as pl
from jax.experimental.pallas import tpu as pltpu
from jax.sharding import PartitionSpec as P

HEADS = 40
HEAD_DIM = 64
STATE = 128
GROUP = 256
KCONV = 4
LANE = 128
BF16 = jnp.bfloat16
F32 = jnp.float32
X_WIDTH = HEADS * HEAD_DIM
PAIRS = HEADS // 2
TAIL_ROWS = 8
VMEM_LIMIT = 56 * 1024 * 1024
SMALL_LIMIT = 24 * 1024 * 1024
PARTS = 4
HIGH = lax.Precision.HIGHEST


def mm(a, b, ca=1, cb=0, precision=None):
    return lax.dot_general(
        a, b, (((ca,), (cb,)), ((), ())), preferred_element_type=F32, precision=precision
    )


def lanes(c):
    return pl.ds(pl.multiple_of(c * LANE, LANE), LANE)


def taps_of(x_ref, halo_ref, c):
    full = jnp.concatenate(
        [
            jnp.zeros((8 - (KCONV - 1), LANE), F32),
            halo_ref[:, lanes(c)].astype(F32),
            x_ref[:, lanes(c)].astype(F32),
        ],
        axis=0,
    )
    return [full[5 + k : 5 + k + GROUP] for k in range(KCONV)]


def triangle(lower):
    row = lax.broadcasted_iota(jnp.int32, (GROUP, GROUP), 0)
    col = lax.broadcasted_iota(jnp.int32, (GROUP, GROUP), 1)
    return jnp.where(row >= col if lower else row <= col, 1.0, 0.0).astype(F32)


def head_column(scalar_ref):
    head = lax.broadcasted_iota(jnp.int32, (HEADS, GROUP), 0)
    found = jnp.zeros((HEADS, GROUP), F32)
    for h in range(HEADS):
        found = jnp.where(head == h, scalar_ref[h], found)
    return found


def pre_act_of(taps, w_ref, bias_ref, c):
    pre = bias_ref[lanes(c)].reshape(1, LANE)
    for k in range(KCONV):
        pre = pre + w_ref[k : k + 1, lanes(c)] * taps[k]
    return pre


def pair_rows(ref, c):
    return jnp.concatenate(
        [jnp.broadcast_to(ref[pl.ds(2 * c + i, 1), :], (HEAD_DIM, GROUP)) for i in range(2)], axis=0
    )


def started(sem, *pairs):
    made = [pltpu.make_async_copy(a, b, sem.at[i]) for i, (a, b) in enumerate(pairs)]
    for copy in made:
        copy.start()
    return made


def logs_of(step_ref, rate_ref):
    return mm(-(step_ref[...] * head_column(rate_ref)), triangle(False), precision=HIGH)


def decay_kernel(
    step_hbm, rate_hbm, dy_hbm, x_hbm,
    dywt_ref, tail_ref, head_ref, rim_ref,
    step_ref, rate_ref, dy_ref, last_ref, few_sem, dy_sem,
):
    span = X_WIDTH // PARTS
    few = started(
        few_sem, (step_hbm, step_ref), (rate_hbm, rate_ref), (x_hbm.at[GROUP - 16 :], last_ref)
    )
    cuts = [slice(g * span, (g + 1) * span) for g in range(PARTS)]
    many = started(dy_sem, *[(dy_hbm.at[:, cut], dy_ref.at[:, cut]) for cut in cuts])
    for copy in few:
        copy.wait()
    rim_ref[...] = last_ref[...].astype(F32)[16 - (KCONV - 1) :].astype(BF16)
    cum = logs_of(step_ref, rate_ref)
    tail_ref[...] = jnp.exp(cum[:, GROUP - 1 :] - cum)
    head_ref[...] = jnp.exp(cum)

    def turn(c, carry):
        head = pair_rows(head_ref, c)
        dywt_ref[lanes(c), :] = (dy_ref[:, lanes(c)].T.astype(F32) * head).astype(BF16)
        return carry

    per = PAIRS // PARTS
    for g in range(PARTS):
        many[g].wait()
        lax.fori_loop(g * per, (g + 1) * per, turn, 0, unroll=True)


def front_kernel(
    halo_ref, dywt_ref, tail_ref, head_ref,
    x_hbm, w_hbm, bias_hbm,
    msg_hbm,
    x_ref, w_ref, bias_ref, msg_ref, bc_ref, xwt_ref, few_sem, x_sem, msg_sem,
    *, chunks, rows,
):
    per = PAIRS // PARTS
    span = per * LANE
    held = chunks // PARTS
    few = started(
        few_sem, (w_hbm, w_ref), (bias_hbm, bias_ref), (x_hbm.at[:, X_WIDTH:], x_ref.at[:, X_WIDTH:])
    )
    cuts = [slice(g * span, (g + 1) * span) for g in range(PARTS)]
    many = started(x_sem, *[(x_hbm.at[:, cut], x_ref.at[:, cut]) for cut in cuts])

    d_end = jnp.broadcast_to(head_ref[:, GROUP - 1 :], (HEADS, LANE))
    part_a = d_end.astype(BF16).astype(F32)
    part_b = (d_end - part_a).astype(BF16).astype(F32)
    part_c = (d_end - part_a - part_b).astype(BF16).astype(F32)
    blank = jnp.zeros((TAIL_ROWS - 6, LANE), F32)
    for j in range(chunks):
        first = rows * j // HEAD_DIM
        last = (rows * j + rows - 1) // HEAD_DIM
        picked = [p[h : h + 1] for h in (first, last) for p in (part_a, part_b, part_c)]
        msg_ref[j, 2 * rows :, :] = jnp.concatenate(picked + [blank], axis=0).astype(BF16)

    def active(c):
        pre = pre_act_of(taps_of(x_ref, halo_ref, c), w_ref, bias_ref, c)
        return (pre * jax.nn.sigmoid(pre)).astype(BF16)

    for copy in few:
        copy.wait()
    bc_ref[:, :STATE] = active(PAIRS)
    bc_ref[:, STATE:] = active(PAIRS + 1)
    sent = []
    for g in range(PARTS):
        many[g].wait()

        def conv(p, carry, g=g):
            c = g * per + p
            tail = pair_rows(tail_ref, c)
            xwt_ref[lanes(p), :] = (active(c).T.astype(F32) * tail).astype(BF16)
            return carry

        lax.fori_loop(0, per, conv, 0, unroll=True)
        s_local = mm(xwt_ref[...], bc_ref[:, :STATE]).astype(BF16)
        u_local = mm(dywt_ref[cuts[g], :], bc_ref[:, STATE:]).astype(BF16)
        for i in range(held):
            at = slice(i * rows, (i + 1) * rows)
            msg_ref[g * held + i, :rows, :] = s_local[at]
            msg_ref[g * held + i, rows : 2 * rows, :] = u_local[at]
        block = slice(g * held, (g + 1) * held)
        sent.append(pltpu.make_async_copy(msg_ref.at[block], msg_hbm.at[block], msg_sem.at[g]))
        sent[-1].start()
    for copy in sent:
        copy.wait()


def within_kernel(
    x_ref, halo_ref, w_ref, bias_ref, dy_ref, step_ref, rate_ref, skip_ref,
    own_ref, scale_ref, xwt_ref, dywt_ref, bc_ref, bct_ref, slope_ref,
    gb_ref, gc_ref, col_ref, row_ref, skiprow_ref, sofar_ref, end_ref,
    column_ref, wsum_ref, cb_ref, hold_ref, base_ref, cum_ref, tail_ref, head_ref,
):
    cum = logs_of(step_ref, rate_ref)
    cum_ref[...] = cum
    tail_ref[...] = jnp.exp(cum[:, GROUP - 1 :] - cum)
    head_ref[...] = jnp.exp(cum)
    end_ref[...] = jnp.broadcast_to(jnp.exp(cum[:, GROUP - 1 :]), (HEADS, LANE))
    sofar_ref[...] = mm(step_ref[...], triangle(False), precision=HIGH)

    def conv(c):
        pre = pre_act_of(taps_of(x_ref, halo_ref, c), w_ref, bias_ref, c)
        sig = jax.nn.sigmoid(pre)
        return (pre * sig).astype(BF16), sig * (1.0 + pre * (1.0 - sig))

    for i in range(2):
        at = slice(i * STATE, (i + 1) * STATE)
        z, slope_ref[:, at] = conv(PAIRS + i)
        bc_ref[:, at] = z
        bct_ref[at, :] = z.T
    hold_ref[...] = jnp.zeros_like(hold_ref)
    hold_ref[:HEADS, :] = cum_ref[...]
    turned = hold_ref[...].T
    for h in range(HEADS):
        column_ref[h] = jnp.broadcast_to(turned[:, h : h + 1], (GROUP, LANE))
    wsum_ref[...] = jnp.zeros_like(wsum_ref)
    cb_ref[...] = mm(bc_ref[:, STATE:], bct_ref[:STATE, :])
    t_index = lax.broadcasted_iota(jnp.int32, (GROUP, GROUP), 0)
    s_index = lax.broadcasted_iota(jnp.int32, (GROUP, GROUP), 1)
    causal = t_index >= s_index

    def pair(c, carry):
        z, slope = conv(c)
        xt_pair = z.T
        dy_pair = dy_ref[:, lanes(c)]
        dyt_pair = dy_pair.T
        tail = pair_rows(tail_ref, c)
        head = pair_rows(head_ref, c)
        xwt_ref[lanes(c), :] = (xt_pair.astype(F32) * tail).astype(BF16)
        dywt_ref[lanes(c), :] = (dyt_pair.astype(F32) * head).astype(BF16)
        scale_ref[:, lanes(c)] = (tail.T * slope).astype(BF16)
        zero = jnp.zeros((HEAD_DIM, GROUP), BF16)
        total = wsum_ref[...]
        for i in range(2):
            h = 2 * c + i
            at = pl.ds(h, 1)
            part = slice(i * HEAD_DIM, (i + 1) * HEAD_DIM)
            xt = xt_pair[part]
            dyt = dyt_pair[part]
            wide = jnp.concatenate([xt, zero] if i == 0 else [zero, xt], axis=0)
            inner = mm(dy_pair, wide)
            column = column_ref[h]
            column = jnp.concatenate([column, column], axis=1)
            gap = column - cum_ref[at, :]
            decay = jnp.exp(jnp.where(causal, gap, -jnp.inf))
            total = total + decay * inner
            kt = (decay * cb_ref[...]).astype(BF16)
            intra = mm(dyt, kt)
            forth = mm(xt, kt, 1, 1)
            xf = xt.astype(F32)
            dyf = dyt.astype(F32)
            base_ref[part, :] = intra + skip_ref[h] * dyf
            col_ref[at, :] = jnp.sum(intra * xf, axis=0, keepdims=True)
            row_ref[at, :] = jnp.sum(forth * dyf, axis=0, keepdims=True)
            skiprow_ref[at, :] = jnp.sum(xf * dyf, axis=0, keepdims=True)
        wsum_ref[...] = total
        own_ref[:, lanes(c)] = base_ref[...].T * slope
        return carry

    lax.fori_loop(0, PAIRS, pair, 0)
    w_summed = wsum_ref[...].astype(BF16)
    gb_ref[...] = mm(bct_ref[STATE:, :], w_summed)
    gc_ref[...] = mm(bct_ref[:STATE, :], w_summed, 1, 1)


def chain_kernel(got_ref, out_hbm, out_ref, sem, *, chunks, rows):
    j = lax.axis_index("seq")
    split = HEAD_DIM - lax.rem(rows * j, HEAD_DIM)
    ahead = lax.broadcasted_iota(jnp.int32, (rows, LANE), 0) < split

    def decay_of(i):
        ends = got_ref[i, 2 * rows :, :].astype(F32)
        one = ends[0:1] + ends[1:2] + ends[2:3]
        two = ends[3:4] + ends[4:5] + ends[5:6]
        return jnp.where(ahead, one, two)

    def step(k, carry):
        state, adjoint = carry
        out_ref[k, :rows, :] = state.astype(BF16)
        state = decay_of(k) * state + got_ref[k, :rows, :].astype(F32)
        m = chunks - 1 - k
        out_ref[m, rows:, :] = adjoint.astype(BF16)
        adjoint = decay_of(m) * adjoint + got_ref[m, rows : 2 * rows, :].astype(F32)
        return state, adjoint

    carry = (jnp.zeros((rows, LANE), F32), jnp.zeros((rows, LANE), F32))
    half = chunks // 2
    sent = []
    for g in range(2):
        carry = lax.fori_loop(g * half, (g + 1) * half, step, carry, unroll=4)
        fore = (slice(g * half, (g + 1) * half), slice(0, rows))
        rear = (slice((1 - g) * half, (2 - g) * half), slice(rows, 2 * rows))
        for i, at in enumerate((fore, rear)):
            sent.append(pltpu.make_async_copy(out_ref.at[at], out_hbm.at[at], sem.at[2 * g + i]))
            sent[-1].start()
    for copy in sent:
        copy.wait()


def back_kernel(
    back_ref, bc_ref, bct_ref, slope_ref,
    gbin_ref, gcin_ref, colin_ref, row_ref, skiprow_ref,
    halo_ref, w_ref, step_ref, sofar_ref, end_ref,
    own_hbm, scale_hbm, xwt_hbm, dywt_hbm, x_hbm,
    gin_ref, last_ref, edge_ref, q_ref, r_ref, four_ref, params_ref,
    own_ref, scale_ref, xwt_ref, dywt_ref, x_ref,
    cdot_ref, bdot_ref, btok_ref, product_ref, grad_ref, sums_ref, flip_ref, part_sem,
    *, chunks, rows,
):
    rim = KCONV - 1
    per = PAIRS // PARTS
    span = per * LANE
    held = chunks // PARTS

    def finish(c, grad):
        edge_ref[:, lanes(c)] = grad[:rim]
        x = x_ref[:, lanes(c)].astype(F32)
        halo = halo_ref[:, lanes(c)].astype(F32)
        full = jnp.concatenate([grad, jnp.zeros((8, LANE), F32)], axis=0)
        spread = w_ref[rim : rim + 1, lanes(c)] * grad
        found = []
        for k in range(rim):
            moved = full[rim - k : rim - k + GROUP]
            spread = spread + w_ref[k : k + 1, lanes(c)] * moved
            entering = jnp.sum(grad[: rim - k] * halo[k:], axis=0, keepdims=True)
            found.append(jnp.sum(moved * x, axis=0, keepdims=True) + entering)
        found.append(jnp.sum(grad * x, axis=0, keepdims=True))
        found.append(jnp.sum(grad, axis=0, keepdims=True))
        found.append(jnp.zeros((8 - len(found), LANE), F32))
        sums_ref[c] = jnp.concatenate(found, axis=0)
        gin_ref[:, lanes(c)] = spread.astype(BF16)
        last_ref[:, lanes(c)] = spread[GROUP - 16 :]

    def begin(g):
        if g == PARTS:
            return started(part_sem.at[g], (x_hbm.at[:, X_WIDTH:], x_ref.at[:, X_WIDTH:]))
        at = slice(g * span, (g + 1) * span)
        return started(
            part_sem.at[g],
            (xwt_hbm.at[at], xwt_ref.at[at]),
            (dywt_hbm.at[at], dywt_ref.at[at]),
            (own_hbm.at[:, at], own_ref.at[:, at]),
            (scale_hbm.at[:, at], scale_ref.at[:, at]),
            (x_hbm.at[:, at], x_ref.at[:, at]),
        )

    coming = [begin(0), begin(1)]
    b_proj = bc_ref[:, :STATE]
    gb = gbin_ref[...]
    gc = gcin_ref[...]
    for g in range(PARTS):
        at = slice(g * span, (g + 1) * span)
        states = back_ref[g * held : (g + 1) * held, :rows, :].reshape(span, STATE)
        adjoint = back_ref[g * held : (g + 1) * held, rows:, :].reshape(span, STATE)
        cdot_ref[...] = mm(states, bct_ref[STATE:, :])
        bdot_ref[...] = mm(adjoint, bct_ref[:STATE, :])
        btok_ref[...] = mm(b_proj, adjoint, 1, 1)
        both = states.astype(F32) * adjoint.astype(F32)
        for i in range(2 * per):
            h = 2 * per * g + i
            product = both[i * HEAD_DIM : (i + 1) * HEAD_DIM]
            product_ref[h : h + 1, :] = jnp.sum(product, axis=0, keepdims=True)
        for copy in coming[g]:
            copy.wait()
        if g + 2 <= PARTS:
            coming.append(begin(g + 2))
        gb = gb + mm(adjoint, xwt_ref[at, :], 0, 0)
        gc = gc + mm(states, dywt_ref[at, :], 0, 0)

        def pair(p, carry, g=g):
            c = g * per + p
            c_dot = cdot_ref[lanes(p), :] * dywt_ref[lanes(c), :].astype(F32)
            b_dot = bdot_ref[lanes(p), :] * xwt_ref[lanes(c), :].astype(F32)
            for i in range(2):
                part = slice(i * HEAD_DIM, (i + 1) * HEAD_DIM)
                h = pl.ds(2 * c + i, 1)
                q_ref[h, :] = jnp.sum(c_dot[part], axis=0, keepdims=True)
                r_ref[h, :] = jnp.sum(b_dot[part], axis=0, keepdims=True)
            state_part = scale_ref[:, lanes(c)].astype(F32) * btok_ref[:, lanes(p)]
            finish(c, own_ref[:, lanes(c)] + state_part)
            return carry

        lax.fori_loop(0, per, pair, 0, unroll=True)
    for copy in coming[PARTS]:
        copy.wait()
    for i, total in enumerate((gb, gc)):
        grad_ref[...] = total
        finish(PAIRS + i, grad_ref[...].T * slope_ref[:, i * STATE : (i + 1) * STATE])

    four = end_ref[...] * jnp.sum(product_ref[...], axis=1, keepdims=True)
    four_ref[...] = four
    steps = step_ref[...]
    sofar = sofar_ref[...]
    every = sofar[:, GROUP - 1 :]
    own = row_ref[...] - colin_ref[...] - r_ref[...]
    met = steps * own - (every - sofar + steps) * own + sofar * q_ref[...]
    rates = -(jnp.sum(met, axis=1, keepdims=True) + four[:, :1] * every)
    skips = jnp.sum(skiprow_ref[...], axis=1, keepdims=True)
    flip_ref[...] = jnp.zeros_like(flip_ref)
    lane = lax.broadcasted_iota(jnp.int32, (HEADS, LANE), 1)
    flip_ref[:HEADS, :] = jnp.where(lane == 0, rates, 0.0) + jnp.where(lane == 1, skips, 0.0)
    tiles = PAIRS + 2
    for c in range(tiles):
        sums = sums_ref[c]
        for k in range(KCONV + 1):
            at = k * tiles + c
            params_ref[at : at + 1, :] = sums[k : k + 1]
    at = (KCONV + 1) * tiles
    params_ref[at : at + 2, :] = flip_ref[...].T[:2]


def log_kernel(q_ref, r_ref, four_ref, col_ref, row_ref, rate_ref, gsteps_ref):
    own = row_ref[...] - col_ref[...] - r_ref[...]
    running = mm(own, triangle(False), precision=HIGH)
    ending = mm(q_ref[...], triangle(True), precision=HIGH)
    grad_log = own - running + ending + four_ref[:, :1]
    gsteps_ref[...] = -head_column(rate_ref) * grad_log


def unpack_kernel(near_ref, far_ref, weight_ref, bias_ref, rates_ref, skip_ref, sum_ref):
    sum_ref[...] = near_ref[...] + far_ref[...]
    tiles = PAIRS + 2
    for c in range(tiles):
        at = slice(c * LANE, (c + 1) * LANE)
        for k in range(KCONV):
            weight_ref[k : k + 1, at] = sum_ref[k * tiles + c : k * tiles + c + 1, :]
        bias_ref[at] = sum_ref[KCONV * tiles + c, :]
    at = (KCONV + 1) * tiles
    rates_ref[...] = sum_ref[at, :HEADS]
    skip_ref[...] = sum_ref[at + 1, :HEADS]


def call(
    kernel, outs, scratch, *operands, large=0, scalars=0, kept=(), large_out=False, limit=VMEM_LIMIT
):
    small = len(operands) - large - scalars
    spaces = [pltpu.VMEM] * small + [pltpu.HBM] * large + [pltpu.SMEM] * scalars
    operands = [
        pltpu.with_memory_space_constraint(operand, pltpu.HBM)
        if space == pltpu.HBM
        else operand
        for operand, space in zip(operands, spaces)
    ]
    out_space = pltpu.HBM if large_out else pltpu.VMEM
    return pl.pallas_call(
        kernel,
        out_shape=[
            out_space(*out) if large_out or i in kept else jax.ShapeDtypeStruct(*out)
            for i, out in enumerate(outs)
        ],
        in_specs=[pl.BlockSpec(memory_space=space) for space in spaces],
        out_specs=[pl.BlockSpec(memory_space=out_space)] * len(outs),
        scratch_shapes=[pltpu.VMEM(*item) if isinstance(item, tuple) else item for item in scratch],
        compiler_params=pltpu.CompilerParams(vmem_limit_bytes=limit),
    )(*operands)


def shifted(array, axis, by):
    length = lax.axis_size(axis)
    pairs = [(i, i + by) for i in range(length) if 0 <= i + by < length]
    return lax.ppermute(array, axis, pairs)


def flipped(array, axis, bits):
    return lax.ppermute(array, axis, [(i, i ^ bits) for i in range(lax.axis_size(axis))])


def four_summed(array, axis, bit):
    near = flipped(array, axis, bit)
    far = flipped(array, axis, 2 * bit)
    both = flipped(array, axis, 3 * bit)
    return (array + near) + (far + both)


def shards(xbc_in, conv_weight, conv_bias, step_sizes, decay_rates, skip_gain, grad_out):
    channels = xbc_in.shape[2]
    rim = KCONV - 1
    chunks = lax.axis_size("seq")
    rows = X_WIDTH // chunks
    x_in = xbc_in[0]
    dy = grad_out[0]
    steps = step_sizes[0]
    wide_heads = ((HEADS, GROUP), F32)
    by_head = ((X_WIDTH, GROUP), BF16)
    dma = pltpu.SemaphoreType.DMA
    dywt, tail, head, x_rim = call(
        decay_kernel,
        [((X_WIDTH, GROUP), BF16), wide_heads, wide_heads, ((rim, channels), BF16)],
        [
            wide_heads,
            pltpu.SMEM((HEADS,), F32),
            ((GROUP, X_WIDTH), BF16),
            ((16, channels), BF16),
            dma((3,)),
            dma((PARTS,)),
        ],
        steps, decay_rates, dy, x_in, large=4, kept=(0,), limit=SMALL_LIMIT,
    )
    halo = shifted(x_rim, "seq", 1)
    (msg,) = call(
        functools.partial(front_kernel, chunks=chunks, rows=rows),
        [((chunks, 2 * rows + TAIL_ROWS, LANE), BF16)],
        [
            ((GROUP, channels), BF16),
            ((KCONV, channels), F32),
            ((channels,), F32),
            ((chunks, 2 * rows + TAIL_ROWS, LANE), BF16),
            ((GROUP, 2 * STATE), BF16),
            ((X_WIDTH // PARTS, GROUP), BF16),
            dma((3,)),
            dma((PARTS,)),
            dma((PARTS,)),
        ],
        halo, dywt, tail, head, x_in, conv_weight, conv_bias,
        large=3, large_out=True, limit=SMALL_LIMIT,
    )
    got = lax.all_to_all(msg, "seq", 0, 0, tiled=True)
    (own, scale, xwt, dywt, bc, bct, slope, gb, gc, col_sums, row_sums, skip_rows, sofar, d_end) = call(
        within_kernel,
        [
            ((GROUP, X_WIDTH), F32),
            ((GROUP, X_WIDTH), BF16),
            by_head,
            by_head,
            ((GROUP, 2 * STATE), BF16),
            ((2 * STATE, GROUP), BF16),
            ((GROUP, 2 * STATE), F32),
            ((STATE, GROUP), F32),
            ((STATE, GROUP), F32),
            wide_heads,
            wide_heads,
            wide_heads,
            wide_heads,
            ((HEADS, LANE), F32),
        ],
        [
            ((HEADS, GROUP, LANE), F32),
            ((GROUP, GROUP), F32),
            ((GROUP, GROUP), F32),
            ((LANE, GROUP), F32),
            ((LANE, GROUP), F32),
            wide_heads,
            wide_heads,
            wide_heads,
        ],
        x_in, halo, conv_weight, conv_bias, dy, steps, decay_rates, skip_gain, scalars=2,
    )
    got, own = lax.optimization_barrier((got, own))
    (turned,) = call(
        functools.partial(chain_kernel, chunks=chunks, rows=rows),
        [((chunks, 2 * rows, LANE), BF16)],
        [((chunks, 2 * rows, LANE), BF16), dma((4,))],
        got, large_out=True, limit=SMALL_LIMIT,
    )
    back = lax.all_to_all(turned, "seq", 0, 0, tiled=True)
    grad_in, last, edge, q_rows, r_rows, four, params = call(
        functools.partial(back_kernel, chunks=chunks, rows=rows),
        [
            ((GROUP, channels), BF16),
            ((16, channels), F32),
            ((rim, channels), F32),
            wide_heads,
            wide_heads,
            ((HEADS, LANE), F32),
            (((KCONV + 1) * (PAIRS + 2) + 2, LANE), F32),
        ],
        [
            ((GROUP, X_WIDTH), F32),
            ((GROUP, X_WIDTH), BF16),
            by_head,
            by_head,
            ((GROUP, channels), BF16),
            ((X_WIDTH // PARTS, GROUP), F32),
            ((X_WIDTH // PARTS, GROUP), F32),
            ((GROUP, X_WIDTH // PARTS), F32),
            ((HEADS, LANE), F32),
            ((STATE, GROUP), F32),
            ((PAIRS + 2, 8, LANE), F32),
            ((LANE, LANE), F32),
            dma((PARTS + 1, 5)),
        ],
        back, bc, bct, slope, gb, gc, col_sums, row_sums, skip_rows,
        halo, conv_weight, steps, sofar, d_end,
        own, scale, xwt, dywt, x_in,
        large=5, limit=SMALL_LIMIT,
    )
    sums = params + flipped(params, "dp", 1)
    sums, edge = lax.optimization_barrier((sums, edge))
    next_rows = shifted(edge, "seq", -1)
    sums = four_summed(sums, "dp", 2)
    sums, q_rows = lax.optimization_barrier((sums, q_rows))
    sums = four_summed(sums, "seq", 8)
    sums, last = lax.optimization_barrier((sums, last))
    sums = four_summed(sums, "seq", 1)
    far_sums = flipped(sums, "seq", 4)
    (gsteps,) = call(
        log_kernel, [wide_heads], [], q_rows, r_rows, four, col_sums, row_sums, decay_rates,
        scalars=1, limit=SMALL_LIMIT,
    )
    ahead = jnp.concatenate([jnp.zeros_like(next_rows), next_rows], axis=0)
    added = last[16 - rim :]
    for k in range(rim):
        added = added + conv_weight[k][None] * ahead[rim - k : 2 * rim - k]
    ending = jnp.concatenate([last[: 16 - rim], added], axis=0).astype(BF16)
    grad_in = lax.dynamic_update_slice(grad_in, ending, (GROUP - 16, 0))
    grad_weight, grad_bias, grad_rates, grad_skip = call(
        unpack_kernel,
        [((KCONV, channels), F32), ((channels,), F32), ((HEADS,), F32), ((HEADS,), F32)],
        [(params.shape, F32)],
        sums, far_sums, limit=SMALL_LIMIT,
    )
    return (grad_in[None], gsteps[None], grad_weight, grad_bias, grad_rates, grad_skip)


def solution(mesh):
    return jax.shard_map(
        shards,
        mesh=mesh,
        in_specs=(
            P("dp", "seq", None),
            P(),
            P(),
            P("dp", None, "seq"),
            P(),
            P(),
            P("dp", "seq", None),
        ),
        out_specs=(P("dp", "seq", None), P("dp", None, "seq"), P(), P(), P(), P()),
        check_vma=False,
    )
```

```python
import functools

import jax
import jax.numpy as jnp
from jax import lax
from jax.experimental import pallas as pl
from jax.experimental.pallas import tpu as pltpu
from jax.sharding import PartitionSpec as P

HEADS = 40
HEAD_DIM = 64
STATE = 128
GROUP = 256
KCONV = 4
LANE = 128
BF16 = jnp.bfloat16
F32 = jnp.float32
X_WIDTH = HEADS * HEAD_DIM
PAIRS = HEADS // 2
TAIL_ROWS = 8
VMEM_LIMIT = 56 * 1024 * 1024
SMALL_LIMIT = 24 * 1024 * 1024
PARTS = 4
HIGH = lax.Precision.HIGHEST


def mm(a, b, ca=1, cb=0, precision=None):
    return lax.dot_general(
        a, b, (((ca,), (cb,)), ((), ())), preferred_element_type=F32, precision=precision
    )


def lanes(c):
    return pl.ds(pl.multiple_of(c * LANE, LANE), LANE)


def taps_of(x_ref, halo_ref, c):
    full = jnp.concatenate(
        [
            jnp.zeros((8 - (KCONV - 1), LANE), F32),
            halo_ref[:, lanes(c)].astype(F32),
            x_ref[:, lanes(c)].astype(F32),
        ],
        axis=0,
    )
    return [full[5 + k : 5 + k + GROUP] for k in range(KCONV)]


def triangle(lower):
    row = lax.broadcasted_iota(jnp.int32, (GROUP, GROUP), 0)
    col = lax.broadcasted_iota(jnp.int32, (GROUP, GROUP), 1)
    return jnp.where(row >= col if lower else row <= col, 1.0, 0.0).astype(F32)


def head_column(scalar_ref):
    head = lax.broadcasted_iota(jnp.int32, (HEADS, GROUP), 0)
    found = jnp.zeros((HEADS, GROUP), F32)
    for h in range(HEADS):
        found = jnp.where(head == h, scalar_ref[h], found)
    return found


def pre_act_of(taps, w_ref, bias_ref, c):
    pre = bias_ref[lanes(c)].reshape(1, LANE)
    for k in range(KCONV):
        pre = pre + w_ref[k : k + 1, lanes(c)] * taps[k]
    return pre


def pair_rows(ref, c):
    return jnp.concatenate(
        [jnp.broadcast_to(ref[pl.ds(2 * c + i, 1), :], (HEAD_DIM, GROUP)) for i in range(2)], axis=0
    )


def started(sem, *pairs):
    made = [pltpu.make_async_copy(a, b, sem.at[i]) for i, (a, b) in enumerate(pairs)]
    for copy in made:
        copy.start()
    return made


def logs_of(step_ref, rate_ref):
    return mm(-(step_ref[...] * head_column(rate_ref)), triangle(False), precision=HIGH)


def decay_kernel(
    step_hbm, rate_hbm, dy_hbm,
    dywt_ref, tail_ref, head_ref,
    step_ref, rate_ref, dy_ref, few_sem, dy_sem,
):
    span = X_WIDTH // PARTS
    few = started(few_sem, (step_hbm, step_ref), (rate_hbm, rate_ref))
    cuts = [slice(g * span, (g + 1) * span) for g in range(PARTS)]
    many = started(dy_sem, *[(dy_hbm.at[:, cut], dy_ref.at[:, cut]) for cut in cuts])
    for copy in few:
        copy.wait()
    cum = logs_of(step_ref, rate_ref)
    tail_ref[...] = jnp.exp(cum[:, GROUP - 1 :] - cum)
    head_ref[...] = jnp.exp(cum)

    def turn(c, carry):
        head = pair_rows(head_ref, c)
        dywt_ref[lanes(c), :] = (dy_ref[:, lanes(c)].T.astype(F32) * head).astype(BF16)
        return carry

    per = PAIRS // PARTS
    for g in range(PARTS):
        many[g].wait()
        lax.fori_loop(g * per, (g + 1) * per, turn, 0, unroll=True)


def front_kernel(
    halo_ref, dywt_ref, tail_ref, head_ref,
    x_hbm, w_hbm, bias_hbm,
    msg_hbm,
    x_ref, w_ref, bias_ref, msg_ref, bc_ref, xwt_ref, few_sem, x_sem, msg_sem,
    *, chunks, rows,
):
    per = PAIRS // PARTS
    span = per * LANE
    held = chunks // PARTS
    few = started(
        few_sem, (w_hbm, w_ref), (bias_hbm, bias_ref), (x_hbm.at[:, X_WIDTH:], x_ref.at[:, X_WIDTH:])
    )
    cuts = [slice(g * span, (g + 1) * span) for g in range(PARTS)]
    many = started(x_sem, *[(x_hbm.at[:, cut], x_ref.at[:, cut]) for cut in cuts])

    d_end = jnp.broadcast_to(head_ref[:, GROUP - 1 :], (HEADS, LANE))
    part_a = d_end.astype(BF16).astype(F32)
    part_b = (d_end - part_a).astype(BF16).astype(F32)
    part_c = (d_end - part_a - part_b).astype(BF16).astype(F32)
    blank = jnp.zeros((TAIL_ROWS - 6, LANE), F32)
    for j in range(chunks):
        first = rows * j // HEAD_DIM
        last = (rows * j + rows - 1) // HEAD_DIM
        picked = [p[h : h + 1] for h in (first, last) for p in (part_a, part_b, part_c)]
        msg_ref[j, 2 * rows :, :] = jnp.concatenate(picked + [blank], axis=0).astype(BF16)

    def active(c):
        pre = pre_act_of(taps_of(x_ref, halo_ref, c), w_ref, bias_ref, c)
        return (pre * jax.nn.sigmoid(pre)).astype(BF16)

    for copy in few:
        copy.wait()
    bc_ref[:, :STATE] = active(PAIRS)
    bc_ref[:, STATE:] = active(PAIRS + 1)
    sent = []
    for g in range(PARTS):
        many[g].wait()

        def conv(p, carry, g=g):
            c = g * per + p
            tail = pair_rows(tail_ref, c)
            xwt_ref[lanes(p), :] = (active(c).T.astype(F32) * tail).astype(BF16)
            return carry

        lax.fori_loop(0, per, conv, 0, unroll=True)
        s_local = mm(xwt_ref[...], bc_ref[:, :STATE]).astype(BF16)
        u_local = mm(dywt_ref[cuts[g], :], bc_ref[:, STATE:]).astype(BF16)
        for i in range(held):
            at = slice(i * rows, (i + 1) * rows)
            msg_ref[g * held + i, :rows, :] = s_local[at]
            msg_ref[g * held + i, rows : 2 * rows, :] = u_local[at]
        block = slice(g * held, (g + 1) * held)
        sent.append(pltpu.make_async_copy(msg_ref.at[block], msg_hbm.at[block], msg_sem.at[g]))
        sent[-1].start()
    for copy in sent:
        copy.wait()


def within_kernel(
    x_ref, halo_ref, w_ref, bias_ref, dy_ref, step_ref, rate_ref, skip_ref,
    own_ref, scale_ref, xwt_ref, dywt_ref, bc_ref, bct_ref, slope_ref,
    gb_ref, gc_ref, col_ref, row_ref, skiprow_ref, sofar_ref, end_ref,
    column_ref, wsum_ref, cb_ref, hold_ref, base_ref, cum_ref, tail_ref, head_ref,
):
    cum = logs_of(step_ref, rate_ref)
    cum_ref[...] = cum
    tail_ref[...] = jnp.exp(cum[:, GROUP - 1 :] - cum)
    head_ref[...] = jnp.exp(cum)
    end_ref[...] = jnp.broadcast_to(jnp.exp(cum[:, GROUP - 1 :]), (HEADS, LANE))
    sofar_ref[...] = mm(step_ref[...], triangle(False), precision=HIGH)

    def conv(c):
        pre = pre_act_of(taps_of(x_ref, halo_ref, c), w_ref, bias_ref, c)
        sig = jax.nn.sigmoid(pre)
        return (pre * sig).astype(BF16), sig * (1.0 + pre * (1.0 - sig))

    for i in range(2):
        at = slice(i * STATE, (i + 1) * STATE)
        z, slope_ref[:, at] = conv(PAIRS + i)
        bc_ref[:, at] = z
        bct_ref[at, :] = z.T
    hold_ref[...] = jnp.zeros_like(hold_ref)
    hold_ref[:HEADS, :] = cum_ref[...]
    turned = hold_ref[...].T
    for h in range(HEADS):
        column_ref[h] = jnp.broadcast_to(turned[:, h : h + 1], (GROUP, LANE))
    wsum_ref[...] = jnp.zeros_like(wsum_ref)
    cb_ref[...] = mm(bc_ref[:, STATE:], bct_ref[:STATE, :])
    t_index = lax.broadcasted_iota(jnp.int32, (GROUP, GROUP), 0)
    s_index = lax.broadcasted_iota(jnp.int32, (GROUP, GROUP), 1)
    causal = t_index >= s_index

    def pair(c, carry):
        z, slope = conv(c)
        xt_pair = z.T
        dy_pair = dy_ref[:, lanes(c)]
        dyt_pair = dy_pair.T
        tail = pair_rows(tail_ref, c)
        head = pair_rows(head_ref, c)
        xwt_ref[lanes(c), :] = (xt_pair.astype(F32) * tail).astype(BF16)
        dywt_ref[lanes(c), :] = (dyt_pair.astype(F32) * head).astype(BF16)
        scale_ref[:, lanes(c)] = (tail.T * slope).astype(BF16)
        zero = jnp.zeros((HEAD_DIM, GROUP), BF16)
        total = wsum_ref[...]
        for i in range(2):
            h = 2 * c + i
            at = pl.ds(h, 1)
            part = slice(i * HEAD_DIM, (i + 1) * HEAD_DIM)
            xt = xt_pair[part]
            dyt = dyt_pair[part]
            wide = jnp.concatenate([xt, zero] if i == 0 else [zero, xt], axis=0)
            inner = mm(dy_pair, wide)
            column = column_ref[h]
            column = jnp.concatenate([column, column], axis=1)
            gap = column - cum_ref[at, :]
            decay = jnp.exp(jnp.where(causal, gap, -jnp.inf))
            total = total + decay * inner
            kt = (decay * cb_ref[...]).astype(BF16)
            intra = mm(dyt, kt)
            forth = mm(xt, kt, 1, 1)
            xf = xt.astype(F32)
            dyf = dyt.astype(F32)
            base_ref[part, :] = intra + skip_ref[h] * dyf
            col_ref[at, :] = jnp.sum(intra * xf, axis=0, keepdims=True)
            row_ref[at, :] = jnp.sum(forth * dyf, axis=0, keepdims=True)
            skiprow_ref[at, :] = jnp.sum(xf * dyf, axis=0, keepdims=True)
        wsum_ref[...] = total
        own_ref[:, lanes(c)] = base_ref[...].T * slope
        return carry

    lax.fori_loop(0, PAIRS, pair, 0)
    w_summed = wsum_ref[...].astype(BF16)
    gb_ref[...] = mm(bct_ref[STATE:, :], w_summed)
    gc_ref[...] = mm(bct_ref[:STATE, :], w_summed, 1, 1)


def chain_kernel(got_ref, out_hbm, out_ref, sem, *, chunks, rows):
    j = lax.axis_index("seq")
    split = HEAD_DIM - lax.rem(rows * j, HEAD_DIM)
    ahead = lax.broadcasted_iota(jnp.int32, (rows, LANE), 0) < split

    def decay_of(i):
        ends = got_ref[i, 2 * rows :, :].astype(F32)
        one = ends[0:1] + ends[1:2] + ends[2:3]
        two = ends[3:4] + ends[4:5] + ends[5:6]
        return jnp.where(ahead, one, two)

    def step(k, carry):
        state, adjoint = carry
        out_ref[k, :rows, :] = state.astype(BF16)
        state = decay_of(k) * state + got_ref[k, :rows, :].astype(F32)
        m = chunks - 1 - k
        out_ref[m, rows:, :] = adjoint.astype(BF16)
        adjoint = decay_of(m) * adjoint + got_ref[m, rows : 2 * rows, :].astype(F32)
        return state, adjoint

    carry = (jnp.zeros((rows, LANE), F32), jnp.zeros((rows, LANE), F32))
    half = chunks // 2
    sent = []
    for g in range(2):
        carry = lax.fori_loop(g * half, (g + 1) * half, step, carry, unroll=4)
        fore = (slice(g * half, (g + 1) * half), slice(0, rows))
        rear = (slice((1 - g) * half, (2 - g) * half), slice(rows, 2 * rows))
        for i, at in enumerate((fore, rear)):
            sent.append(pltpu.make_async_copy(out_ref.at[at], out_hbm.at[at], sem.at[2 * g + i]))
            sent[-1].start()
    for copy in sent:
        copy.wait()


def back_kernel(
    back_ref, bc_ref, bct_ref, slope_ref,
    gbin_ref, gcin_ref, colin_ref, row_ref, skiprow_ref,
    halo_ref, step_ref, sofar_ref, end_ref,
    own_hbm, scale_hbm, xwt_hbm, dywt_hbm, x_hbm,
    gpre_ref, edge_ref, q_ref, r_ref, four_ref, params_ref,
    own_ref, scale_ref, xwt_ref, dywt_ref, x_ref,
    cdot_ref, bdot_ref, btok_ref, product_ref, grad_ref, sums_ref, flip_ref, part_sem,
    *, chunks, rows,
):
    rim = KCONV - 1
    per = PAIRS // PARTS
    span = per * LANE
    held = chunks // PARTS

    def finish(c, grad):
        edge_ref[:, lanes(c)] = grad[:rim]
        gpre_ref[:, lanes(c)] = grad
        x = x_ref[:, lanes(c)].astype(F32)
        halo = halo_ref[:, lanes(c)].astype(F32)
        full = jnp.concatenate([grad, jnp.zeros((8, LANE), F32)], axis=0)
        found = []
        for k in range(rim):
            moved = full[rim - k : rim - k + GROUP]
            entering = jnp.sum(grad[: rim - k] * halo[k:], axis=0, keepdims=True)
            found.append(jnp.sum(moved * x, axis=0, keepdims=True) + entering)
        found.append(jnp.sum(grad * x, axis=0, keepdims=True))
        found.append(jnp.sum(grad, axis=0, keepdims=True))
        found.append(jnp.zeros((8 - len(found), LANE), F32))
        sums_ref[c] = jnp.concatenate(found, axis=0)

    def begin(g):
        if g == PARTS:
            return started(part_sem.at[g], (x_hbm.at[:, X_WIDTH:], x_ref.at[:, X_WIDTH:]))
        at = slice(g * span, (g + 1) * span)
        return started(
            part_sem.at[g],
            (xwt_hbm.at[at], xwt_ref.at[at]),
            (dywt_hbm.at[at], dywt_ref.at[at]),
            (own_hbm.at[:, at], own_ref.at[:, at]),
            (scale_hbm.at[:, at], scale_ref.at[:, at]),
            (x_hbm.at[:, at], x_ref.at[:, at]),
        )

    coming = [begin(0), begin(1)]
    b_proj = bc_ref[:, :STATE]
    gb = gbin_ref[...]
    gc = gcin_ref[...]
    for g in range(PARTS):
        at = slice(g * span, (g + 1) * span)
        states = back_ref[g * held : (g + 1) * held, :rows, :].reshape(span, STATE)
        adjoint = back_ref[g * held : (g + 1) * held, rows:, :].reshape(span, STATE)
        cdot_ref[...] = mm(states, bct_ref[STATE:, :])
        bdot_ref[...] = mm(adjoint, bct_ref[:STATE, :])
        btok_ref[...] = mm(b_proj, adjoint, 1, 1)
        both = states.astype(F32) * adjoint.astype(F32)
        for i in range(2 * per):
            h = 2 * per * g + i
            product = both[i * HEAD_DIM : (i + 1) * HEAD_DIM]
            product_ref[h : h + 1, :] = jnp.sum(product, axis=0, keepdims=True)
        for copy in coming[g]:
            copy.wait()
        if g + 2 <= PARTS:
            coming.append(begin(g + 2))
        gb = gb + mm(adjoint, xwt_ref[at, :], 0, 0)
        gc = gc + mm(states, dywt_ref[at, :], 0, 0)

        def pair(p, carry, g=g):
            c = g * per + p
            c_dot = cdot_ref[lanes(p), :] * dywt_ref[lanes(c), :].astype(F32)
            b_dot = bdot_ref[lanes(p), :] * xwt_ref[lanes(c), :].astype(F32)
            for i in range(2):
                part = slice(i * HEAD_DIM, (i + 1) * HEAD_DIM)
                h = pl.ds(2 * c + i, 1)
                q_ref[h, :] = jnp.sum(c_dot[part], axis=0, keepdims=True)
                r_ref[h, :] = jnp.sum(b_dot[part], axis=0, keepdims=True)
            state_part = scale_ref[:, lanes(c)].astype(F32) * btok_ref[:, lanes(p)]
            finish(c, own_ref[:, lanes(c)] + state_part)
            return carry

        lax.fori_loop(0, per, pair, 0, unroll=True)
    for copy in coming[PARTS]:
        copy.wait()
    for i, total in enumerate((gb, gc)):
        grad_ref[...] = total
        finish(PAIRS + i, grad_ref[...].T * slope_ref[:, i * STATE : (i + 1) * STATE])

    four = end_ref[...] * jnp.sum(product_ref[...], axis=1, keepdims=True)
    four_ref[...] = four
    steps = step_ref[...]
    sofar = sofar_ref[...]
    every = sofar[:, GROUP - 1 :]
    own = row_ref[...] - colin_ref[...] - r_ref[...]
    met = steps * own - (every - sofar + steps) * own + sofar * q_ref[...]
    rates = -(jnp.sum(met, axis=1, keepdims=True) + four[:, :1] * every)
    skips = jnp.sum(skiprow_ref[...], axis=1, keepdims=True)
    flip_ref[...] = jnp.zeros_like(flip_ref)
    lane = lax.broadcasted_iota(jnp.int32, (HEADS, LANE), 1)
    flip_ref[:HEADS, :] = jnp.where(lane == 0, rates, 0.0) + jnp.where(lane == 1, skips, 0.0)
    tiles = PAIRS + 2
    for c in range(tiles):
        sums = sums_ref[c]
        for k in range(KCONV + 1):
            at = k * tiles + c
            params_ref[at : at + 1, :] = sums[k : k + 1]
    at = (KCONV + 1) * tiles
    params_ref[at : at + 2, :] = flip_ref[...].T[:2]


def spread_kernel(gpre_ref, next_ref, w_ref, gin_ref):
    rim = KCONV - 1

    def tile(c, carry):
        grad = gpre_ref[:, lanes(c)]
        below = jnp.concatenate([next_ref[:, lanes(c)], jnp.zeros((8 - rim, LANE), F32)], axis=0)
        full = jnp.concatenate([grad, below], axis=0)
        spread = w_ref[rim : rim + 1, lanes(c)] * grad
        for k in range(rim):
            spread = spread + w_ref[k : k + 1, lanes(c)] * full[rim - k : rim - k + GROUP]
        gin_ref[:, lanes(c)] = spread.astype(BF16)
        return carry

    lax.fori_loop(0, PAIRS + 2, tile, 0, unroll=2)


def log_kernel(q_ref, r_ref, four_ref, col_ref, row_ref, rate_ref, gsteps_ref):
    own = row_ref[...] - col_ref[...] - r_ref[...]
    running = mm(own, triangle(False), precision=HIGH)
    ending = mm(q_ref[...], triangle(True), precision=HIGH)
    grad_log = own - running + ending + four_ref[:, :1]
    gsteps_ref[...] = -head_column(rate_ref) * grad_log


def unpack_kernel(near_ref, far_ref, weight_ref, bias_ref, rates_ref, skip_ref, sum_ref):
    sum_ref[...] = near_ref[...] + far_ref[...]
    tiles = PAIRS + 2
    for c in range(tiles):
        at = slice(c * LANE, (c + 1) * LANE)
        for k in range(KCONV):
            weight_ref[k : k + 1, at] = sum_ref[k * tiles + c : k * tiles + c + 1, :]
        bias_ref[at] = sum_ref[KCONV * tiles + c, :]
    at = (KCONV + 1) * tiles
    rates_ref[...] = sum_ref[at, :HEADS]
    skip_ref[...] = sum_ref[at + 1, :HEADS]


def call(
    kernel, outs, scratch, *operands, large=0, scalars=0, kept=(), large_out=False, limit=VMEM_LIMIT
):
    small = len(operands) - large - scalars
    spaces = [pltpu.VMEM] * small + [pltpu.HBM] * large + [pltpu.SMEM] * scalars
    operands = [
        pltpu.with_memory_space_constraint(operand, pltpu.HBM)
        if space == pltpu.HBM
        else operand
        for operand, space in zip(operands, spaces)
    ]
    out_space = pltpu.HBM if large_out else pltpu.VMEM
    return pl.pallas_call(
        kernel,
        out_shape=[
            out_space(*out) if large_out or i in kept else jax.ShapeDtypeStruct(*out)
            for i, out in enumerate(outs)
        ],
        in_specs=[pl.BlockSpec(memory_space=space) for space in spaces],
        out_specs=[pl.BlockSpec(memory_space=out_space)] * len(outs),
        scratch_shapes=[pltpu.VMEM(*item) if isinstance(item, tuple) else item for item in scratch],
        compiler_params=pltpu.CompilerParams(vmem_limit_bytes=limit),
    )(*operands)


def shifted(array, axis, by):
    length = lax.axis_size(axis)
    pairs = [(i, i + by) for i in range(length) if 0 <= i + by < length]
    return lax.ppermute(array, axis, pairs)


def flipped(array, axis, bits):
    return lax.ppermute(array, axis, [(i, i ^ bits) for i in range(lax.axis_size(axis))])


def four_summed(array, axis, bit):
    near = flipped(array, axis, bit)
    far = flipped(array, axis, 2 * bit)
    both = flipped(array, axis, 3 * bit)
    return (array + near) + (far + both)


def shards(xbc_in, conv_weight, conv_bias, step_sizes, decay_rates, skip_gain, grad_out):
    channels = xbc_in.shape[2]
    rim = KCONV - 1
    chunks = lax.axis_size("seq")
    rows = X_WIDTH // chunks
    x_in = xbc_in[0]
    dy = grad_out[0]
    steps = step_sizes[0]
    wide_heads = ((HEADS, GROUP), F32)
    by_head = ((X_WIDTH, GROUP), BF16)
    dma = pltpu.SemaphoreType.DMA
    halo = shifted(x_in[GROUP - rim :], "seq", 1)
    dywt, tail, head = call(
        decay_kernel,
        [((X_WIDTH, GROUP), BF16), wide_heads, wide_heads],
        [wide_heads, pltpu.SMEM((HEADS,), F32), ((GROUP, X_WIDTH), BF16), dma((2,)), dma((PARTS,))],
        steps, decay_rates, dy, large=3, kept=(0,), limit=SMALL_LIMIT,
    )
    (msg,) = call(
        functools.partial(front_kernel, chunks=chunks, rows=rows),
        [((chunks, 2 * rows + TAIL_ROWS, LANE), BF16)],
        [
            ((GROUP, channels), BF16),
            ((KCONV, channels), F32),
            ((channels,), F32),
            ((chunks, 2 * rows + TAIL_ROWS, LANE), BF16),
            ((GROUP, 2 * STATE), BF16),
            ((X_WIDTH // PARTS, GROUP), BF16),
            dma((3,)),
            dma((PARTS,)),
            dma((PARTS,)),
        ],
        halo, dywt, tail, head, x_in, conv_weight, conv_bias,
        large=3, large_out=True, limit=SMALL_LIMIT,
    )
    got = lax.all_to_all(msg, "seq", 0, 0, tiled=True)
    (own, scale, xwt, dywt, bc, bct, slope, gb, gc, col_sums, row_sums, skip_rows, sofar, d_end) = call(
        within_kernel,
        [
            ((GROUP, X_WIDTH), F32),
            ((GROUP, X_WIDTH), BF16),
            by_head,
            by_head,
            ((GROUP, 2 * STATE), BF16),
            ((2 * STATE, GROUP), BF16),
            ((GROUP, 2 * STATE), F32),
            ((STATE, GROUP), F32),
            ((STATE, GROUP), F32),
            wide_heads,
            wide_heads,
            wide_heads,
            wide_heads,
            ((HEADS, LANE), F32),
        ],
        [
            ((HEADS, GROUP, LANE), F32),
            ((GROUP, GROUP), F32),
            ((GROUP, GROUP), F32),
            ((LANE, GROUP), F32),
            ((LANE, GROUP), F32),
            wide_heads,
            wide_heads,
            wide_heads,
        ],
        x_in, halo, conv_weight, conv_bias, dy, steps, decay_rates, skip_gain, scalars=2,
    )
    got, own = lax.optimization_barrier((got, own))
    (turned,) = call(
        functools.partial(chain_kernel, chunks=chunks, rows=rows),
        [((chunks, 2 * rows, LANE), BF16)],
        [((chunks, 2 * rows, LANE), BF16), dma((4,))],
        got, large_out=True, limit=SMALL_LIMIT,
    )
    back = lax.all_to_all(turned, "seq", 0, 0, tiled=True)
    gpre, edge, q_rows, r_rows, four, params = call(
        functools.partial(back_kernel, chunks=chunks, rows=rows),
        [
            ((GROUP, channels), F32),
            ((rim, channels), F32),
            wide_heads,
            wide_heads,
            ((HEADS, LANE), F32),
            (((KCONV + 1) * (PAIRS + 2) + 2, LANE), F32),
        ],
        [
            ((GROUP, X_WIDTH), F32),
            ((GROUP, X_WIDTH), BF16),
            by_head,
            by_head,
            ((GROUP, channels), BF16),
            ((X_WIDTH // PARTS, GROUP), F32),
            ((X_WIDTH // PARTS, GROUP), F32),
            ((GROUP, X_WIDTH // PARTS), F32),
            ((HEADS, LANE), F32),
            ((STATE, GROUP), F32),
            ((PAIRS + 2, 8, LANE), F32),
            ((LANE, LANE), F32),
            dma((PARTS + 1, 5)),
        ],
        back, bc, bct, slope, gb, gc, col_sums, row_sums, skip_rows,
        halo, steps, sofar, d_end,
        own, scale, xwt, dywt, x_in,
        large=5, limit=SMALL_LIMIT,
    )
    sums = params + flipped(params, "dp", 1)
    sums, edge, q_rows = lax.optimization_barrier((sums, edge, q_rows))
    next_rows = shifted(edge, "seq", -1)
    (gsteps,) = call(
        log_kernel, [wide_heads], [], q_rows, r_rows, four, col_sums, row_sums, decay_rates,
        scalars=1, limit=SMALL_LIMIT,
    )
    sums = four_summed(sums, "dp", 2)
    sums, gsteps = lax.optimization_barrier((sums, gsteps))
    sums = four_summed(sums, "seq", 8)
    sums, next_rows = lax.optimization_barrier((sums, next_rows))
    sums = four_summed(sums, "seq", 1)
    sums, gpre = lax.optimization_barrier((sums, gpre))
    far_sums = flipped(sums, "seq", 4)
    (grad_in,) = call(
        spread_kernel, [((GROUP, channels), BF16)], [], gpre, next_rows, conv_weight,
        limit=SMALL_LIMIT,
    )
    grad_weight, grad_bias, grad_rates, grad_skip = call(
        unpack_kernel,
        [((KCONV, channels), F32), ((channels,), F32), ((HEADS,), F32), ((HEADS,), F32)],
        [(params.shape, F32)],
        sums, far_sums, limit=SMALL_LIMIT,
    )
    return (grad_in[None], gsteps[None], grad_weight, grad_bias, grad_rates, grad_skip)


def solution(mesh):
    return jax.shard_map(
        shards,
        mesh=mesh,
        in_specs=(
            P("dp", "seq", None),
            P(),
            P(),
            P("dp", None, "seq"),
            P(),
            P(),
            P("dp", "seq", None),
        ),
        out_specs=(P("dp", "seq", None), P("dp", None, "seq"), P(), P(), P(), P()),
        check_vma=False,
    )
```

```python
import functools

import jax
import jax.numpy as jnp
from jax import lax
from jax.experimental import pallas as pl
from jax.experimental.pallas import tpu as pltpu
from jax.sharding import PartitionSpec as P

HEADS = 40
HEAD_DIM = 64
STATE = 128
GROUP = 256
KCONV = 4
LANE = 128
BF16 = jnp.bfloat16
F32 = jnp.float32
X_WIDTH = HEADS * HEAD_DIM
PAIRS = HEADS // 2
TAIL_ROWS = 8
VMEM_LIMIT = 56 * 1024 * 1024
SMALL_LIMIT = 24 * 1024 * 1024
PARTS = 4
HIGH = lax.Precision.HIGHEST


def mm(a, b, ca=1, cb=0, precision=None):
    return lax.dot_general(
        a, b, (((ca,), (cb,)), ((), ())), preferred_element_type=F32, precision=precision
    )


def lanes(c):
    return pl.ds(pl.multiple_of(c * LANE, LANE), LANE)


def taps_of(x_ref, halo_ref, c):
    full = jnp.concatenate(
        [
            jnp.zeros((8 - (KCONV - 1), LANE), F32),
            halo_ref[:, lanes(c)].astype(F32),
            x_ref[:, lanes(c)].astype(F32),
        ],
        axis=0,
    )
    return [full[5 + k : 5 + k + GROUP] for k in range(KCONV)]


def triangle(lower):
    row = lax.broadcasted_iota(jnp.int32, (GROUP, GROUP), 0)
    col = lax.broadcasted_iota(jnp.int32, (GROUP, GROUP), 1)
    return jnp.where(row >= col if lower else row <= col, 1.0, 0.0).astype(F32)


def head_column(scalar_ref):
    head = lax.broadcasted_iota(jnp.int32, (HEADS, GROUP), 0)
    found = jnp.zeros((HEADS, GROUP), F32)
    for h in range(HEADS):
        found = jnp.where(head == h, scalar_ref[h], found)
    return found


def pre_act_of(taps, w_ref, bias_ref, c):
    pre = bias_ref[lanes(c)].reshape(1, LANE)
    for k in range(KCONV):
        pre = pre + w_ref[k : k + 1, lanes(c)] * taps[k]
    return pre


def pair_rows(ref, c):
    return jnp.concatenate(
        [jnp.broadcast_to(ref[pl.ds(2 * c + i, 1), :], (HEAD_DIM, GROUP)) for i in range(2)], axis=0
    )


def started(sem, *pairs):
    made = [pltpu.make_async_copy(a, b, sem.at[i]) for i, (a, b) in enumerate(pairs)]
    for copy in made:
        copy.start()
    return made


def logs_of(step_ref, rate_ref):
    return mm(-(step_ref[...] * head_column(rate_ref)), triangle(False), precision=HIGH)


def decay_kernel(
    step_hbm, rate_hbm, dy_hbm,
    dywt_ref, tail_ref, head_ref,
    step_ref, rate_ref, dy_ref, few_sem, dy_sem,
):
    span = X_WIDTH // PARTS
    few = started(few_sem, (step_hbm, step_ref), (rate_hbm, rate_ref))
    cuts = [slice(g * span, (g + 1) * span) for g in range(PARTS)]
    many = started(dy_sem, *[(dy_hbm.at[:, cut], dy_ref.at[:, cut]) for cut in cuts])
    for copy in few:
        copy.wait()
    cum = logs_of(step_ref, rate_ref)
    tail_ref[...] = jnp.exp(cum[:, GROUP - 1 :] - cum)
    head_ref[...] = jnp.exp(cum)

    def turn(c, carry):
        head = pair_rows(head_ref, c)
        dywt_ref[lanes(c), :] = (dy_ref[:, lanes(c)].T.astype(F32) * head).astype(BF16)
        return carry

    per = PAIRS // PARTS
    for g in range(PARTS):
        many[g].wait()
        lax.fori_loop(g * per, (g + 1) * per, turn, 0, unroll=True)


def front_kernel(
    halo_ref, dywt_ref, tail_ref, head_ref,
    x_hbm, w_hbm, bias_hbm,
    msg_hbm,
    x_ref, w_ref, bias_ref, msg_ref, bc_ref, xwt_ref, few_sem, x_sem, msg_sem,
    *, chunks, rows,
):
    per = PAIRS // PARTS
    span = per * LANE
    held = chunks // PARTS
    few = started(
        few_sem, (w_hbm, w_ref), (bias_hbm, bias_ref), (x_hbm.at[:, X_WIDTH:], x_ref.at[:, X_WIDTH:])
    )
    cuts = [slice(g * span, (g + 1) * span) for g in range(PARTS)]
    many = started(x_sem, *[(x_hbm.at[:, cut], x_ref.at[:, cut]) for cut in cuts])

    d_end = jnp.broadcast_to(head_ref[:, GROUP - 1 :], (HEADS, LANE))
    part_a = d_end.astype(BF16).astype(F32)
    part_b = (d_end - part_a).astype(BF16).astype(F32)
    part_c = (d_end - part_a - part_b).astype(BF16).astype(F32)
    blank = jnp.zeros((TAIL_ROWS - 6, LANE), F32)
    for j in range(chunks):
        first = rows * j // HEAD_DIM
        last = (rows * j + rows - 1) // HEAD_DIM
        picked = [p[h : h + 1] for h in (first, last) for p in (part_a, part_b, part_c)]
        msg_ref[j, 2 * rows :, :] = jnp.concatenate(picked + [blank], axis=0).astype(BF16)

    def active(c):
        pre = pre_act_of(taps_of(x_ref, halo_ref, c), w_ref, bias_ref, c)
        return (pre * jax.nn.sigmoid(pre)).astype(BF16)

    for copy in few:
        copy.wait()
    bc_ref[:, :STATE] = active(PAIRS)
    bc_ref[:, STATE:] = active(PAIRS + 1)
    sent = []
    for g in range(PARTS):
        many[g].wait()

        def conv(p, carry, g=g):
            c = g * per + p
            tail = pair_rows(tail_ref, c)
            xwt_ref[lanes(p), :] = (active(c).T.astype(F32) * tail).astype(BF16)
            return carry

        lax.fori_loop(0, per, conv, 0, unroll=True)
        s_local = mm(xwt_ref[...], bc_ref[:, :STATE]).astype(BF16)
        u_local = mm(dywt_ref[cuts[g], :], bc_ref[:, STATE:]).astype(BF16)
        for i in range(held):
            at = slice(i * rows, (i + 1) * rows)
            msg_ref[g * held + i, :rows, :] = s_local[at]
            msg_ref[g * held + i, rows : 2 * rows, :] = u_local[at]
        block = slice(g * held, (g + 1) * held)
        sent.append(pltpu.make_async_copy(msg_ref.at[block], msg_hbm.at[block], msg_sem.at[g]))
        sent[-1].start()
    for copy in sent:
        copy.wait()


def within_kernel(
    x_ref, halo_ref, w_ref, bias_ref, dy_ref, step_ref, rate_ref, skip_ref,
    own_ref, scale_ref, xwt_ref, dywt_ref, bc_ref, bct_ref, slope_ref,
    gb_ref, gc_ref, col_ref, row_ref, skiprow_ref, sofar_ref, end_ref,
    column_ref, wsum_ref, cb_ref, hold_ref, base_ref, cum_ref, tail_ref, head_ref,
):
    cum = logs_of(step_ref, rate_ref)
    cum_ref[...] = cum
    tail_ref[...] = jnp.exp(cum[:, GROUP - 1 :] - cum)
    head_ref[...] = jnp.exp(cum)
    end_ref[...] = jnp.broadcast_to(jnp.exp(cum[:, GROUP - 1 :]), (HEADS, LANE))
    sofar_ref[...] = mm(step_ref[...], triangle(False), precision=HIGH)

    def conv(c):
        pre = pre_act_of(taps_of(x_ref, halo_ref, c), w_ref, bias_ref, c)
        sig = jax.nn.sigmoid(pre)
        return (pre * sig).astype(BF16), sig * (1.0 + pre * (1.0 - sig))

    for i in range(2):
        at = slice(i * STATE, (i + 1) * STATE)
        z, slope_ref[:, at] = conv(PAIRS + i)
        bc_ref[:, at] = z
        bct_ref[at, :] = z.T
    hold_ref[...] = jnp.zeros_like(hold_ref)
    hold_ref[:HEADS, :] = cum_ref[...]
    turned = hold_ref[...].T
    for h in range(HEADS):
        column_ref[h] = jnp.broadcast_to(turned[:, h : h + 1], (GROUP, LANE))
    wsum_ref[...] = jnp.zeros_like(wsum_ref)
    cb_ref[...] = mm(bc_ref[:, STATE:], bct_ref[:STATE, :])
    t_index = lax.broadcasted_iota(jnp.int32, (GROUP, GROUP), 0)
    s_index = lax.broadcasted_iota(jnp.int32, (GROUP, GROUP), 1)
    causal = t_index >= s_index

    def pair(c, carry):
        z, slope = conv(c)
        xt_pair = z.T
        dy_pair = dy_ref[:, lanes(c)]
        dyt_pair = dy_pair.T
        tail = pair_rows(tail_ref, c)
        head = pair_rows(head_ref, c)
        xwt_ref[lanes(c), :] = (xt_pair.astype(F32) * tail).astype(BF16)
        dywt_ref[lanes(c), :] = (dyt_pair.astype(F32) * head).astype(BF16)
        scale_ref[:, lanes(c)] = (tail.T * slope).astype(BF16)
        zero = jnp.zeros((HEAD_DIM, GROUP), BF16)
        total = wsum_ref[...]
        for i in range(2):
            h = 2 * c + i
            at = pl.ds(h, 1)
            part = slice(i * HEAD_DIM, (i + 1) * HEAD_DIM)
            xt = xt_pair[part]
            dyt = dyt_pair[part]
            wide = jnp.concatenate([xt, zero] if i == 0 else [zero, xt], axis=0)
            inner = mm(dy_pair, wide)
            column = column_ref[h]
            column = jnp.concatenate([column, column], axis=1)
            gap = column - cum_ref[at, :]
            decay = jnp.exp(jnp.where(causal, gap, -jnp.inf))
            total = total + decay * inner
            kt = (decay * cb_ref[...]).astype(BF16)
            intra = mm(dyt, kt)
            forth = mm(xt, kt, 1, 1)
            xf = xt.astype(F32)
            dyf = dyt.astype(F32)
            base_ref[part, :] = intra + skip_ref[h] * dyf
            col_ref[at, :] = jnp.sum(intra * xf, axis=0, keepdims=True)
            row_ref[at, :] = jnp.sum(forth * dyf, axis=0, keepdims=True)
            skiprow_ref[at, :] = jnp.sum(xf * dyf, axis=0, keepdims=True)
        wsum_ref[...] = total
        own_ref[:, lanes(c)] = base_ref[...].T * slope
        return carry

    lax.fori_loop(0, PAIRS, pair, 0)
    w_summed = wsum_ref[...].astype(BF16)
    gb_ref[...] = mm(bct_ref[STATE:, :], w_summed)
    gc_ref[...] = mm(bct_ref[:STATE, :], w_summed, 1, 1)


def chain_kernel(got_ref, out_hbm, out_ref, sem, *, chunks, rows):
    j = lax.axis_index("seq")
    split = HEAD_DIM - lax.rem(rows * j, HEAD_DIM)
    ahead = lax.broadcasted_iota(jnp.int32, (rows, LANE), 0) < split

    def decay_of(i):
        ends = got_ref[i, 2 * rows :, :].astype(F32)
        one = ends[0:1] + ends[1:2] + ends[2:3]
        two = ends[3:4] + ends[4:5] + ends[5:6]
        return jnp.where(ahead, one, two)

    def step(k, carry):
        state, adjoint = carry
        out_ref[k, :rows, :] = state.astype(BF16)
        state = decay_of(k) * state + got_ref[k, :rows, :].astype(F32)
        m = chunks - 1 - k
        out_ref[m, rows:, :] = adjoint.astype(BF16)
        adjoint = decay_of(m) * adjoint + got_ref[m, rows : 2 * rows, :].astype(F32)
        return state, adjoint

    carry = (jnp.zeros((rows, LANE), F32), jnp.zeros((rows, LANE), F32))
    half = chunks // 2
    sent = []
    for g in range(2):
        carry = lax.fori_loop(g * half, (g + 1) * half, step, carry, unroll=4)
        fore = (slice(g * half, (g + 1) * half), slice(0, rows))
        rear = (slice((1 - g) * half, (2 - g) * half), slice(rows, 2 * rows))
        for i, at in enumerate((fore, rear)):
            sent.append(pltpu.make_async_copy(out_ref.at[at], out_hbm.at[at], sem.at[2 * g + i]))
            sent[-1].start()
    for copy in sent:
        copy.wait()


def back_kernel(
    back_ref, bc_ref, bct_ref, slope_ref,
    gbin_ref, gcin_ref, colin_ref, row_ref, skiprow_ref,
    halo_ref, step_ref, sofar_ref, end_ref,
    own_hbm, scale_hbm, xwt_hbm, dywt_hbm, x_hbm,
    gpre_ref, edge_ref, q_ref, r_ref, four_ref, params_ref,
    own_ref, scale_ref, xwt_ref, dywt_ref, x_ref,
    cdot_ref, bdot_ref, btok_ref, product_ref, grad_ref, sums_ref, flip_ref, part_sem,
    *, chunks, rows,
):
    rim = KCONV - 1
    per = PAIRS // PARTS
    span = per * LANE
    held = chunks // PARTS

    def finish(c, grad):
        edge_ref[:, lanes(c)] = grad[:rim]
        gpre_ref[:, lanes(c)] = grad
        x = x_ref[:, lanes(c)].astype(F32)
        halo = halo_ref[:, lanes(c)].astype(F32)
        full = jnp.concatenate([grad, jnp.zeros((8, LANE), F32)], axis=0)
        found = []
        for k in range(rim):
            moved = full[rim - k : rim - k + GROUP]
            entering = jnp.sum(grad[: rim - k] * halo[k:], axis=0, keepdims=True)
            found.append(jnp.sum(moved * x, axis=0, keepdims=True) + entering)
        found.append(jnp.sum(grad * x, axis=0, keepdims=True))
        found.append(jnp.sum(grad, axis=0, keepdims=True))
        found.append(jnp.zeros((8 - len(found), LANE), F32))
        sums_ref[c] = jnp.concatenate(found, axis=0)

    def begin(g):
        if g == PARTS:
            return started(part_sem.at[g], (x_hbm.at[:, X_WIDTH:], x_ref.at[:, X_WIDTH:]))
        at = slice(g * span, (g + 1) * span)
        return started(
            part_sem.at[g],
            (xwt_hbm.at[at], xwt_ref.at[at]),
            (dywt_hbm.at[at], dywt_ref.at[at]),
            (own_hbm.at[:, at], own_ref.at[:, at]),
            (scale_hbm.at[:, at], scale_ref.at[:, at]),
            (x_hbm.at[:, at], x_ref.at[:, at]),
        )

    coming = [begin(0), begin(1)]
    b_proj = bc_ref[:, :STATE]
    gb = gbin_ref[...]
    gc = gcin_ref[...]
    for g in range(PARTS):
        at = slice(g * span, (g + 1) * span)
        states = back_ref[g * held : (g + 1) * held, :rows, :].reshape(span, STATE)
        adjoint = back_ref[g * held : (g + 1) * held, rows:, :].reshape(span, STATE)
        cdot_ref[...] = mm(states, bct_ref[STATE:, :])
        bdot_ref[...] = mm(adjoint, bct_ref[:STATE, :])
        btok_ref[...] = mm(b_proj, adjoint, 1, 1)
        both = states.astype(F32) * adjoint.astype(F32)
        for i in range(2 * per):
            h = 2 * per * g + i
            product = both[i * HEAD_DIM : (i + 1) * HEAD_DIM]
            product_ref[h : h + 1, :] = jnp.sum(product, axis=0, keepdims=True)
        for copy in coming[g]:
            copy.wait()
        if g + 2 <= PARTS:
            coming.append(begin(g + 2))
        gb = gb + mm(adjoint, xwt_ref[at, :], 0, 0)
        gc = gc + mm(states, dywt_ref[at, :], 0, 0)

        def pair(p, carry, g=g):
            c = g * per + p
            c_dot = cdot_ref[lanes(p), :] * dywt_ref[lanes(c), :].astype(F32)
            b_dot = bdot_ref[lanes(p), :] * xwt_ref[lanes(c), :].astype(F32)
            for i in range(2):
                part = slice(i * HEAD_DIM, (i + 1) * HEAD_DIM)
                h = pl.ds(2 * c + i, 1)
                q_ref[h, :] = jnp.sum(c_dot[part], axis=0, keepdims=True)
                r_ref[h, :] = jnp.sum(b_dot[part], axis=0, keepdims=True)
            state_part = scale_ref[:, lanes(c)].astype(F32) * btok_ref[:, lanes(p)]
            finish(c, own_ref[:, lanes(c)] + state_part)
            return carry

        lax.fori_loop(0, per, pair, 0, unroll=True)
    for copy in coming[PARTS]:
        copy.wait()
    for i, total in enumerate((gb, gc)):
        grad_ref[...] = total
        finish(PAIRS + i, grad_ref[...].T * slope_ref[:, i * STATE : (i + 1) * STATE])

    four = end_ref[...] * jnp.sum(product_ref[...], axis=1, keepdims=True)
    four_ref[...] = four
    steps = step_ref[...]
    sofar = sofar_ref[...]
    every = sofar[:, GROUP - 1 :]
    own = row_ref[...] - colin_ref[...] - r_ref[...]
    met = steps * own - (every - sofar + steps) * own + sofar * q_ref[...]
    rates = -(jnp.sum(met, axis=1, keepdims=True) + four[:, :1] * every)
    skips = jnp.sum(skiprow_ref[...], axis=1, keepdims=True)
    flip_ref[...] = jnp.zeros_like(flip_ref)
    lane = lax.broadcasted_iota(jnp.int32, (HEADS, LANE), 1)
    flip_ref[:HEADS, :] = jnp.where(lane == 0, rates, 0.0) + jnp.where(lane == 1, skips, 0.0)
    tiles = PAIRS + 2
    for c in range(tiles):
        sums = sums_ref[c]
        for k in range(KCONV + 1):
            at = k * tiles + c
            params_ref[at : at + 1, :] = sums[k : k + 1]
    at = (KCONV + 1) * tiles
    params_ref[at : at + 2, :] = flip_ref[...].T[:2]


def spread_kernel(gpre_ref, next_ref, w_ref, gin_ref):
    rim = KCONV - 1

    def tile(c, carry):
        grad = gpre_ref[:, lanes(c)]
        below = jnp.concatenate([next_ref[:, lanes(c)], jnp.zeros((8 - rim, LANE), F32)], axis=0)
        full = jnp.concatenate([grad, below], axis=0)
        spread = w_ref[rim : rim + 1, lanes(c)] * grad
        for k in range(rim):
            spread = spread + w_ref[k : k + 1, lanes(c)] * full[rim - k : rim - k + GROUP]
        gin_ref[:, lanes(c)] = spread.astype(BF16)
        return carry

    lax.fori_loop(0, PAIRS + 2, tile, 0, unroll=2)


def log_kernel(q_ref, r_ref, four_ref, col_ref, row_ref, rate_ref, gsteps_ref):
    own = row_ref[...] - col_ref[...] - r_ref[...]
    running = mm(own, triangle(False), precision=HIGH)
    ending = mm(q_ref[...], triangle(True), precision=HIGH)
    grad_log = own - running + ending + four_ref[:, :1]
    gsteps_ref[...] = -head_column(rate_ref) * grad_log


def unpack_kernel(near_ref, far_ref, weight_ref, bias_ref, rates_ref, skip_ref, sum_ref):
    sum_ref[...] = near_ref[...] + far_ref[...]
    tiles = PAIRS + 2
    for c in range(tiles):
        at = slice(c * LANE, (c + 1) * LANE)
        for k in range(KCONV):
            weight_ref[k : k + 1, at] = sum_ref[k * tiles + c : k * tiles + c + 1, :]
        bias_ref[at] = sum_ref[KCONV * tiles + c, :]
    at = (KCONV + 1) * tiles
    rates_ref[...] = sum_ref[at, :HEADS]
    skip_ref[...] = sum_ref[at + 1, :HEADS]


def call(
    kernel, outs, scratch, *operands, large=0, scalars=0, kept=(), large_out=False, limit=VMEM_LIMIT
):
    small = len(operands) - large - scalars
    spaces = [pltpu.VMEM] * small + [pltpu.HBM] * large + [pltpu.SMEM] * scalars
    operands = [
        pltpu.with_memory_space_constraint(operand, pltpu.HBM)
        if space == pltpu.HBM
        else operand
        for operand, space in zip(operands, spaces)
    ]
    out_space = pltpu.HBM if large_out else pltpu.VMEM
    return pl.pallas_call(
        kernel,
        out_shape=[
            out_space(*out) if large_out or i in kept else jax.ShapeDtypeStruct(*out)
            for i, out in enumerate(outs)
        ],
        in_specs=[pl.BlockSpec(memory_space=space) for space in spaces],
        out_specs=[pl.BlockSpec(memory_space=out_space)] * len(outs),
        scratch_shapes=[pltpu.VMEM(*item) if isinstance(item, tuple) else item for item in scratch],
        compiler_params=pltpu.CompilerParams(vmem_limit_bytes=limit),
    )(*operands)


def shifted(array, axis, by):
    length = lax.axis_size(axis)
    pairs = [(i, i + by) for i in range(length) if 0 <= i + by < length]
    return lax.ppermute(array, axis, pairs)


def flipped(array, axis, bits):
    return lax.ppermute(array, axis, [(i, i ^ bits) for i in range(lax.axis_size(axis))])


def four_summed(array, axis, bit):
    near = flipped(array, axis, bit)
    far = flipped(array, axis, 2 * bit)
    both = flipped(array, axis, 3 * bit)
    return (array + near) + (far + both)


def shards(xbc_in, conv_weight, conv_bias, step_sizes, decay_rates, skip_gain, grad_out):
    channels = xbc_in.shape[2]
    rim = KCONV - 1
    chunks = lax.axis_size("seq")
    rows = X_WIDTH // chunks
    x_in = xbc_in[0]
    dy = grad_out[0]
    steps = step_sizes[0]
    wide_heads = ((HEADS, GROUP), F32)
    by_head = ((X_WIDTH, GROUP), BF16)
    dma = pltpu.SemaphoreType.DMA
    halo = shifted(x_in[GROUP - rim :], "seq", 1)
    dywt, tail, head = call(
        decay_kernel,
        [((X_WIDTH, GROUP), BF16), wide_heads, wide_heads],
        [wide_heads, pltpu.SMEM((HEADS,), F32), ((GROUP, X_WIDTH), BF16), dma((2,)), dma((PARTS,))],
        steps, decay_rates, dy, large=3, kept=(0,), limit=SMALL_LIMIT,
    )
    (msg,) = call(
        functools.partial(front_kernel, chunks=chunks, rows=rows),
        [((chunks, 2 * rows + TAIL_ROWS, LANE), BF16)],
        [
            ((GROUP, channels), BF16),
            ((KCONV, channels), F32),
            ((channels,), F32),
            ((chunks, 2 * rows + TAIL_ROWS, LANE), BF16),
            ((GROUP, 2 * STATE), BF16),
            ((X_WIDTH // PARTS, GROUP), BF16),
            dma((3,)),
            dma((PARTS,)),
            dma((PARTS,)),
        ],
        halo, dywt, tail, head, x_in, conv_weight, conv_bias,
        large=3, large_out=True, limit=SMALL_LIMIT,
    )
    got = lax.all_to_all(msg, "seq", 0, 0, tiled=True)
    (own, scale, xwt, dywt, bc, bct, slope, gb, gc, col_sums, row_sums, skip_rows, sofar, d_end) = call(
        within_kernel,
        [
            ((GROUP, X_WIDTH), F32),
            ((GROUP, X_WIDTH), BF16),
            by_head,
            by_head,
            ((GROUP, 2 * STATE), BF16),
            ((2 * STATE, GROUP), BF16),
            ((GROUP, 2 * STATE), F32),
            ((STATE, GROUP), F32),
            ((STATE, GROUP), F32),
            wide_heads,
            wide_heads,
            wide_heads,
            wide_heads,
            ((HEADS, LANE), F32),
        ],
        [
            ((HEADS, GROUP, LANE), F32),
            ((GROUP, GROUP), F32),
            ((GROUP, GROUP), F32),
            ((LANE, GROUP), F32),
            ((LANE, GROUP), F32),
            wide_heads,
            wide_heads,
            wide_heads,
        ],
        x_in, halo, conv_weight, conv_bias, dy, steps, decay_rates, skip_gain, scalars=2,
    )
    got, own = lax.optimization_barrier((got, own))
    (turned,) = call(
        functools.partial(chain_kernel, chunks=chunks, rows=rows),
        [((chunks, 2 * rows, LANE), BF16)],
        [((chunks, 2 * rows, LANE), BF16), dma((4,))],
        got, large_out=True, limit=SMALL_LIMIT,
    )
    back = lax.all_to_all(turned, "seq", 0, 0, tiled=True)
    gpre, edge, q_rows, r_rows, four, params = call(
        functools.partial(back_kernel, chunks=chunks, rows=rows),
        [
            ((GROUP, channels), F32),
            ((rim, channels), F32),
            wide_heads,
            wide_heads,
            ((HEADS, LANE), F32),
            (((KCONV + 1) * (PAIRS + 2) + 2, LANE), F32),
        ],
        [
            ((GROUP, X_WIDTH), F32),
            ((GROUP, X_WIDTH), BF16),
            by_head,
            by_head,
            ((GROUP, channels), BF16),
            ((X_WIDTH // PARTS, GROUP), F32),
            ((X_WIDTH // PARTS, GROUP), F32),
            ((GROUP, X_WIDTH // PARTS), F32),
            ((HEADS, LANE), F32),
            ((STATE, GROUP), F32),
            ((PAIRS + 2, 8, LANE), F32),
            ((LANE, LANE), F32),
            dma((PARTS + 1, 5)),
        ],
        back, bc, bct, slope, gb, gc, col_sums, row_sums, skip_rows,
        halo, steps, sofar, d_end,
        own, scale, xwt, dywt, x_in,
        large=5, limit=SMALL_LIMIT,
    )
    sums = params + flipped(params, "dp", 1)
    sums, q_rows = lax.optimization_barrier((sums, q_rows))
    (gsteps,) = call(
        log_kernel, [wide_heads], [], q_rows, r_rows, four, col_sums, row_sums, decay_rates,
        scalars=1, limit=SMALL_LIMIT,
    )
    sums = four_summed(sums, "dp", 2)
    sums, gsteps = lax.optimization_barrier((sums, gsteps))
    sums = four_summed(sums, "seq", 8)
    sums, edge = lax.optimization_barrier((sums, edge))
    next_rows = shifted(edge, "seq", -1)
    sums = four_summed(sums, "seq", 1)
    sums, gpre, next_rows = lax.optimization_barrier((sums, gpre, next_rows))
    far_sums = flipped(sums, "seq", 4)
    (grad_in,) = call(
        spread_kernel, [((GROUP, channels), BF16)], [], gpre, next_rows, conv_weight,
        limit=SMALL_LIMIT,
    )
    grad_weight, grad_bias, grad_rates, grad_skip = call(
        unpack_kernel,
        [((KCONV, channels), F32), ((channels,), F32), ((HEADS,), F32), ((HEADS,), F32)],
        [(params.shape, F32)],
        sums, far_sums, limit=SMALL_LIMIT,
    )
    return (grad_in[None], gsteps[None], grad_weight, grad_bias, grad_rates, grad_skip)


def solution(mesh):
    return jax.shard_map(
        shards,
        mesh=mesh,
        in_specs=(
            P("dp", "seq", None),
            P(),
            P(),
            P("dp", None, "seq"),
            P(),
            P(),
            P("dp", "seq", None),
        ),
        out_specs=(P("dp", "seq", None), P("dp", None, "seq"), P(), P(), P(), P()),
        check_vma=False,
    )
```

```python
import functools

import jax
import jax.numpy as jnp
from jax import lax
from jax.experimental import pallas as pl
from jax.experimental.pallas import tpu as pltpu
from jax.sharding import PartitionSpec as P

HEADS = 40
HEAD_DIM = 64
STATE = 128
GROUP = 256
KCONV = 4
LANE = 128
BF16 = jnp.bfloat16
F32 = jnp.float32
X_WIDTH = HEADS * HEAD_DIM
PAIRS = HEADS // 2
TAIL_ROWS = 8
VMEM_LIMIT = 56 * 1024 * 1024
SMALL_LIMIT = 24 * 1024 * 1024
PARTS = 4
HIGH = lax.Precision.HIGHEST


def mm(a, b, ca=1, cb=0, precision=None):
    return lax.dot_general(
        a, b, (((ca,), (cb,)), ((), ())), preferred_element_type=F32, precision=precision
    )


def lanes(c):
    return pl.ds(pl.multiple_of(c * LANE, LANE), LANE)


def taps_of(x_ref, halo_ref, c):
    full = jnp.concatenate(
        [
            jnp.zeros((8 - (KCONV - 1), LANE), F32),
            halo_ref[:, lanes(c)].astype(F32),
            x_ref[:, lanes(c)].astype(F32),
        ],
        axis=0,
    )
    return [full[5 + k : 5 + k + GROUP] for k in range(KCONV)]


def triangle(lower):
    row = lax.broadcasted_iota(jnp.int32, (GROUP, GROUP), 0)
    col = lax.broadcasted_iota(jnp.int32, (GROUP, GROUP), 1)
    return jnp.where(row >= col if lower else row <= col, 1.0, 0.0).astype(F32)


def head_column(scalar_ref):
    head = lax.broadcasted_iota(jnp.int32, (HEADS, GROUP), 0)
    found = jnp.zeros((HEADS, GROUP), F32)
    for h in range(HEADS):
        found = jnp.where(head == h, scalar_ref[h], found)
    return found


def pre_act_of(taps, w_ref, bias_ref, c):
    pre = bias_ref[lanes(c)].reshape(1, LANE)
    for k in range(KCONV):
        pre = pre + w_ref[k : k + 1, lanes(c)] * taps[k]
    return pre


def pair_rows(ref, c):
    return jnp.concatenate(
        [jnp.broadcast_to(ref[pl.ds(2 * c + i, 1), :], (HEAD_DIM, GROUP)) for i in range(2)], axis=0
    )


def started(sem, *pairs):
    made = [pltpu.make_async_copy(a, b, sem.at[i]) for i, (a, b) in enumerate(pairs)]
    for copy in made:
        copy.start()
    return made


def logs_of(step_ref, rate_ref):
    return mm(-(step_ref[...] * head_column(rate_ref)), triangle(False), precision=HIGH)


def decay_kernel(
    step_hbm, rate_hbm, dy_hbm,
    dywt_ref, tail_ref, head_ref,
    step_ref, rate_ref, dy_ref, few_sem, dy_sem,
):
    span = X_WIDTH // PARTS
    few = started(few_sem, (step_hbm, step_ref), (rate_hbm, rate_ref))
    cuts = [slice(g * span, (g + 1) * span) for g in range(PARTS)]
    many = started(dy_sem, *[(dy_hbm.at[:, cut], dy_ref.at[:, cut]) for cut in cuts])
    for copy in few:
        copy.wait()
    cum = logs_of(step_ref, rate_ref)
    tail_ref[...] = jnp.exp(cum[:, GROUP - 1 :] - cum)
    head_ref[...] = jnp.exp(cum)

    def turn(c, carry):
        head = pair_rows(head_ref, c)
        dywt_ref[lanes(c), :] = (dy_ref[:, lanes(c)].T.astype(F32) * head).astype(BF16)
        return carry

    per = PAIRS // PARTS
    for g in range(PARTS):
        many[g].wait()
        lax.fori_loop(g * per, (g + 1) * per, turn, 0, unroll=True)


def front_kernel(
    halo_ref, dywt_ref, tail_ref, head_ref,
    x_hbm, w_hbm, bias_hbm,
    msg_hbm,
    x_ref, w_ref, bias_ref, msg_ref, bc_ref, xwt_ref, few_sem, x_sem, msg_sem,
    *, chunks, rows,
):
    per = PAIRS // PARTS
    span = per * LANE
    held = chunks // PARTS
    few = started(
        few_sem, (w_hbm, w_ref), (bias_hbm, bias_ref), (x_hbm.at[:, X_WIDTH:], x_ref.at[:, X_WIDTH:])
    )
    cuts = [slice(g * span, (g + 1) * span) for g in range(PARTS)]
    many = started(x_sem, *[(x_hbm.at[:, cut], x_ref.at[:, cut]) for cut in cuts])

    d_end = jnp.broadcast_to(head_ref[:, GROUP - 1 :], (HEADS, LANE))
    part_a = d_end.astype(BF16).astype(F32)
    part_b = (d_end - part_a).astype(BF16).astype(F32)
    part_c = (d_end - part_a - part_b).astype(BF16).astype(F32)
    blank = jnp.zeros((TAIL_ROWS - 6, LANE), F32)
    for j in range(chunks):
        first = rows * j // HEAD_DIM
        last = (rows * j + rows - 1) // HEAD_DIM
        picked = [p[h : h + 1] for h in (first, last) for p in (part_a, part_b, part_c)]
        msg_ref[j, 2 * rows :, :] = jnp.concatenate(picked + [blank], axis=0).astype(BF16)

    def active(c):
        pre = pre_act_of(taps_of(x_ref, halo_ref, c), w_ref, bias_ref, c)
        return (pre * jax.nn.sigmoid(pre)).astype(BF16)

    for copy in few:
        copy.wait()
    bc_ref[:, :STATE] = active(PAIRS)
    bc_ref[:, STATE:] = active(PAIRS + 1)
    sent = []
    for g in range(PARTS):
        many[g].wait()

        def conv(p, carry, g=g):
            c = g * per + p
            tail = pair_rows(tail_ref, c)
            xwt_ref[lanes(p), :] = (active(c).T.astype(F32) * tail).astype(BF16)
            return carry

        lax.fori_loop(0, per, conv, 0, unroll=True)
        s_local = mm(xwt_ref[...], bc_ref[:, :STATE]).astype(BF16)
        u_local = mm(dywt_ref[cuts[g], :], bc_ref[:, STATE:]).astype(BF16)
        for i in range(held):
            at = slice(i * rows, (i + 1) * rows)
            msg_ref[g * held + i, :rows, :] = s_local[at]
            msg_ref[g * held + i, rows : 2 * rows, :] = u_local[at]
        block = slice(g * held, (g + 1) * held)
        sent.append(pltpu.make_async_copy(msg_ref.at[block], msg_hbm.at[block], msg_sem.at[g]))
        sent[-1].start()
    for copy in sent:
        copy.wait()


def within_kernel(
    x_ref, halo_ref, w_ref, bias_ref, dy_ref, step_ref, rate_ref, skip_ref,
    own_ref, scale_ref, xwt_ref, dywt_ref, bc_ref, bct_ref, slope_ref,
    gb_ref, gc_ref, col_ref, row_ref, skiprow_ref, sofar_ref, end_ref,
    column_ref, wsum_ref, cb_ref, hold_ref, base_ref, cum_ref, tail_ref, head_ref,
):
    cum = logs_of(step_ref, rate_ref)
    cum_ref[...] = cum
    tail_ref[...] = jnp.exp(cum[:, GROUP - 1 :] - cum)
    head_ref[...] = jnp.exp(cum)
    end_ref[...] = jnp.broadcast_to(jnp.exp(cum[:, GROUP - 1 :]), (HEADS, LANE))
    sofar_ref[...] = mm(step_ref[...], triangle(False), precision=HIGH)

    def conv(c):
        pre = pre_act_of(taps_of(x_ref, halo_ref, c), w_ref, bias_ref, c)
        sig = jax.nn.sigmoid(pre)
        return (pre * sig).astype(BF16), sig * (1.0 + pre * (1.0 - sig))

    for i in range(2):
        at = slice(i * STATE, (i + 1) * STATE)
        z, slope_ref[:, at] = conv(PAIRS + i)
        bc_ref[:, at] = z
        bct_ref[at, :] = z.T
    hold_ref[...] = jnp.zeros_like(hold_ref)
    hold_ref[:HEADS, :] = cum_ref[...]
    turned = hold_ref[...].T
    for h in range(HEADS):
        column_ref[h] = jnp.broadcast_to(turned[:, h : h + 1], (GROUP, LANE))
    wsum_ref[...] = jnp.zeros_like(wsum_ref)
    cb_ref[...] = mm(bc_ref[:, STATE:], bct_ref[:STATE, :])
    t_index = lax.broadcasted_iota(jnp.int32, (GROUP, GROUP), 0)
    s_index = lax.broadcasted_iota(jnp.int32, (GROUP, GROUP), 1)
    causal = t_index >= s_index

    def pair(c, carry):
        z, slope = conv(c)
        xt_pair = z.T
        dy_pair = dy_ref[:, lanes(c)]
        dyt_pair = dy_pair.T
        tail = pair_rows(tail_ref, c)
        head = pair_rows(head_ref, c)
        xwt_ref[lanes(c), :] = (xt_pair.astype(F32) * tail).astype(BF16)
        dywt_ref[lanes(c), :] = (dyt_pair.astype(F32) * head).astype(BF16)
        scale_ref[:, lanes(c)] = (tail.T * slope).astype(BF16)
        zero = jnp.zeros((HEAD_DIM, GROUP), BF16)
        total = wsum_ref[...]
        for i in range(2):
            h = 2 * c + i
            at = pl.ds(h, 1)
            part = slice(i * HEAD_DIM, (i + 1) * HEAD_DIM)
            xt = xt_pair[part]
            dyt = dyt_pair[part]
            wide = jnp.concatenate([xt, zero] if i == 0 else [zero, xt], axis=0)
            inner = mm(dy_pair, wide)
            column = column_ref[h]
            column = jnp.concatenate([column, column], axis=1)
            gap = column - cum_ref[at, :]
            decay = jnp.exp(jnp.where(causal, gap, -jnp.inf))
            total = total + decay * inner
            kt = (decay * cb_ref[...]).astype(BF16)
            intra = mm(dyt, kt)
            forth = mm(xt, kt, 1, 1)
            xf = xt.astype(F32)
            dyf = dyt.astype(F32)
            base_ref[part, :] = intra + skip_ref[h] * dyf
            col_ref[at, :] = jnp.sum(intra * xf, axis=0, keepdims=True)
            row_ref[at, :] = jnp.sum(forth * dyf, axis=0, keepdims=True)
            skiprow_ref[at, :] = jnp.sum(xf * dyf, axis=0, keepdims=True)
        wsum_ref[...] = total
        own_ref[:, lanes(c)] = base_ref[...].T * slope
        return carry

    lax.fori_loop(0, PAIRS, pair, 0)
    w_summed = wsum_ref[...].astype(BF16)
    gb_ref[...] = mm(bct_ref[STATE:, :], w_summed)
    gc_ref[...] = mm(bct_ref[:STATE, :], w_summed, 1, 1)


def chain_kernel(got_ref, out_hbm, out_ref, sem, *, chunks, rows):
    j = lax.axis_index("seq")
    split = HEAD_DIM - lax.rem(rows * j, HEAD_DIM)
    ahead = lax.broadcasted_iota(jnp.int32, (rows, LANE), 0) < split

    def decay_of(i):
        ends = got_ref[i, 2 * rows :, :].astype(F32)
        one = ends[0:1] + ends[1:2] + ends[2:3]
        two = ends[3:4] + ends[4:5] + ends[5:6]
        return jnp.where(ahead, one, two)

    def step(k, carry):
        state, adjoint = carry
        out_ref[k, :rows, :] = state.astype(BF16)
        state = decay_of(k) * state + got_ref[k, :rows, :].astype(F32)
        m = chunks - 1 - k
        out_ref[m, rows:, :] = adjoint.astype(BF16)
        adjoint = decay_of(m) * adjoint + got_ref[m, rows : 2 * rows, :].astype(F32)
        return state, adjoint

    carry = (jnp.zeros((rows, LANE), F32), jnp.zeros((rows, LANE), F32))
    half = chunks // 2
    sent = []
    for g in range(2):
        carry = lax.fori_loop(g * half, (g + 1) * half, step, carry, unroll=4)
        fore = (slice(g * half, (g + 1) * half), slice(0, rows))
        rear = (slice((1 - g) * half, (2 - g) * half), slice(rows, 2 * rows))
        for i, at in enumerate((fore, rear)):
            sent.append(pltpu.make_async_copy(out_ref.at[at], out_hbm.at[at], sem.at[2 * g + i]))
            sent[-1].start()
    for copy in sent:
        copy.wait()


def back_kernel(
    back_ref, bc_ref, bct_ref, slope_ref,
    gbin_ref, gcin_ref, colin_ref, row_ref, skiprow_ref,
    halo_ref, step_ref, sofar_ref, end_ref,
    own_hbm, scale_hbm, xwt_hbm, dywt_hbm, x_hbm,
    gpre_ref, edge_ref, q_ref, r_ref, four_ref, params_ref,
    own_ref, scale_ref, xwt_ref, dywt_ref, x_ref,
    cdot_ref, bdot_ref, btok_ref, product_ref, grad_ref, sums_ref, flip_ref, part_sem,
    *, chunks, rows,
):
    rim = KCONV - 1
    per = PAIRS // PARTS
    span = per * LANE
    held = chunks // PARTS

    def finish(c, grad):
        edge_ref[:, lanes(c)] = grad[:rim]
        gpre_ref[:, lanes(c)] = grad
        x = x_ref[:, lanes(c)].astype(F32)
        halo = halo_ref[:, lanes(c)].astype(F32)
        full = jnp.concatenate([grad, jnp.zeros((8, LANE), F32)], axis=0)
        found = []
        for k in range(rim):
            moved = full[rim - k : rim - k + GROUP]
            entering = jnp.sum(grad[: rim - k] * halo[k:], axis=0, keepdims=True)
            found.append(jnp.sum(moved * x, axis=0, keepdims=True) + entering)
        found.append(jnp.sum(grad * x, axis=0, keepdims=True))
        found.append(jnp.sum(grad, axis=0, keepdims=True))
        found.append(jnp.zeros((8 - len(found), LANE), F32))
        sums_ref[c] = jnp.concatenate(found, axis=0)

    def begin(g):
        if g == PARTS:
            return started(part_sem.at[g], (x_hbm.at[:, X_WIDTH:], x_ref.at[:, X_WIDTH:]))
        at = slice(g * span, (g + 1) * span)
        return started(
            part_sem.at[g],
            (xwt_hbm.at[at], xwt_ref.at[at]),
            (dywt_hbm.at[at], dywt_ref.at[at]),
            (own_hbm.at[:, at], own_ref.at[:, at]),
            (scale_hbm.at[:, at], scale_ref.at[:, at]),
            (x_hbm.at[:, at], x_ref.at[:, at]),
        )

    coming = [begin(0), begin(1)]
    b_proj = bc_ref[:, :STATE]
    gb = gbin_ref[...]
    gc = gcin_ref[...]
    for g in range(PARTS):
        at = slice(g * span, (g + 1) * span)
        states = back_ref[g * held : (g + 1) * held, :rows, :].reshape(span, STATE)
        adjoint = back_ref[g * held : (g + 1) * held, rows:, :].reshape(span, STATE)
        cdot_ref[...] = mm(states, bct_ref[STATE:, :])
        bdot_ref[...] = mm(adjoint, bct_ref[:STATE, :])
        btok_ref[...] = mm(b_proj, adjoint, 1, 1)
        both = states.astype(F32) * adjoint.astype(F32)
        for i in range(2 * per):
            h = 2 * per * g + i
            product = both[i * HEAD_DIM : (i + 1) * HEAD_DIM]
            product_ref[h : h + 1, :] = jnp.sum(product, axis=0, keepdims=True)
        for copy in coming[g]:
            copy.wait()
        if g + 2 <= PARTS:
            coming.append(begin(g + 2))
        gb = gb + mm(adjoint, xwt_ref[at, :], 0, 0)
        gc = gc + mm(states, dywt_ref[at, :], 0, 0)

        def pair(p, carry, g=g):
            c = g * per + p
            c_dot = cdot_ref[lanes(p), :] * dywt_ref[lanes(c), :].astype(F32)
            b_dot = bdot_ref[lanes(p), :] * xwt_ref[lanes(c), :].astype(F32)
            for i in range(2):
                part = slice(i * HEAD_DIM, (i + 1) * HEAD_DIM)
                h = pl.ds(2 * c + i, 1)
                q_ref[h, :] = jnp.sum(c_dot[part], axis=0, keepdims=True)
                r_ref[h, :] = jnp.sum(b_dot[part], axis=0, keepdims=True)
            state_part = scale_ref[:, lanes(c)].astype(F32) * btok_ref[:, lanes(p)]
            finish(c, own_ref[:, lanes(c)] + state_part)
            return carry

        lax.fori_loop(0, per, pair, 0, unroll=True)
    for copy in coming[PARTS]:
        copy.wait()
    for i, total in enumerate((gb, gc)):
        grad_ref[...] = total
        finish(PAIRS + i, grad_ref[...].T * slope_ref[:, i * STATE : (i + 1) * STATE])

    four = end_ref[...] * jnp.sum(product_ref[...], axis=1, keepdims=True)
    four_ref[...] = four
    steps = step_ref[...]
    sofar = sofar_ref[...]
    every = sofar[:, GROUP - 1 :]
    own = row_ref[...] - colin_ref[...] - r_ref[...]
    met = steps * own - (every - sofar + steps) * own + sofar * q_ref[...]
    rates = -(jnp.sum(met, axis=1, keepdims=True) + four[:, :1] * every)
    skips = jnp.sum(skiprow_ref[...], axis=1, keepdims=True)
    flip_ref[...] = jnp.zeros_like(flip_ref)
    lane = lax.broadcasted_iota(jnp.int32, (HEADS, LANE), 1)
    flip_ref[:HEADS, :] = jnp.where(lane == 0, rates, 0.0) + jnp.where(lane == 1, skips, 0.0)
    tiles = PAIRS + 2
    for c in range(tiles):
        sums = sums_ref[c]
        for k in range(KCONV + 1):
            at = k * tiles + c
            params_ref[at : at + 1, :] = sums[k : k + 1]
    at = (KCONV + 1) * tiles
    params_ref[at : at + 2, :] = flip_ref[...].T[:2]


def spread_kernel(gpre_ref, w_ref, gin_ref, last_ref):
    rim = KCONV - 1

    def tile(c, carry):
        grad = gpre_ref[:, lanes(c)]
        full = jnp.concatenate([grad, jnp.zeros((8, LANE), F32)], axis=0)
        spread = w_ref[rim : rim + 1, lanes(c)] * grad
        for k in range(rim):
            spread = spread + w_ref[k : k + 1, lanes(c)] * full[rim - k : rim - k + GROUP]
        gin_ref[:, lanes(c)] = spread.astype(BF16)
        last_ref[:, lanes(c)] = spread[GROUP - 16 :]
        return carry

    lax.fori_loop(0, PAIRS + 2, tile, 0, unroll=2)


def log_kernel(q_ref, r_ref, four_ref, col_ref, row_ref, rate_ref, gsteps_ref):
    own = row_ref[...] - col_ref[...] - r_ref[...]
    running = mm(own, triangle(False), precision=HIGH)
    ending = mm(q_ref[...], triangle(True), precision=HIGH)
    grad_log = own - running + ending + four_ref[:, :1]
    gsteps_ref[...] = -head_column(rate_ref) * grad_log


def unpack_kernel(near_ref, far_ref, weight_ref, bias_ref, rates_ref, skip_ref, sum_ref):
    sum_ref[...] = near_ref[...] + far_ref[...]
    tiles = PAIRS + 2
    for c in range(tiles):
        at = slice(c * LANE, (c + 1) * LANE)
        for k in range(KCONV):
            weight_ref[k : k + 1, at] = sum_ref[k * tiles + c : k * tiles + c + 1, :]
        bias_ref[at] = sum_ref[KCONV * tiles + c, :]
    at = (KCONV + 1) * tiles
    rates_ref[...] = sum_ref[at, :HEADS]
    skip_ref[...] = sum_ref[at + 1, :HEADS]


def call(
    kernel, outs, scratch, *operands, large=0, scalars=0, kept=(), large_out=False, limit=VMEM_LIMIT
):
    small = len(operands) - large - scalars
    spaces = [pltpu.VMEM] * small + [pltpu.HBM] * large + [pltpu.SMEM] * scalars
    operands = [
        pltpu.with_memory_space_constraint(operand, pltpu.HBM)
        if space == pltpu.HBM
        else operand
        for operand, space in zip(operands, spaces)
    ]
    out_space = pltpu.HBM if large_out else pltpu.VMEM
    return pl.pallas_call(
        kernel,
        out_shape=[
            out_space(*out) if large_out or i in kept else jax.ShapeDtypeStruct(*out)
            for i, out in enumerate(outs)
        ],
        in_specs=[pl.BlockSpec(memory_space=space) for space in spaces],
        out_specs=[pl.BlockSpec(memory_space=out_space)] * len(outs),
        scratch_shapes=[pltpu.VMEM(*item) if isinstance(item, tuple) else item for item in scratch],
        compiler_params=pltpu.CompilerParams(vmem_limit_bytes=limit),
    )(*operands)


def shifted(array, axis, by):
    length = lax.axis_size(axis)
    pairs = [(i, i + by) for i in range(length) if 0 <= i + by < length]
    return lax.ppermute(array, axis, pairs)


def flipped(array, axis, bits):
    return lax.ppermute(array, axis, [(i, i ^ bits) for i in range(lax.axis_size(axis))])


def four_summed(array, axis, bit):
    near = flipped(array, axis, bit)
    far = flipped(array, axis, 2 * bit)
    both = flipped(array, axis, 3 * bit)
    return (array + near) + (far + both)


def shards(xbc_in, conv_weight, conv_bias, step_sizes, decay_rates, skip_gain, grad_out):
    channels = xbc_in.shape[2]
    rim = KCONV - 1
    chunks = lax.axis_size("seq")
    rows = X_WIDTH // chunks
    x_in = xbc_in[0]
    dy = grad_out[0]
    steps = step_sizes[0]
    wide_heads = ((HEADS, GROUP), F32)
    by_head = ((X_WIDTH, GROUP), BF16)
    dma = pltpu.SemaphoreType.DMA
    halo = shifted(x_in[GROUP - rim :], "seq", 1)
    dywt, tail, head = call(
        decay_kernel,
        [((X_WIDTH, GROUP), BF16), wide_heads, wide_heads],
        [wide_heads, pltpu.SMEM((HEADS,), F32), ((GROUP, X_WIDTH), BF16), dma((2,)), dma((PARTS,))],
        steps, decay_rates, dy, large=3, kept=(0,), limit=SMALL_LIMIT,
    )
    (msg,) = call(
        functools.partial(front_kernel, chunks=chunks, rows=rows),
        [((chunks, 2 * rows + TAIL_ROWS, LANE), BF16)],
        [
            ((GROUP, channels), BF16),
            ((KCONV, channels), F32),
            ((channels,), F32),
            ((chunks, 2 * rows + TAIL_ROWS, LANE), BF16),
            ((GROUP, 2 * STATE), BF16),
            ((X_WIDTH // PARTS, GROUP), BF16),
            dma((3,)),
            dma((PARTS,)),
            dma((PARTS,)),
        ],
        halo, dywt, tail, head, x_in, conv_weight, conv_bias,
        large=3, large_out=True, limit=SMALL_LIMIT,
    )
    got = lax.all_to_all(msg, "seq", 0, 0, tiled=True)
    (own, scale, xwt, dywt, bc, bct, slope, gb, gc, col_sums, row_sums, skip_rows, sofar, d_end) = call(
        within_kernel,
        [
            ((GROUP, X_WIDTH), F32),
            ((GROUP, X_WIDTH), BF16),
            by_head,
            by_head,
            ((GROUP, 2 * STATE), BF16),
            ((2 * STATE, GROUP), BF16),
            ((GROUP, 2 * STATE), F32),
            ((STATE, GROUP), F32),
            ((STATE, GROUP), F32),
            wide_heads,
            wide_heads,
            wide_heads,
            wide_heads,
            ((HEADS, LANE), F32),
        ],
        [
            ((HEADS, GROUP, LANE), F32),
            ((GROUP, GROUP), F32),
            ((GROUP, GROUP), F32),
            ((LANE, GROUP), F32),
            ((LANE, GROUP), F32),
            wide_heads,
            wide_heads,
            wide_heads,
        ],
        x_in, halo, conv_weight, conv_bias, dy, steps, decay_rates, skip_gain, scalars=2,
    )
    got, own = lax.optimization_barrier((got, own))
    (turned,) = call(
        functools.partial(chain_kernel, chunks=chunks, rows=rows),
        [((chunks, 2 * rows, LANE), BF16)],
        [((chunks, 2 * rows, LANE), BF16), dma((4,))],
        got, large_out=True, limit=SMALL_LIMIT,
    )
    back = lax.all_to_all(turned, "seq", 0, 0, tiled=True)
    gpre, edge, q_rows, r_rows, four, params = call(
        functools.partial(back_kernel, chunks=chunks, rows=rows),
        [
            ((GROUP, channels), F32),
            ((rim, channels), F32),
            wide_heads,
            wide_heads,
            ((HEADS, LANE), F32),
            (((KCONV + 1) * (PAIRS + 2) + 2, LANE), F32),
        ],
        [
            ((GROUP, X_WIDTH), F32),
            ((GROUP, X_WIDTH), BF16),
            by_head,
            by_head,
            ((GROUP, channels), BF16),
            ((X_WIDTH // PARTS, GROUP), F32),
            ((X_WIDTH // PARTS, GROUP), F32),
            ((GROUP, X_WIDTH // PARTS), F32),
            ((HEADS, LANE), F32),
            ((STATE, GROUP), F32),
            ((PAIRS + 2, 8, LANE), F32),
            ((LANE, LANE), F32),
            dma((PARTS + 1, 5)),
        ],
        back, bc, bct, slope, gb, gc, col_sums, row_sums, skip_rows,
        halo, steps, sofar, d_end,
        own, scale, xwt, dywt, x_in,
        large=5, limit=SMALL_LIMIT,
    )
    sums = params + flipped(params, "dp", 1)
    sums, q_rows = lax.optimization_barrier((sums, q_rows))
    (gsteps,) = call(
        log_kernel, [wide_heads], [], q_rows, r_rows, four, col_sums, row_sums, decay_rates,
        scalars=1, limit=SMALL_LIMIT,
    )
    sums = four_summed(sums, "dp", 2)
    sums, gsteps, gpre = lax.optimization_barrier((sums, gsteps, gpre))
    grad_in, last = call(
        spread_kernel, [((GROUP, channels), BF16), ((16, channels), F32)], [], gpre, conv_weight,
        limit=SMALL_LIMIT,
    )
    sums = four_summed(sums, "seq", 8)
    sums, edge, grad_in = lax.optimization_barrier((sums, edge, grad_in))
    next_rows = shifted(edge, "seq", -1)
    sums = four_summed(sums, "seq", 1)
    sums, last = lax.optimization_barrier((sums, last))
    far_sums = flipped(sums, "seq", 4)
    ahead = jnp.concatenate([jnp.zeros_like(next_rows), next_rows], axis=0)
    added = last[16 - rim :]
    for k in range(rim):
        added = added + conv_weight[k][None] * ahead[rim - k : 2 * rim - k]
    ending = jnp.concatenate([last[: 16 - rim], added], axis=0).astype(BF16)
    grad_in = lax.dynamic_update_slice(grad_in, ending, (GROUP - 16, 0))
    grad_weight, grad_bias, grad_rates, grad_skip = call(
        unpack_kernel,
        [((KCONV, channels), F32), ((channels,), F32), ((HEADS,), F32), ((HEADS,), F32)],
        [(params.shape, F32)],
        sums, far_sums, limit=SMALL_LIMIT,
    )
    return (grad_in[None], gsteps[None], grad_weight, grad_bias, grad_rates, grad_skip)


def solution(mesh):
    return jax.shard_map(
        shards,
        mesh=mesh,
        in_specs=(
            P("dp", "seq", None),
            P(),
            P(),
            P("dp", None, "seq"),
            P(),
            P(),
            P("dp", "seq", None),
        ),
        out_specs=(P("dp", "seq", None), P("dp", None, "seq"), P(), P(), P(), P()),
        check_vma=False,
    )
```

```python
import functools

import jax
import jax.numpy as jnp
from jax import lax
from jax.experimental import pallas as pl
from jax.experimental.pallas import tpu as pltpu
from jax.sharding import PartitionSpec as P

HEADS = 40
HEAD_DIM = 64
STATE = 128
GROUP = 256
KCONV = 4
LANE = 128
BF16 = jnp.bfloat16
F32 = jnp.float32
X_WIDTH = HEADS * HEAD_DIM
PAIRS = HEADS // 2
TAIL_ROWS = 8
VMEM_LIMIT = 56 * 1024 * 1024
SMALL_LIMIT = 24 * 1024 * 1024
PARTS = 4
HIGH = lax.Precision.HIGHEST


def mm(a, b, ca=1, cb=0, precision=None):
    return lax.dot_general(
        a, b, (((ca,), (cb,)), ((), ())), preferred_element_type=F32, precision=precision
    )


def lanes(c):
    return pl.ds(pl.multiple_of(c * LANE, LANE), LANE)


def taps_of(x_ref, halo_ref, c):
    full = jnp.concatenate(
        [
            jnp.zeros((8 - (KCONV - 1), LANE), F32),
            halo_ref[:, lanes(c)].astype(F32),
            x_ref[:, lanes(c)].astype(F32),
        ],
        axis=0,
    )
    return [full[5 + k : 5 + k + GROUP] for k in range(KCONV)]


def triangle(lower):
    row = lax.broadcasted_iota(jnp.int32, (GROUP, GROUP), 0)
    col = lax.broadcasted_iota(jnp.int32, (GROUP, GROUP), 1)
    return jnp.where(row >= col if lower else row <= col, 1.0, 0.0).astype(F32)


def head_column(scalar_ref):
    head = lax.broadcasted_iota(jnp.int32, (HEADS, GROUP), 0)
    found = jnp.zeros((HEADS, GROUP), F32)
    for h in range(HEADS):
        found = jnp.where(head == h, scalar_ref[h], found)
    return found


def pre_act_of(taps, w_ref, bias_ref, c):
    pre = bias_ref[lanes(c)].reshape(1, LANE)
    for k in range(KCONV):
        pre = pre + w_ref[k : k + 1, lanes(c)] * taps[k]
    return pre


def pair_rows(ref, c):
    return jnp.concatenate(
        [jnp.broadcast_to(ref[pl.ds(2 * c + i, 1), :], (HEAD_DIM, GROUP)) for i in range(2)], axis=0
    )


def started(sem, *pairs):
    made = [pltpu.make_async_copy(a, b, sem.at[i]) for i, (a, b) in enumerate(pairs)]
    for copy in made:
        copy.start()
    return made


def logs_of(step_ref, rate_ref):
    return mm(-(step_ref[...] * head_column(rate_ref)), triangle(False), precision=HIGH)


def decay_kernel(
    step_hbm, rate_hbm, dy_hbm, x_hbm, w_hbm, bias_hbm,
    dywt_ref, x_ref, w_ref, bias_ref, tail_ref, head_ref,
    step_ref, rate_ref, dy_ref, few_sem, dy_sem, next_sem,
):
    span = X_WIDTH // PARTS
    few = started(few_sem, (step_hbm, step_ref), (rate_hbm, rate_ref))
    cuts = [slice(g * span, (g + 1) * span) for g in range(PARTS)]
    many = started(dy_sem, *[(dy_hbm.at[:, cut], dy_ref.at[:, cut]) for cut in cuts])
    ahead = started(next_sem, (x_hbm, x_ref), (w_hbm, w_ref), (bias_hbm, bias_ref))
    for copy in few:
        copy.wait()
    cum = logs_of(step_ref, rate_ref)
    tail_ref[...] = jnp.exp(cum[:, GROUP - 1 :] - cum)
    head_ref[...] = jnp.exp(cum)

    def turn(c, carry):
        head = pair_rows(head_ref, c)
        dywt_ref[lanes(c), :] = (dy_ref[:, lanes(c)].T.astype(F32) * head).astype(BF16)
        return carry

    per = PAIRS // PARTS
    for g in range(PARTS):
        many[g].wait()
        lax.fori_loop(g * per, (g + 1) * per, turn, 0, unroll=True)
    for copy in ahead:
        copy.wait()


def front_kernel(
    halo_ref, dywt_ref, tail_ref, head_ref, x_ref, w_ref, bias_ref,
    msg_hbm,
    msg_ref, bc_ref, xwt_ref, msg_sem,
    *, chunks, rows,
):
    per = PAIRS // PARTS
    span = per * LANE
    held = chunks // PARTS
    cuts = [slice(g * span, (g + 1) * span) for g in range(PARTS)]

    d_end = jnp.broadcast_to(head_ref[:, GROUP - 1 :], (HEADS, LANE))
    part_a = d_end.astype(BF16).astype(F32)
    part_b = (d_end - part_a).astype(BF16).astype(F32)
    part_c = (d_end - part_a - part_b).astype(BF16).astype(F32)
    blank = jnp.zeros((TAIL_ROWS - 6, LANE), F32)
    for j in range(chunks):
        first = rows * j // HEAD_DIM
        last = (rows * j + rows - 1) // HEAD_DIM
        picked = [p[h : h + 1] for h in (first, last) for p in (part_a, part_b, part_c)]
        msg_ref[j, 2 * rows :, :] = jnp.concatenate(picked + [blank], axis=0).astype(BF16)

    def active(c):
        pre = pre_act_of(taps_of(x_ref, halo_ref, c), w_ref, bias_ref, c)
        return (pre * jax.nn.sigmoid(pre)).astype(BF16)

    bc_ref[:, :STATE] = active(PAIRS)
    bc_ref[:, STATE:] = active(PAIRS + 1)
    sent = []
    for g in range(PARTS):

        def conv(p, carry, g=g):
            c = g * per + p
            tail = pair_rows(tail_ref, c)
            xwt_ref[lanes(p), :] = (active(c).T.astype(F32) * tail).astype(BF16)
            return carry

        lax.fori_loop(0, per, conv, 0, unroll=True)
        s_local = mm(xwt_ref[...], bc_ref[:, :STATE]).astype(BF16)
        u_local = mm(dywt_ref[cuts[g], :], bc_ref[:, STATE:]).astype(BF16)
        for i in range(held):
            at = slice(i * rows, (i + 1) * rows)
            msg_ref[g * held + i, :rows, :] = s_local[at]
            msg_ref[g * held + i, rows : 2 * rows, :] = u_local[at]
        block = slice(g * held, (g + 1) * held)
        sent.append(pltpu.make_async_copy(msg_ref.at[block], msg_hbm.at[block], msg_sem.at[g]))
        sent[-1].start()
    for copy in sent:
        copy.wait()


def within_kernel(
    x_ref, halo_ref, w_ref, bias_ref, dy_ref, step_ref, rate_ref, skip_ref,
    own_ref, scale_ref, xwt_ref, dywt_ref, bc_ref, bct_ref, slope_ref,
    gb_ref, gc_ref, col_ref, row_ref, skiprow_ref, sofar_ref, end_ref,
    column_ref, wsum_ref, cb_ref, hold_ref, base_ref, cum_ref, tail_ref, head_ref,
):
    cum = logs_of(step_ref, rate_ref)
    cum_ref[...] = cum
    tail_ref[...] = jnp.exp(cum[:, GROUP - 1 :] - cum)
    head_ref[...] = jnp.exp(cum)
    end_ref[...] = jnp.broadcast_to(jnp.exp(cum[:, GROUP - 1 :]), (HEADS, LANE))
    sofar_ref[...] = mm(step_ref[...], triangle(False), precision=HIGH)

    def conv(c):
        pre = pre_act_of(taps_of(x_ref, halo_ref, c), w_ref, bias_ref, c)
        sig = jax.nn.sigmoid(pre)
        return (pre * sig).astype(BF16), sig * (1.0 + pre * (1.0 - sig))

    for i in range(2):
        at = slice(i * STATE, (i + 1) * STATE)
        z, slope_ref[:, at] = conv(PAIRS + i)
        bc_ref[:, at] = z
        bct_ref[at, :] = z.T
    hold_ref[...] = jnp.zeros_like(hold_ref)
    hold_ref[:HEADS, :] = cum_ref[...]
    turned = hold_ref[...].T
    for h in range(HEADS):
        column_ref[h] = jnp.broadcast_to(turned[:, h : h + 1], (GROUP, LANE))
    wsum_ref[...] = jnp.zeros_like(wsum_ref)
    cb_ref[...] = mm(bc_ref[:, STATE:], bct_ref[:STATE, :])
    t_index = lax.broadcasted_iota(jnp.int32, (GROUP, GROUP), 0)
    s_index = lax.broadcasted_iota(jnp.int32, (GROUP, GROUP), 1)
    causal = t_index >= s_index

    def pair(c, carry):
        z, slope = conv(c)
        xt_pair = z.T
        dy_pair = dy_ref[:, lanes(c)]
        dyt_pair = dy_pair.T
        tail = pair_rows(tail_ref, c)
        head = pair_rows(head_ref, c)
        xwt_ref[lanes(c), :] = (xt_pair.astype(F32) * tail).astype(BF16)
        dywt_ref[lanes(c), :] = (dyt_pair.astype(F32) * head).astype(BF16)
        scale_ref[:, lanes(c)] = (tail.T * slope).astype(BF16)
        zero = jnp.zeros((HEAD_DIM, GROUP), BF16)
        total = wsum_ref[...]
        for i in range(2):
            h = 2 * c + i
            at = pl.ds(h, 1)
            part = slice(i * HEAD_DIM, (i + 1) * HEAD_DIM)
            xt = xt_pair[part]
            dyt = dyt_pair[part]
            wide = jnp.concatenate([xt, zero] if i == 0 else [zero, xt], axis=0)
            inner = mm(dy_pair, wide)
            column = column_ref[h]
            column = jnp.concatenate([column, column], axis=1)
            gap = column - cum_ref[at, :]
            decay = jnp.exp(jnp.where(causal, gap, -jnp.inf))
            total = total + decay * inner
            kt = (decay * cb_ref[...]).astype(BF16)
            intra = mm(dyt, kt)
            forth = mm(xt, kt, 1, 1)
            xf = xt.astype(F32)
            dyf = dyt.astype(F32)
            base_ref[part, :] = intra + skip_ref[h] * dyf
            col_ref[at, :] = jnp.sum(intra * xf, axis=0, keepdims=True)
            row_ref[at, :] = jnp.sum(forth * dyf, axis=0, keepdims=True)
            skiprow_ref[at, :] = jnp.sum(xf * dyf, axis=0, keepdims=True)
        wsum_ref[...] = total
        own_ref[:, lanes(c)] = base_ref[...].T * slope
        return carry

    lax.fori_loop(0, PAIRS, pair, 0)
    w_summed = wsum_ref[...].astype(BF16)
    gb_ref[...] = mm(bct_ref[STATE:, :], w_summed)
    gc_ref[...] = mm(bct_ref[:STATE, :], w_summed, 1, 1)


def chain_kernel(got_ref, out_hbm, out_ref, sem, *, chunks, rows):
    j = lax.axis_index("seq")
    split = HEAD_DIM - lax.rem(rows * j, HEAD_DIM)
    ahead = lax.broadcasted_iota(jnp.int32, (rows, LANE), 0) < split

    def decay_of(i):
        ends = got_ref[i, 2 * rows :, :].astype(F32)
        one = ends[0:1] + ends[1:2] + ends[2:3]
        two = ends[3:4] + ends[4:5] + ends[5:6]
        return jnp.where(ahead, one, two)

    def step(k, carry):
        state, adjoint = carry
        out_ref[k, :rows, :] = state.astype(BF16)
        state = decay_of(k) * state + got_ref[k, :rows, :].astype(F32)
        m = chunks - 1 - k
        out_ref[m, rows:, :] = adjoint.astype(BF16)
        adjoint = decay_of(m) * adjoint + got_ref[m, rows : 2 * rows, :].astype(F32)
        return state, adjoint

    carry = (jnp.zeros((rows, LANE), F32), jnp.zeros((rows, LANE), F32))
    half = chunks // 2
    sent = []
    for g in range(2):
        carry = lax.fori_loop(g * half, (g + 1) * half, step, carry, unroll=4)
        fore = (slice(g * half, (g + 1) * half), slice(0, rows))
        rear = (slice((1 - g) * half, (2 - g) * half), slice(rows, 2 * rows))
        for i, at in enumerate((fore, rear)):
            sent.append(pltpu.make_async_copy(out_ref.at[at], out_hbm.at[at], sem.at[2 * g + i]))
            sent[-1].start()
    for copy in sent:
        copy.wait()


def back_kernel(
    back_ref, bc_ref, bct_ref, slope_ref,
    gbin_ref, gcin_ref, colin_ref, row_ref, skiprow_ref,
    halo_ref, step_ref, sofar_ref, end_ref,
    own_hbm, scale_hbm, xwt_hbm, dywt_hbm, x_hbm,
    gpre_ref, edge_ref, q_ref, r_ref, four_ref, params_ref,
    own_ref, scale_ref, xwt_ref, dywt_ref, x_ref,
    cdot_ref, bdot_ref, btok_ref, product_ref, grad_ref, sums_ref, flip_ref, part_sem,
    *, chunks, rows,
):
    rim = KCONV - 1
    per = PAIRS // PARTS
    span = per * LANE
    held = chunks // PARTS

    def finish(c, grad):
        edge_ref[:, lanes(c)] = grad[:rim]
        gpre_ref[:, lanes(c)] = grad
        x = x_ref[:, lanes(c)].astype(F32)
        halo = halo_ref[:, lanes(c)].astype(F32)
        full = jnp.concatenate([grad, jnp.zeros((8, LANE), F32)], axis=0)
        found = []
        for k in range(rim):
            moved = full[rim - k : rim - k + GROUP]
            entering = jnp.sum(grad[: rim - k] * halo[k:], axis=0, keepdims=True)
            found.append(jnp.sum(moved * x, axis=0, keepdims=True) + entering)
        found.append(jnp.sum(grad * x, axis=0, keepdims=True))
        found.append(jnp.sum(grad, axis=0, keepdims=True))
        found.append(jnp.zeros((8 - len(found), LANE), F32))
        sums_ref[c] = jnp.concatenate(found, axis=0)

    def begin(g):
        if g == PARTS:
            return started(part_sem.at[g], (x_hbm.at[:, X_WIDTH:], x_ref.at[:, X_WIDTH:]))
        at = slice(g * span, (g + 1) * span)
        return started(
            part_sem.at[g],
            (xwt_hbm.at[at], xwt_ref.at[at]),
            (dywt_hbm.at[at], dywt_ref.at[at]),
            (own_hbm.at[:, at], own_ref.at[:, at]),
            (scale_hbm.at[:, at], scale_ref.at[:, at]),
            (x_hbm.at[:, at], x_ref.at[:, at]),
        )

    coming = [begin(0), begin(1)]
    b_proj = bc_ref[:, :STATE]
    gb = gbin_ref[...]
    gc = gcin_ref[...]
    for g in range(PARTS):
        at = slice(g * span, (g + 1) * span)
        states = back_ref[g * held : (g + 1) * held, :rows, :].reshape(span, STATE)
        adjoint = back_ref[g * held : (g + 1) * held, rows:, :].reshape(span, STATE)
        cdot_ref[...] = mm(states, bct_ref[STATE:, :])
        bdot_ref[...] = mm(adjoint, bct_ref[:STATE, :])
        btok_ref[...] = mm(b_proj, adjoint, 1, 1)
        both = states.astype(F32) * adjoint.astype(F32)
        for i in range(2 * per):
            h = 2 * per * g + i
            product = both[i * HEAD_DIM : (i + 1) * HEAD_DIM]
            product_ref[h : h + 1, :] = jnp.sum(product, axis=0, keepdims=True)
        for copy in coming[g]:
            copy.wait()
        if g + 2 <= PARTS:
            coming.append(begin(g + 2))
        gb = gb + mm(adjoint, xwt_ref[at, :], 0, 0)
        gc = gc + mm(states, dywt_ref[at, :], 0, 0)

        def pair(p, carry, g=g):
            c = g * per + p
            c_dot = cdot_ref[lanes(p), :] * dywt_ref[lanes(c), :].astype(F32)
            b_dot = bdot_ref[lanes(p), :] * xwt_ref[lanes(c), :].astype(F32)
            for i in range(2):
                part = slice(i * HEAD_DIM, (i + 1) * HEAD_DIM)
                h = pl.ds(2 * c + i, 1)
                q_ref[h, :] = jnp.sum(c_dot[part], axis=0, keepdims=True)
                r_ref[h, :] = jnp.sum(b_dot[part], axis=0, keepdims=True)
            state_part = scale_ref[:, lanes(c)].astype(F32) * btok_ref[:, lanes(p)]
            finish(c, own_ref[:, lanes(c)] + state_part)
            return carry

        lax.fori_loop(0, per, pair, 0, unroll=True)
    for copy in coming[PARTS]:
        copy.wait()
    for i, total in enumerate((gb, gc)):
        grad_ref[...] = total
        finish(PAIRS + i, grad_ref[...].T * slope_ref[:, i * STATE : (i + 1) * STATE])

    four = end_ref[...] * jnp.sum(product_ref[...], axis=1, keepdims=True)
    four_ref[...] = four
    steps = step_ref[...]
    sofar = sofar_ref[...]
    every = sofar[:, GROUP - 1 :]
    own = row_ref[...] - colin_ref[...] - r_ref[...]
    met = steps * own - (every - sofar + steps) * own + sofar * q_ref[...]
    rates = -(jnp.sum(met, axis=1, keepdims=True) + four[:, :1] * every)
    skips = jnp.sum(skiprow_ref[...], axis=1, keepdims=True)
    flip_ref[...] = jnp.zeros_like(flip_ref)
    lane = lax.broadcasted_iota(jnp.int32, (HEADS, LANE), 1)
    flip_ref[:HEADS, :] = jnp.where(lane == 0, rates, 0.0) + jnp.where(lane == 1, skips, 0.0)
    tiles = PAIRS + 2
    for c in range(tiles):
        sums = sums_ref[c]
        for k in range(KCONV + 1):
            at = k * tiles + c
            params_ref[at : at + 1, :] = sums[k : k + 1]
    at = (KCONV + 1) * tiles
    params_ref[at : at + 2, :] = flip_ref[...].T[:2]


def spread_kernel(gpre_ref, w_ref, gin_ref, last_ref):
    rim = KCONV - 1

    def tile(c, carry):
        grad = gpre_ref[:, lanes(c)]
        full = jnp.concatenate([grad, jnp.zeros((8, LANE), F32)], axis=0)
        spread = w_ref[rim : rim + 1, lanes(c)] * grad
        for k in range(rim):
            spread = spread + w_ref[k : k + 1, lanes(c)] * full[rim - k : rim - k + GROUP]
        gin_ref[:, lanes(c)] = spread.astype(BF16)
        last_ref[:, lanes(c)] = spread[GROUP - 16 :]
        return carry

    lax.fori_loop(0, PAIRS + 2, tile, 0, unroll=2)


def log_kernel(q_ref, r_ref, four_ref, col_ref, row_ref, rate_ref, gsteps_ref):
    own = row_ref[...] - col_ref[...] - r_ref[...]
    running = mm(own, triangle(False), precision=HIGH)
    ending = mm(q_ref[...], triangle(True), precision=HIGH)
    grad_log = own - running + ending + four_ref[:, :1]
    gsteps_ref[...] = -head_column(rate_ref) * grad_log


def unpack_kernel(near_ref, far_ref, weight_ref, bias_ref, rates_ref, skip_ref, sum_ref):
    sum_ref[...] = near_ref[...] + far_ref[...]
    tiles = PAIRS + 2
    for c in range(tiles):
        at = slice(c * LANE, (c + 1) * LANE)
        for k in range(KCONV):
            weight_ref[k : k + 1, at] = sum_ref[k * tiles + c : k * tiles + c + 1, :]
        bias_ref[at] = sum_ref[KCONV * tiles + c, :]
    at = (KCONV + 1) * tiles
    rates_ref[...] = sum_ref[at, :HEADS]
    skip_ref[...] = sum_ref[at + 1, :HEADS]


def call(
    kernel, outs, scratch, *operands, large=0, scalars=0, kept=(), large_out=False, limit=VMEM_LIMIT
):
    small = len(operands) - large - scalars
    spaces = [pltpu.VMEM] * small + [pltpu.HBM] * large + [pltpu.SMEM] * scalars
    operands = [
        pltpu.with_memory_space_constraint(operand, pltpu.HBM)
        if space == pltpu.HBM
        else operand
        for operand, space in zip(operands, spaces)
    ]
    out_space = pltpu.HBM if large_out else pltpu.VMEM
    return pl.pallas_call(
        kernel,
        out_shape=[
            out_space(*out) if large_out or i in kept else jax.ShapeDtypeStruct(*out)
            for i, out in enumerate(outs)
        ],
        in_specs=[pl.BlockSpec(memory_space=space) for space in spaces],
        out_specs=[pl.BlockSpec(memory_space=out_space)] * len(outs),
        scratch_shapes=[pltpu.VMEM(*item) if isinstance(item, tuple) else item for item in scratch],
        compiler_params=pltpu.CompilerParams(vmem_limit_bytes=limit),
    )(*operands)


def shifted(array, axis, by):
    length = lax.axis_size(axis)
    pairs = [(i, i + by) for i in range(length) if 0 <= i + by < length]
    return lax.ppermute(array, axis, pairs)


def flipped(array, axis, bits):
    return lax.ppermute(array, axis, [(i, i ^ bits) for i in range(lax.axis_size(axis))])


def four_summed(array, axis, bit):
    near = flipped(array, axis, bit)
    far = flipped(array, axis, 2 * bit)
    both = flipped(array, axis, 3 * bit)
    return (array + near) + (far + both)


def shards(xbc_in, conv_weight, conv_bias, step_sizes, decay_rates, skip_gain, grad_out):
    channels = xbc_in.shape[2]
    rim = KCONV - 1
    chunks = lax.axis_size("seq")
    rows = X_WIDTH // chunks
    x_in = xbc_in[0]
    dy = grad_out[0]
    steps = step_sizes[0]
    wide_heads = ((HEADS, GROUP), F32)
    by_head = ((X_WIDTH, GROUP), BF16)
    dma = pltpu.SemaphoreType.DMA
    halo = shifted(x_in[GROUP - rim :], "seq", 1)
    dywt, x_near, w_near, bias_near, tail, head = call(
        decay_kernel,
        [
            by_head,
            ((GROUP, channels), BF16),
            ((KCONV, channels), F32),
            ((channels,), F32),
            wide_heads,
            wide_heads,
        ],
        [
            wide_heads,
            pltpu.SMEM((HEADS,), F32),
            ((GROUP, X_WIDTH), BF16),
            dma((2,)),
            dma((PARTS,)),
            dma((3,)),
        ],
        steps, decay_rates, dy, x_in, conv_weight, conv_bias,
        large=6, kept=range(4), limit=SMALL_LIMIT,
    )
    (msg,) = call(
        functools.partial(front_kernel, chunks=chunks, rows=rows),
        [((chunks, 2 * rows + TAIL_ROWS, LANE), BF16)],
        [
            ((chunks, 2 * rows + TAIL_ROWS, LANE), BF16),
            ((GROUP, 2 * STATE), BF16),
            ((X_WIDTH // PARTS, GROUP), BF16),
            dma((PARTS,)),
        ],
        halo, dywt, tail, head, x_near, w_near, bias_near, large_out=True, limit=SMALL_LIMIT,
    )
    got = lax.all_to_all(msg, "seq", 0, 0, tiled=True)
    (own, scale, xwt, dywt, bc, bct, slope, gb, gc, col_sums, row_sums, skip_rows, sofar, d_end) = call(
        within_kernel,
        [
            ((GROUP, X_WIDTH), F32),
            ((GROUP, X_WIDTH), BF16),
            by_head,
            by_head,
            ((GROUP, 2 * STATE), BF16),
            ((2 * STATE, GROUP), BF16),
            ((GROUP, 2 * STATE), F32),
            ((STATE, GROUP), F32),
            ((STATE, GROUP), F32),
            wide_heads,
            wide_heads,
            wide_heads,
            wide_heads,
            ((HEADS, LANE), F32),
        ],
        [
            ((HEADS, GROUP, LANE), F32),
            ((GROUP, GROUP), F32),
            ((GROUP, GROUP), F32),
            ((LANE, GROUP), F32),
            ((LANE, GROUP), F32),
            wide_heads,
            wide_heads,
            wide_heads,
        ],
        x_in, halo, conv_weight, conv_bias, dy, steps, decay_rates, skip_gain, scalars=2,
    )
    got, own = lax.optimization_barrier((got, own))
    (turned,) = call(
        functools.partial(chain_kernel, chunks=chunks, rows=rows),
        [((chunks, 2 * rows, LANE), BF16)],
        [((chunks, 2 * rows, LANE), BF16), dma((4,))],
        got, large_out=True, limit=SMALL_LIMIT,
    )
    back = lax.all_to_all(turned, "seq", 0, 0, tiled=True)
    gpre, edge, q_rows, r_rows, four, params = call(
        functools.partial(back_kernel, chunks=chunks, rows=rows),
        [
            ((GROUP, channels), F32),
            ((rim, channels), F32),
            wide_heads,
            wide_heads,
            ((HEADS, LANE), F32),
            (((KCONV + 1) * (PAIRS + 2) + 2, LANE), F32),
        ],
        [
            ((GROUP, X_WIDTH), F32),
            ((GROUP, X_WIDTH), BF16),
            by_head,
            by_head,
            ((GROUP, channels), BF16),
            ((X_WIDTH // PARTS, GROUP), F32),
            ((X_WIDTH // PARTS, GROUP), F32),
            ((GROUP, X_WIDTH // PARTS), F32),
            ((HEADS, LANE), F32),
            ((STATE, GROUP), F32),
            ((PAIRS + 2, 8, LANE), F32),
            ((LANE, LANE), F32),
            dma((PARTS + 1, 5)),
        ],
        back, bc, bct, slope, gb, gc, col_sums, row_sums, skip_rows,
        halo, steps, sofar, d_end,
        own, scale, xwt, dywt, x_in,
        large=5, limit=SMALL_LIMIT,
    )
    sums = params + flipped(params, "dp", 1)
    sums, q_rows = lax.optimization_barrier((sums, q_rows))
    (gsteps,) = call(
        log_kernel, [wide_heads], [], q_rows, r_rows, four, col_sums, row_sums, decay_rates,
        scalars=1, limit=SMALL_LIMIT,
    )
    sums = four_summed(sums, "dp", 2)
    sums, gsteps, gpre = lax.optimization_barrier((sums, gsteps, gpre))
    grad_in, last = call(
        spread_kernel, [((GROUP, channels), BF16), ((16, channels), F32)], [], gpre, conv_weight,
        limit=SMALL_LIMIT,
    )
    sums = four_summed(sums, "seq", 8)
    sums, edge, grad_in = lax.optimization_barrier((sums, edge, grad_in))
    next_rows = shifted(edge, "seq", -1)
    sums = four_summed(sums, "seq", 1)
    sums, last = lax.optimization_barrier((sums, last))
    far_sums = flipped(sums, "seq", 4)
    ahead = jnp.concatenate([jnp.zeros_like(next_rows), next_rows], axis=0)
    added = last[16 - rim :]
    for k in range(rim):
        added = added + conv_weight[k][None] * ahead[rim - k : 2 * rim - k]
    ending = jnp.concatenate([last[: 16 - rim], added], axis=0).astype(BF16)
    grad_in = lax.dynamic_update_slice(grad_in, ending, (GROUP - 16, 0))
    grad_weight, grad_bias, grad_rates, grad_skip = call(
        unpack_kernel,
        [((KCONV, channels), F32), ((channels,), F32), ((HEADS,), F32), ((HEADS,), F32)],
        [(params.shape, F32)],
        sums, far_sums, limit=SMALL_LIMIT,
    )
    return (grad_in[None], gsteps[None], grad_weight, grad_bias, grad_rates, grad_skip)


def solution(mesh):
    return jax.shard_map(
        shards,
        mesh=mesh,
        in_specs=(
            P("dp", "seq", None),
            P(),
            P(),
            P("dp", None, "seq"),
            P(),
            P(),
            P("dp", "seq", None),
        ),
        out_specs=(P("dp", "seq", None), P("dp", None, "seq"), P(), P(), P(), P()),
        check_vma=False,
    )
```

```python
import functools

import jax
import jax.numpy as jnp
from jax import lax
from jax.experimental import pallas as pl
from jax.experimental.pallas import tpu as pltpu
from jax.sharding import PartitionSpec as P

HEADS = 40
HEAD_DIM = 64
STATE = 128
GROUP = 256
KCONV = 4
LANE = 128
BF16 = jnp.bfloat16
F32 = jnp.float32
X_WIDTH = HEADS * HEAD_DIM
PAIRS = HEADS // 2
TAIL_ROWS = 8
VMEM_LIMIT = 56 * 1024 * 1024
SMALL_LIMIT = 24 * 1024 * 1024
PARTS = 4
HIGH = lax.Precision.HIGHEST


def mm(a, b, ca=1, cb=0, precision=None):
    return lax.dot_general(
        a, b, (((ca,), (cb,)), ((), ())), preferred_element_type=F32, precision=precision
    )


def lanes(c):
    return pl.ds(pl.multiple_of(c * LANE, LANE), LANE)


def taps_of(x_ref, halo_ref, c):
    full = jnp.concatenate(
        [
            jnp.zeros((8 - (KCONV - 1), LANE), F32),
            halo_ref[:, lanes(c)].astype(F32),
            x_ref[:, lanes(c)].astype(F32),
        ],
        axis=0,
    )
    return [full[5 + k : 5 + k + GROUP] for k in range(KCONV)]


def triangle(lower):
    row = lax.broadcasted_iota(jnp.int32, (GROUP, GROUP), 0)
    col = lax.broadcasted_iota(jnp.int32, (GROUP, GROUP), 1)
    return jnp.where(row >= col if lower else row <= col, 1.0, 0.0).astype(F32)


def head_column(scalar_ref):
    head = lax.broadcasted_iota(jnp.int32, (HEADS, GROUP), 0)
    found = jnp.zeros((HEADS, GROUP), F32)
    for h in range(HEADS):
        found = jnp.where(head == h, scalar_ref[h], found)
    return found


def pre_act_of(taps, w_ref, bias_ref, c):
    pre = bias_ref[lanes(c)].reshape(1, LANE)
    for k in range(KCONV):
        pre = pre + w_ref[k : k + 1, lanes(c)] * taps[k]
    return pre


def pair_rows(ref, c):
    return jnp.concatenate(
        [jnp.broadcast_to(ref[pl.ds(2 * c + i, 1), :], (HEAD_DIM, GROUP)) for i in range(2)], axis=0
    )


def started(sem, *pairs):
    made = [pltpu.make_async_copy(a, b, sem.at[i]) for i, (a, b) in enumerate(pairs)]
    for copy in made:
        copy.start()
    return made


def logs_of(step_ref, rate_ref):
    return mm(-(step_ref[...] * head_column(rate_ref)), triangle(False), precision=HIGH)


def decay_kernel(
    step_hbm, rate_hbm, dy_hbm, x_hbm, w_hbm, bias_hbm,
    dywt_ref, x_ref, w_ref, bias_ref, tail_ref, head_ref,
    step_ref, rate_ref, dy_ref, few_sem, dy_sem, next_sem,
):
    span = X_WIDTH // PARTS
    few = started(few_sem, (step_hbm, step_ref), (rate_hbm, rate_ref))
    cuts = [slice(g * span, (g + 1) * span) for g in range(PARTS)]
    many = started(dy_sem, *[(dy_hbm.at[:, cut], dy_ref.at[:, cut]) for cut in cuts])
    ahead = started(next_sem, (x_hbm, x_ref), (w_hbm, w_ref), (bias_hbm, bias_ref))
    for copy in few:
        copy.wait()
    cum = logs_of(step_ref, rate_ref)
    tail_ref[...] = jnp.exp(cum[:, GROUP - 1 :] - cum)
    head_ref[...] = jnp.exp(cum)

    def turn(c, carry):
        head = pair_rows(head_ref, c)
        dywt_ref[lanes(c), :] = (dy_ref[:, lanes(c)].T.astype(F32) * head).astype(BF16)
        return carry

    per = PAIRS // PARTS
    for g in range(PARTS):
        many[g].wait()
        lax.fori_loop(g * per, (g + 1) * per, turn, 0, unroll=True)
    for copy in ahead:
        copy.wait()


def front_kernel(
    halo_ref, dywt_ref, tail_ref, head_ref, x_ref, w_ref, bias_ref,
    msg_hbm,
    msg_ref, bc_ref, xwt_ref, msg_sem,
    *, chunks, rows,
):
    per = PAIRS // PARTS
    span = per * LANE
    held = chunks // PARTS
    cuts = [slice(g * span, (g + 1) * span) for g in range(PARTS)]

    d_end = jnp.broadcast_to(head_ref[:, GROUP - 1 :], (HEADS, LANE))
    part_a = d_end.astype(BF16).astype(F32)
    part_b = (d_end - part_a).astype(BF16).astype(F32)
    part_c = (d_end - part_a - part_b).astype(BF16).astype(F32)
    blank = jnp.zeros((TAIL_ROWS - 6, LANE), F32)
    for j in range(chunks):
        first = rows * j // HEAD_DIM
        last = (rows * j + rows - 1) // HEAD_DIM
        picked = [p[h : h + 1] for h in (first, last) for p in (part_a, part_b, part_c)]
        msg_ref[j, 2 * rows :, :] = jnp.concatenate(picked + [blank], axis=0).astype(BF16)

    def active(c):
        pre = pre_act_of(taps_of(x_ref, halo_ref, c), w_ref, bias_ref, c)
        return (pre * jax.nn.sigmoid(pre)).astype(BF16)

    bc_ref[:, :STATE] = active(PAIRS)
    bc_ref[:, STATE:] = active(PAIRS + 1)
    sent = []
    for g in range(PARTS):

        def conv(p, carry, g=g):
            c = g * per + p
            tail = pair_rows(tail_ref, c)
            xwt_ref[lanes(p), :] = (active(c).T.astype(F32) * tail).astype(BF16)
            return carry

        lax.fori_loop(0, per, conv, 0, unroll=True)
        s_local = mm(xwt_ref[...], bc_ref[:, :STATE]).astype(BF16)
        u_local = mm(dywt_ref[cuts[g], :], bc_ref[:, STATE:]).astype(BF16)
        for i in range(held):
            at = slice(i * rows, (i + 1) * rows)
            msg_ref[g * held + i, :rows, :] = s_local[at]
            msg_ref[g * held + i, rows : 2 * rows, :] = u_local[at]
        block = slice(g * held, (g + 1) * held)
        sent.append(pltpu.make_async_copy(msg_ref.at[block], msg_hbm.at[block], msg_sem.at[g]))
        sent[-1].start()
    for copy in sent:
        copy.wait()


def within_kernel(
    x_ref, halo_ref, w_ref, bias_ref, dy_ref, step_ref, rate_ref, skip_ref,
    own_ref, scale_ref, xwt_ref, dywt_ref, bc_ref, bct_ref, slope_ref,
    gb_ref, gc_ref, col_ref, row_ref, skiprow_ref, sofar_ref, end_ref,
    column_ref, wsum_ref, cb_ref, hold_ref, base_ref, cum_ref, tail_ref, head_ref,
):
    cum = logs_of(step_ref, rate_ref)
    cum_ref[...] = cum
    tail_ref[...] = jnp.exp(cum[:, GROUP - 1 :] - cum)
    head_ref[...] = jnp.exp(cum)
    end_ref[...] = jnp.broadcast_to(jnp.exp(cum[:, GROUP - 1 :]), (HEADS, LANE))
    sofar_ref[...] = mm(step_ref[...], triangle(False), precision=HIGH)

    def conv(c):
        pre = pre_act_of(taps_of(x_ref, halo_ref, c), w_ref, bias_ref, c)
        sig = jax.nn.sigmoid(pre)
        return (pre * sig).astype(BF16), sig * (1.0 + pre * (1.0 - sig))

    for i in range(2):
        at = slice(i * STATE, (i + 1) * STATE)
        z, slope_ref[:, at] = conv(PAIRS + i)
        bc_ref[:, at] = z
        bct_ref[at, :] = z.T
    hold_ref[...] = jnp.zeros_like(hold_ref)
    hold_ref[:HEADS, :] = cum_ref[...]
    turned = hold_ref[...].T
    for h in range(HEADS):
        column_ref[h] = jnp.broadcast_to(turned[:, h : h + 1], (GROUP, LANE))
    wsum_ref[...] = jnp.zeros_like(wsum_ref)
    cb_ref[...] = mm(bc_ref[:, STATE:], bct_ref[:STATE, :])
    t_index = lax.broadcasted_iota(jnp.int32, (GROUP, GROUP), 0)
    s_index = lax.broadcasted_iota(jnp.int32, (GROUP, GROUP), 1)
    causal = t_index >= s_index

    def pair(c, carry):
        z, slope = conv(c)
        xt_pair = z.T
        dy_pair = dy_ref[:, lanes(c)]
        dyt_pair = dy_pair.T
        tail = pair_rows(tail_ref, c)
        head = pair_rows(head_ref, c)
        xwt_ref[lanes(c), :] = (xt_pair.astype(F32) * tail).astype(BF16)
        dywt_ref[lanes(c), :] = (dyt_pair.astype(F32) * head).astype(BF16)
        scale_ref[:, lanes(c)] = (tail.T * slope).astype(BF16)
        zero = jnp.zeros((HEAD_DIM, GROUP), BF16)
        total = wsum_ref[...]
        for i in range(2):
            h = 2 * c + i
            at = pl.ds(h, 1)
            part = slice(i * HEAD_DIM, (i + 1) * HEAD_DIM)
            xt = xt_pair[part]
            dyt = dyt_pair[part]
            wide = jnp.concatenate([xt, zero] if i == 0 else [zero, xt], axis=0)
            inner = mm(dy_pair, wide)
            column = column_ref[h]
            column = jnp.concatenate([column, column], axis=1)
            gap = column - cum_ref[at, :]
            decay = jnp.exp(jnp.where(causal, gap, -jnp.inf))
            total = total + decay * inner
            kt = (decay * cb_ref[...]).astype(BF16)
            intra = mm(dyt, kt)
            forth = mm(xt, kt, 1, 1)
            xf = xt.astype(F32)
            dyf = dyt.astype(F32)
            base_ref[part, :] = intra + skip_ref[h] * dyf
            col_ref[at, :] = jnp.sum(intra * xf, axis=0, keepdims=True)
            row_ref[at, :] = jnp.sum(forth * dyf, axis=0, keepdims=True)
            skiprow_ref[at, :] = jnp.sum(xf * dyf, axis=0, keepdims=True)
        wsum_ref[...] = total
        own_ref[:, lanes(c)] = base_ref[...].T * slope
        return carry

    lax.fori_loop(0, PAIRS, pair, 0)
    w_summed = wsum_ref[...].astype(BF16)
    gb_ref[...] = mm(bct_ref[STATE:, :], w_summed)
    gc_ref[...] = mm(bct_ref[:STATE, :], w_summed, 1, 1)


def chain_kernel(got_ref, out_hbm, out_ref, sem, *, chunks, rows):
    j = lax.axis_index("seq")
    split = HEAD_DIM - lax.rem(rows * j, HEAD_DIM)
    ahead = lax.broadcasted_iota(jnp.int32, (rows, LANE), 0) < split

    def decay_of(i):
        ends = got_ref[i, 2 * rows :, :].astype(F32)
        one = ends[0:1] + ends[1:2] + ends[2:3]
        two = ends[3:4] + ends[4:5] + ends[5:6]
        return jnp.where(ahead, one, two)

    def step(k, carry):
        state, adjoint = carry
        out_ref[k, :rows, :] = state.astype(BF16)
        state = decay_of(k) * state + got_ref[k, :rows, :].astype(F32)
        m = chunks - 1 - k
        out_ref[m, rows:, :] = adjoint.astype(BF16)
        adjoint = decay_of(m) * adjoint + got_ref[m, rows : 2 * rows, :].astype(F32)
        return state, adjoint

    carry = (jnp.zeros((rows, LANE), F32), jnp.zeros((rows, LANE), F32))
    half = chunks // 2
    sent = []
    for g in range(2):
        carry = lax.fori_loop(g * half, (g + 1) * half, step, carry, unroll=4)
        fore = (slice(g * half, (g + 1) * half), slice(0, rows))
        rear = (slice((1 - g) * half, (2 - g) * half), slice(rows, 2 * rows))
        for i, at in enumerate((fore, rear)):
            sent.append(pltpu.make_async_copy(out_ref.at[at], out_hbm.at[at], sem.at[2 * g + i]))
            sent[-1].start()
    for copy in sent:
        copy.wait()


def back_kernel(
    back_ref, bc_ref, bct_ref, slope_ref,
    gbin_ref, gcin_ref, colin_ref, row_ref, skiprow_ref,
    halo_ref, step_ref, sofar_ref, end_ref,
    own_hbm, scale_hbm, xwt_hbm, dywt_hbm, x_hbm,
    gpre_ref, edge_ref, q_ref, r_ref, four_ref, params_ref,
    own_ref, scale_ref, xwt_ref, dywt_ref, x_ref,
    cdot_ref, bdot_ref, btok_ref, product_ref, grad_ref, sums_ref, flip_ref, part_sem,
    *, chunks, rows,
):
    rim = KCONV - 1
    per = PAIRS // PARTS
    span = per * LANE
    held = chunks // PARTS

    def finish(c, grad):
        edge_ref[:, lanes(c)] = grad[:rim]
        gpre_ref[:, lanes(c)] = grad
        x = x_ref[:, lanes(c)].astype(F32)
        halo = halo_ref[:, lanes(c)].astype(F32)
        full = jnp.concatenate([grad, jnp.zeros((8, LANE), F32)], axis=0)
        found = []
        for k in range(rim):
            moved = full[rim - k : rim - k + GROUP]
            entering = jnp.sum(grad[: rim - k] * halo[k:], axis=0, keepdims=True)
            found.append(jnp.sum(moved * x, axis=0, keepdims=True) + entering)
        found.append(jnp.sum(grad * x, axis=0, keepdims=True))
        found.append(jnp.sum(grad, axis=0, keepdims=True))
        found.append(jnp.zeros((8 - len(found), LANE), F32))
        sums_ref[c] = jnp.concatenate(found, axis=0)

    def begin(g):
        if g == PARTS:
            return started(part_sem.at[g], (x_hbm.at[:, X_WIDTH:], x_ref.at[:, X_WIDTH:]))
        at = slice(g * span, (g + 1) * span)
        return started(
            part_sem.at[g],
            (xwt_hbm.at[at], xwt_ref.at[at]),
            (dywt_hbm.at[at], dywt_ref.at[at]),
            (own_hbm.at[:, at], own_ref.at[:, at]),
            (scale_hbm.at[:, at], scale_ref.at[:, at]),
            (x_hbm.at[:, at], x_ref.at[:, at]),
        )

    coming = [begin(0), begin(1)]
    b_proj = bc_ref[:, :STATE]
    gb = gbin_ref[...]
    gc = gcin_ref[...]
    for g in range(PARTS):
        at = slice(g * span, (g + 1) * span)
        states = back_ref[g * held : (g + 1) * held, :rows, :].reshape(span, STATE)
        adjoint = back_ref[g * held : (g + 1) * held, rows:, :].reshape(span, STATE)
        cdot_ref[...] = mm(states, bct_ref[STATE:, :])
        bdot_ref[...] = mm(adjoint, bct_ref[:STATE, :])
        btok_ref[...] = mm(b_proj, adjoint, 1, 1)
        both = states.astype(F32) * adjoint.astype(F32)
        for i in range(2 * per):
            h = 2 * per * g + i
            product = both[i * HEAD_DIM : (i + 1) * HEAD_DIM]
            product_ref[h : h + 1, :] = jnp.sum(product, axis=0, keepdims=True)
        for copy in coming[g]:
            copy.wait()
        if g + 2 <= PARTS:
            coming.append(begin(g + 2))
        gb = gb + mm(adjoint, xwt_ref[at, :], 0, 0)
        gc = gc + mm(states, dywt_ref[at, :], 0, 0)

        def pair(p, carry, g=g):
            c = g * per + p
            c_dot = cdot_ref[lanes(p), :] * dywt_ref[lanes(c), :].astype(F32)
            b_dot = bdot_ref[lanes(p), :] * xwt_ref[lanes(c), :].astype(F32)
            for i in range(2):
                part = slice(i * HEAD_DIM, (i + 1) * HEAD_DIM)
                h = pl.ds(2 * c + i, 1)
                q_ref[h, :] = jnp.sum(c_dot[part], axis=0, keepdims=True)
                r_ref[h, :] = jnp.sum(b_dot[part], axis=0, keepdims=True)
            state_part = scale_ref[:, lanes(c)].astype(F32) * btok_ref[:, lanes(p)]
            finish(c, own_ref[:, lanes(c)] + state_part)
            return carry

        lax.fori_loop(0, per, pair, 0, unroll=True)
    for copy in coming[PARTS]:
        copy.wait()
    for i, total in enumerate((gb, gc)):
        grad_ref[...] = total
        finish(PAIRS + i, grad_ref[...].T * slope_ref[:, i * STATE : (i + 1) * STATE])

    four = end_ref[...] * jnp.sum(product_ref[...], axis=1, keepdims=True)
    four_ref[...] = four
    steps = step_ref[...]
    sofar = sofar_ref[...]
    every = sofar[:, GROUP - 1 :]
    own = row_ref[...] - colin_ref[...] - r_ref[...]
    met = steps * own - (every - sofar + steps) * own + sofar * q_ref[...]
    rates = -(jnp.sum(met, axis=1, keepdims=True) + four[:, :1] * every)
    skips = jnp.sum(skiprow_ref[...], axis=1, keepdims=True)
    flip_ref[...] = jnp.zeros_like(flip_ref)
    lane = lax.broadcasted_iota(jnp.int32, (HEADS, LANE), 1)
    flip_ref[:HEADS, :] = jnp.where(lane == 0, rates, 0.0) + jnp.where(lane == 1, skips, 0.0)
    tiles = PAIRS + 2
    for c in range(tiles):
        sums = sums_ref[c]
        for k in range(KCONV + 1):
            at = k * tiles + c
            params_ref[at : at + 1, :] = sums[k : k + 1]
    at = (KCONV + 1) * tiles
    params_ref[at : at + 2, :] = flip_ref[...].T[:2]


def spread_kernel(gpre_ref, w_ref, gin_ref, last_ref):
    rim = KCONV - 1

    def tile(c, carry):
        grad = gpre_ref[:, lanes(c)]
        full = jnp.concatenate([grad, jnp.zeros((8, LANE), F32)], axis=0)
        spread = w_ref[rim : rim + 1, lanes(c)] * grad
        for k in range(rim):
            spread = spread + w_ref[k : k + 1, lanes(c)] * full[rim - k : rim - k + GROUP]
        gin_ref[:, lanes(c)] = spread.astype(BF16)
        last_ref[:, lanes(c)] = spread[GROUP - 16 :]
        return carry

    lax.fori_loop(0, PAIRS + 2, tile, 0, unroll=2)


def log_kernel(q_ref, r_ref, four_ref, col_ref, row_ref, rate_ref, gsteps_ref):
    own = row_ref[...] - col_ref[...] - r_ref[...]
    running = mm(own, triangle(False), precision=HIGH)
    ending = mm(q_ref[...], triangle(True), precision=HIGH)
    grad_log = own - running + ending + four_ref[:, :1]
    gsteps_ref[...] = -head_column(rate_ref) * grad_log


def unpack_kernel(
    own_ref, near_ref, far_ref, both_ref, weight_ref, bias_ref, rates_ref, skip_ref, sum_ref
):
    sum_ref[...] = (own_ref[...] + near_ref[...]) + (far_ref[...] + both_ref[...])
    tiles = PAIRS + 2
    for c in range(tiles):
        at = slice(c * LANE, (c + 1) * LANE)
        for k in range(KCONV):
            weight_ref[k : k + 1, at] = sum_ref[k * tiles + c : k * tiles + c + 1, :]
        bias_ref[at] = sum_ref[KCONV * tiles + c, :]
    at = (KCONV + 1) * tiles
    rates_ref[...] = sum_ref[at, :HEADS]
    skip_ref[...] = sum_ref[at + 1, :HEADS]


def call(
    kernel, outs, scratch, *operands, large=0, scalars=0, kept=(), large_out=False, limit=VMEM_LIMIT
):
    small = len(operands) - large - scalars
    spaces = [pltpu.VMEM] * small + [pltpu.HBM] * large + [pltpu.SMEM] * scalars
    operands = [
        pltpu.with_memory_space_constraint(operand, pltpu.HBM)
        if space == pltpu.HBM
        else operand
        for operand, space in zip(operands, spaces)
    ]
    out_space = pltpu.HBM if large_out else pltpu.VMEM
    return pl.pallas_call(
        kernel,
        out_shape=[
            out_space(*out) if large_out or i in kept else jax.ShapeDtypeStruct(*out)
            for i, out in enumerate(outs)
        ],
        in_specs=[pl.BlockSpec(memory_space=space) for space in spaces],
        out_specs=[pl.BlockSpec(memory_space=out_space)] * len(outs),
        scratch_shapes=[pltpu.VMEM(*item) if isinstance(item, tuple) else item for item in scratch],
        compiler_params=pltpu.CompilerParams(vmem_limit_bytes=limit),
    )(*operands)


def shifted(array, axis, by):
    length = lax.axis_size(axis)
    pairs = [(i, i + by) for i in range(length) if 0 <= i + by < length]
    return lax.ppermute(array, axis, pairs)


def flipped(array, axis, bits):
    return lax.ppermute(array, axis, [(i, i ^ bits) for i in range(lax.axis_size(axis))])


def four_summed(array, axis, bit):
    near = flipped(array, axis, bit)
    far = flipped(array, axis, 2 * bit)
    both = flipped(array, axis, 3 * bit)
    return (array + near) + (far + both)


def shards(xbc_in, conv_weight, conv_bias, step_sizes, decay_rates, skip_gain, grad_out):
    channels = xbc_in.shape[2]
    rim = KCONV - 1
    chunks = lax.axis_size("seq")
    rows = X_WIDTH // chunks
    x_in = xbc_in[0]
    dy = grad_out[0]
    steps = step_sizes[0]
    wide_heads = ((HEADS, GROUP), F32)
    by_head = ((X_WIDTH, GROUP), BF16)
    dma = pltpu.SemaphoreType.DMA
    halo = shifted(x_in[GROUP - rim :], "seq", 1)
    dywt, x_near, w_near, bias_near, tail, head = call(
        decay_kernel,
        [
            by_head,
            ((GROUP, channels), BF16),
            ((KCONV, channels), F32),
            ((channels,), F32),
            wide_heads,
            wide_heads,
        ],
        [
            wide_heads,
            pltpu.SMEM((HEADS,), F32),
            ((GROUP, X_WIDTH), BF16),
            dma((2,)),
            dma((PARTS,)),
            dma((3,)),
        ],
        steps, decay_rates, dy, x_in, conv_weight, conv_bias,
        large=6, kept=range(4), limit=SMALL_LIMIT,
    )
    (msg,) = call(
        functools.partial(front_kernel, chunks=chunks, rows=rows),
        [((chunks, 2 * rows + TAIL_ROWS, LANE), BF16)],
        [
            ((chunks, 2 * rows + TAIL_ROWS, LANE), BF16),
            ((GROUP, 2 * STATE), BF16),
            ((X_WIDTH // PARTS, GROUP), BF16),
            dma((PARTS,)),
        ],
        halo, dywt, tail, head, x_near, w_near, bias_near, large_out=True, limit=SMALL_LIMIT,
    )
    got = lax.all_to_all(msg, "seq", 0, 0, tiled=True)
    (own, scale, xwt, dywt, bc, bct, slope, gb, gc, col_sums, row_sums, skip_rows, sofar, d_end) = call(
        within_kernel,
        [
            ((GROUP, X_WIDTH), F32),
            ((GROUP, X_WIDTH), BF16),
            by_head,
            by_head,
            ((GROUP, 2 * STATE), BF16),
            ((2 * STATE, GROUP), BF16),
            ((GROUP, 2 * STATE), F32),
            ((STATE, GROUP), F32),
            ((STATE, GROUP), F32),
            wide_heads,
            wide_heads,
            wide_heads,
            wide_heads,
            ((HEADS, LANE), F32),
        ],
        [
            ((HEADS, GROUP, LANE), F32),
            ((GROUP, GROUP), F32),
            ((GROUP, GROUP), F32),
            ((LANE, GROUP), F32),
            ((LANE, GROUP), F32),
            wide_heads,
            wide_heads,
            wide_heads,
        ],
        x_in, halo, conv_weight, conv_bias, dy, steps, decay_rates, skip_gain, scalars=2,
    )
    got, own = lax.optimization_barrier((got, own))
    (turned,) = call(
        functools.partial(chain_kernel, chunks=chunks, rows=rows),
        [((chunks, 2 * rows, LANE), BF16)],
        [((chunks, 2 * rows, LANE), BF16), dma((4,))],
        got, large_out=True, limit=SMALL_LIMIT,
    )
    back = lax.all_to_all(turned, "seq", 0, 0, tiled=True)
    gpre, edge, q_rows, r_rows, four, params = call(
        functools.partial(back_kernel, chunks=chunks, rows=rows),
        [
            ((GROUP, channels), F32),
            ((rim, channels), F32),
            wide_heads,
            wide_heads,
            ((HEADS, LANE), F32),
            (((KCONV + 1) * (PAIRS + 2) + 2, LANE), F32),
        ],
        [
            ((GROUP, X_WIDTH), F32),
            ((GROUP, X_WIDTH), BF16),
            by_head,
            by_head,
            ((GROUP, channels), BF16),
            ((X_WIDTH // PARTS, GROUP), F32),
            ((X_WIDTH // PARTS, GROUP), F32),
            ((GROUP, X_WIDTH // PARTS), F32),
            ((HEADS, LANE), F32),
            ((STATE, GROUP), F32),
            ((PAIRS + 2, 8, LANE), F32),
            ((LANE, LANE), F32),
            dma((PARTS + 1, 5)),
        ],
        back, bc, bct, slope, gb, gc, col_sums, row_sums, skip_rows,
        halo, steps, sofar, d_end,
        own, scale, xwt, dywt, x_in,
        large=5, limit=SMALL_LIMIT,
    )
    sums = params + flipped(params, "dp", 1)
    sums, q_rows = lax.optimization_barrier((sums, q_rows))
    (gsteps,) = call(
        log_kernel, [wide_heads], [], q_rows, r_rows, four, col_sums, row_sums, decay_rates,
        scalars=1, limit=SMALL_LIMIT,
    )
    sums = four_summed(sums, "dp", 2)
    sums, gsteps, gpre = lax.optimization_barrier((sums, gsteps, gpre))
    grad_in, last = call(
        spread_kernel, [((GROUP, channels), BF16), ((16, channels), F32)], [], gpre, conv_weight,
        limit=SMALL_LIMIT,
    )
    sums = four_summed(sums, "seq", 8)
    sums, edge, grad_in = lax.optimization_barrier((sums, edge, grad_in))
    next_rows = shifted(edge, "seq", -1)
    sums = sums + flipped(sums, "seq", 1)
    sums, last = lax.optimization_barrier((sums, last))
    others = [flipped(sums, "seq", bits) for bits in (2, 4, 6)]
    ahead = jnp.concatenate([jnp.zeros_like(next_rows), next_rows], axis=0)
    added = last[16 - rim :]
    for k in range(rim):
        added = added + conv_weight[k][None] * ahead[rim - k : 2 * rim - k]
    ending = jnp.concatenate([last[: 16 - rim], added], axis=0).astype(BF16)
    grad_in = lax.dynamic_update_slice(grad_in, ending, (GROUP - 16, 0))
    grad_weight, grad_bias, grad_rates, grad_skip = call(
        unpack_kernel,
        [((KCONV, channels), F32), ((channels,), F32), ((HEADS,), F32), ((HEADS,), F32)],
        [(params.shape, F32)],
        sums, *others, limit=SMALL_LIMIT,
    )
    return (grad_in[None], gsteps[None], grad_weight, grad_bias, grad_rates, grad_skip)


def solution(mesh):
    return jax.shard_map(
        shards,
        mesh=mesh,
        in_specs=(
            P("dp", "seq", None),
            P(),
            P(),
            P("dp", None, "seq"),
            P(),
            P(),
            P("dp", "seq", None),
        ),
        out_specs=(P("dp", "seq", None), P("dp", None, "seq"), P(), P(), P(), P()),
        check_vma=False,
    )
```
